256 devices in a mesh: band: 8 (over z), grid: 32 (over x, y, core).
Axes of the slice: x: 4, y: 4, z: 8, core: 2. Of those that a mesh axis runs over, the one named last changes fastest.
Arguments:
- orbitals: bfloat16 [16, 256, 256, 256], P('band', 'grid'), may hold values from -60 to 60
- potential: float32 [256, 256, 256], P('grid'), may hold values from -2 to 1
Outputs:
- rotated: bfloat16 [16, 256, 256, 256], P('band', 'grid')
- projected: float32 [16, 16], replicated
The draws below stay inside these ranges and needn't reach their ends.
All inputs are finite; a program needn't handle non-finite values. Where the reference program divides by a largest or mean magnitude, that divisor is 1e-20 or more.
Results may differ from the reference program's by a relative error of at most 0.0005.
The reference program's roundings to bfloat16 on the way count: a program that leaves them out, or rounds other values in their place, can miss the bound.
Values may be sent and summed in bfloat16 or wider, within the bound.
No kernel may reach another device: no remote copies, remote signals or barrier semaphores. Data moves between devices by JAX's collectives and lax.ppermute only.
A program may use at most 128 MiB of HBM per device.

```python
import math
import jax
import jax.numpy as jnp
from jax import lax

NX = 256
NY = 256
NZ = 256
NS_ITERS = 6
NB = 16


def draw_orbitals(key, part):
    key_base = jax.random.fold_in(key, 11)
    key_mix = jax.random.fold_in(key, 23)
    key_scale = jax.random.fold_in(key, 37)
    key_lines = jax.random.fold_in(key, 41)
    key_wave = jax.random.fold_in(key, 53)
    key_phase = jax.random.fold_in(key, 67)
    key_along_y = jax.random.fold_in(key, 79)
    key_along_z = jax.random.fold_in(key, 83)
    base = jnp.clip(jax.random.normal(key_base, (NB, NX * NY * NZ), jnp.float32), -4.0, 4.0)
    line_noise = jnp.clip(jax.random.normal(key_lines, (NB, 2, NY, NZ), jnp.float32), -4.0, 4.0)
    top = 3.0
    mixing = jnp.eye(NB, dtype=jnp.float32) + 0.5 * jax.random.normal(key_mix, (NB, NB), jnp.float32) / math.sqrt(NB)
    scales = jnp.exp(jax.random.uniform(key_scale, (NB,), jnp.float32, 0.0, math.log(3.2)))
    mixed = jnp.dot(mixing, base).reshape(NB, NX, NY, NZ)
    top_mode = max(NX // 32, 1)
    wave_number = jax.random.randint(key_wave, (NB, 2), 1, top_mode + 1).astype(jnp.float32)
    phases = jax.random.uniform(key_phase, (NB, 2), jnp.float32, 0.0, 2.0 * math.pi)
    plane_index = jnp.arange(NX, dtype=jnp.float32)
    wave_rows = jnp.cos(wave_number[:, :, None] * plane_index[None, None, :] * (2.0 * math.pi / NX) + phases[:, :, None])
    smooth = wave_rows[:, 0, :, None, None] * line_noise[:, 0, None, :, :] + wave_rows[:, 1, :, None, None] * line_noise[:, 1, None, :, :]
    along_y = jnp.exp(jax.random.uniform(key_along_y, (NY,), jnp.float32, math.log(0.6), math.log(1.7)))
    along_z = jnp.exp(jax.random.uniform(key_along_z, (NZ,), jnp.float32, math.log(0.6), math.log(1.7)))
    position = jnp.arange(NX, dtype=jnp.float32) / max(NX - 1, 1)
    envelope = 1.0 + (top - 1.0) * position
    values = 0.75 * (mixed + smooth) * scales[:, None, None, None] * envelope[None, :, None, None]
    values = values * along_y[None, None, :, None] * along_z[None, None, None, :]
    return jnp.clip(values, -60.0, 60.0).astype(jnp.bfloat16)


def level_of(own_key, extent, shards, least, top_value):
    def one(dim, blocks):
        draws = jax.random.uniform(jax.random.fold_in(jax.random.fold_in(own_key, 6), dim), (blocks,), jnp.float32, least / len(shards), top_value / len(shards))
        return jnp.repeat(jnp.exp(draws), extent[dim] // blocks).reshape((-1,) + (1,) * (len(extent) - dim - 1))

    level = one(*shards[0])
    for cut in shards[1:]:
        level = level * one(*cut)
    return level


def setup_inputs(seed: int = 0) -> dict:
    key_of = jax.random.split(jax.random.key(seed), 3)
    return {
        "orbitals": draw_orbitals(jax.random.fold_in(key_of[2], 71), 0),
        "potential": jnp.clip(-2.0 + 3.0 * jax.random.uniform(key_of[1], (NX, NY, NZ), jnp.float32) ** level_of(key_of[1], (NX, NY, NZ), ((0, 32),), -0.2, 0.2), -2.0, 1.0),
    }


CENTER = 9.5
HALF_WIDTH = 6.5


def second_derivative(length):
    index = jnp.arange(length, dtype=jnp.int32)
    product = (index[:, None] * index[None, :]) % length
    angles = product.astype(jnp.float32) * (2.0 * math.pi / length)
    freq = jnp.minimum(index, length - index).astype(jnp.float32)
    weight = -((2.0 * math.pi / length) * freq) ** 2 / length
    cosines = jnp.cos(angles)
    sines = jnp.sin(angles)
    matrix = jnp.dot(cosines * weight[None, :], cosines.T, precision=lax.Precision.HIGHEST)
    matrix = matrix + jnp.dot(sines * weight[None, :], sines.T, precision=lax.Precision.HIGHEST)
    return matrix.astype(jnp.bfloat16)


def apply_ham(field, potential, k_x, k_y, k_z):
    wide = field.astype(jnp.float32)
    term_z = jnp.dot(field.reshape(-1, NZ), k_z, preferred_element_type=jnp.float32).reshape(NX, NY, NZ)
    term_y = jnp.einsum('xjz,jy->xyz', wide, k_y.astype(jnp.float32))
    term_x = jnp.einsum('jyz,jx->xyz', wide, k_x.astype(jnp.float32)).astype(jnp.bfloat16)
    return -0.5 * (term_x.astype(jnp.float32) + term_y + term_z) + potential * wide


def ritz(correlation, hamil):
    scale = jnp.max(jnp.sum(jnp.abs(correlation), axis=1))
    current = correlation / scale
    identity = jnp.eye(correlation.shape[0], dtype=jnp.float32)
    inverse_root = identity
    for turn_index in range(NS_ITERS):
        turn = 1.5 * identity - 0.5 * jnp.dot(inverse_root, current, precision=lax.Precision.HIGHEST)
        current = jnp.dot(current, turn, precision=lax.Precision.HIGHEST)
        inverse_root = jnp.dot(turn, inverse_root, precision=lax.Precision.HIGHEST)
    projected = jnp.dot(jnp.dot(inverse_root.T, hamil, precision=lax.Precision.HIGHEST), inverse_root, precision=lax.Precision.HIGHEST) / scale
    return inverse_root.astype(jnp.bfloat16), projected


def reference(orbitals, potential):
    k_x = second_derivative(NX)
    k_y = second_derivative(NY)
    k_z = second_derivative(NZ)

    def filter_one(start):
        start_f = start.astype(jnp.float32)
        first = ((apply_ham(start, potential, k_x, k_y, k_z) - CENTER * start_f) / HALF_WIDTH).astype(jnp.bfloat16)
        first_f = first.astype(jnp.float32)
        filtered = (2.0 * (apply_ham(first, potential, k_x, k_y, k_z) - CENTER * first_f) / HALF_WIDTH - start_f).astype(jnp.bfloat16)
        applied = apply_ham(filtered, potential, k_x, k_y, k_z).astype(jnp.bfloat16)
        return filtered, applied

    filtered, applied = lax.map(filter_one, orbitals)
    flat = filtered.reshape(NB, -1)
    hflat = applied.reshape(NB, -1)
    correlation = jnp.dot(flat, flat.T, preferred_element_type=jnp.float32)
    hamil = jnp.dot(hflat, flat.T, preferred_element_type=jnp.float32)
    coeff, projected = ritz(correlation, hamil)
    rotated = jnp.dot(coeff.T, flat, preferred_element_type=jnp.float32).astype(jnp.bfloat16)
    return rotated.reshape(NB, NX, NY, NZ), projected
```

```python
import functools
import math

import jax
import jax.numpy as jnp
from jax import lax
from jax.experimental import pallas as pl
from jax.experimental.pallas import tpu as pltpu
from jax.sharding import PartitionSpec as P

NS_ITERS = 6

CENTER = 9.5
HALF_WIDTH = 6.5

ROWS = 16
LANES = 128
VMEM_BYTES = 60 * 1024 * 1024
HIGHEST = lax.Precision.HIGHEST


def second_derivative(length):
    index = jnp.arange(length, dtype=jnp.int32)
    product = index[:, None] * index[None, :] % length
    angles = product.astype(jnp.float32) * (2.0 * math.pi / length)
    freq = jnp.minimum(index, length - index).astype(jnp.float32)
    weight = -((2.0 * math.pi / length * freq) ** 2) / length
    cosines = jnp.cos(angles)
    sines = jnp.sin(angles)
    matrix = jnp.dot(cosines * weight[None, :], cosines.T, precision=HIGHEST)
    matrix = matrix + jnp.dot(sines * weight[None, :], sines.T, precision=HIGHEST)
    return matrix.astype(jnp.bfloat16)


def dot(a, b):
    return jnp.dot(a, b, preferred_element_type=jnp.float32)


def dot_nt(a, b):
    return lax.dot_general(a, b, (((1,), (1,)), ((), ())), preferred_element_type=jnp.float32)


def params(dims):
    return pltpu.CompilerParams(
        dimension_semantics=("arbitrary",) * dims, vmem_limit_bytes=VMEM_BYTES
    )


def cost(flops, bytes_accessed):
    return pl.CostEstimate(flops=int(flops), bytes_accessed=int(bytes_accessed), transcendentals=0)


def split_rows(ref, tile, orbital, plane):
    return jnp.concatenate(
        [ref[tile, orbital, plane], ref[tile + 1, orbital, plane]], axis=1
    )


def load_plane(ref, plane):
    tiles = ref.shape[0]
    value = ref[:, 0, plane].reshape(tiles // 2, 2, ROWS, LANES)
    rows = tiles // 2 * ROWS
    return jnp.concatenate(
        [value[:, 0].reshape(rows, LANES), value[:, 1].reshape(rows, LANES)], axis=1
    )


def store_plane(ref, plane, value):
    tiles = ref.shape[0]
    left = value[:, :LANES].reshape(tiles // 2, 1, ROWS, LANES)
    right = value[:, LANES:].reshape(tiles // 2, 1, ROWS, LANES)
    ref[:, 0, plane] = jnp.concatenate([left, right], axis=1).reshape(tiles, ROWS, LANES)


def lines_kernel(field_ref, k_ref, out_ref, work):
    blocks, _, planes, rows, lanes = field_ref.shape
    total = blocks * planes
    work[...] = field_ref[...].reshape(total * rows, lanes).astype(jnp.float32)
    matrix = k_ref[...]
    for row in range(0, rows, 2):
        here = pl.ds(row, total, stride=rows)
        there = pl.ds(row + 1, total, stride=rows)
        value = jnp.concatenate([work[here, :], work[there, :]], axis=1).astype(jnp.bfloat16)
        result = dot(matrix, value)
        work[here, :] = result[:, :lanes]
        work[there, :] = result[:, lanes:]
    out_ref[...] = work[...].astype(jnp.bfloat16).reshape(blocks, 1, planes, rows, lanes)


def derive_lines(field, k_t):
    blocks, count, planes, rows, lanes = field.shape
    block = pl.BlockSpec((blocks, 1, planes, rows, lanes), lambda i: (0, i, 0, 0, 0))
    size = field.size
    return pl.pallas_call(
        lines_kernel,
        grid=(count,),
        in_specs=[block, pl.BlockSpec(k_t.shape, lambda i: (0, 0))],
        out_specs=block,
        out_shape=jax.ShapeDtypeStruct(field.shape, jnp.bfloat16),
        scratch_shapes=[pltpu.VMEM((blocks * planes * rows, lanes), jnp.float32)],
        compiler_params=params(1),
        cost_estimate=cost(2 * size * blocks * planes, 4 * size),
        name="derive_lines",
    )(field, k_t)


def local_terms(plane, ky_t, k_z):
    return dot(ky_t, plane) + dot(plane, k_z)


def first_kernel(field_ref, line_ref, pot_ref, ky_ref, kz_ref, out_ref):
    for plane in range(field_ref.shape[2]):
        field = load_plane(field_ref, plane)
        wide = field.astype(jnp.float32)
        line = load_plane(line_ref, plane).astype(jnp.float32)
        ham = -0.5 * (line + local_terms(field, ky_ref[...], kz_ref[...])) + pot_ref[plane] * wide
        value = (ham - CENTER * wide) * (1.0 / HALF_WIDTH)
        store_plane(out_ref, plane, value.astype(jnp.bfloat16))


def first_step(field, line, potential, ky_t, k_z, step=4):
    tiles, count, planes, rows, lanes = field.shape
    block = pl.BlockSpec((tiles, 1, step, rows, lanes), lambda x, o: (0, o, x, 0, 0))
    whole = pl.BlockSpec(ky_t.shape, lambda x, o: (0, 0))
    pot = pl.BlockSpec((step,) + potential.shape[1:], lambda x, o: (x, 0, 0))
    size = field.size
    return pl.pallas_call(
        first_kernel,
        grid=(planes // step, count),
        in_specs=[block, block, pot, whole, whole],
        out_specs=block,
        out_shape=jax.ShapeDtypeStruct(field.shape, jnp.bfloat16),
        compiler_params=params(2),
        cost_estimate=cost(4 * size * 256, 8 * size),
        name="first_step",
    )(field, line, potential, ky_t, k_z)


def filtered_kernel(me_ref, field_ref, line_ref, start_ref, pot_ref, ky_ref, kz_ref, *rest):
    bands = (len(rest) - 2) // 2
    f_refs, g_refs = rest[:bands], rest[bands : 2 * bands]
    f_work, g_work = rest[2 * bands :]
    me = me_ref[0]
    span = f_work.shape[0] // bands
    for plane in range(field_ref.shape[2]):
        field = load_plane(field_ref, plane)
        wide = field.astype(jnp.float32)
        line = load_plane(line_ref, plane).astype(jnp.float32)
        start = load_plane(start_ref, plane).astype(jnp.float32)
        pot = pot_ref[plane]
        ham = -0.5 * (line + local_terms(field, ky_ref[...], kz_ref[...])) + pot * wide
        value = 2.0 * (ham - CENTER * wide) * (1.0 / HALF_WIDTH) - start
        value = value.astype(jnp.bfloat16)
        part = -0.5 * local_terms(value, ky_ref[...], kz_ref[...]) + pot * value.astype(jnp.float32)
        f_work[...] = value
        g_work[...] = part.astype(jnp.bfloat16)
        for shift in range(bands):
            band = lax.rem(me + shift, bands)
            base = pl.multiple_of(band * span, span)
            for work, refs in ((f_work, f_refs), (g_work, g_refs)):
                store_plane(refs[shift], plane, work[pl.ds(base, span), :])


def filtered_step(me, field, line, start, potential, ky_t, k_z, bands, step=4):
    tiles, count, planes, rows, lanes = field.shape
    block = pl.BlockSpec((tiles, 1, step, rows, lanes), lambda x, o: (0, o, x, 0, 0))
    piece = pl.BlockSpec((tiles // bands, 1, step, rows, lanes), lambda x, o: (0, o, x, 0, 0))
    whole = pl.BlockSpec(ky_t.shape, lambda x, o: (0, 0))
    pot = pl.BlockSpec((step,) + potential.shape[1:], lambda x, o: (x, 0, 0))
    shape = jax.ShapeDtypeStruct((tiles // bands, count, planes, rows, lanes), jnp.bfloat16)
    size = field.size
    out = pl.pallas_call(
        filtered_kernel,
        grid=(planes // step, count),
        in_specs=[
            pl.BlockSpec(memory_space=pltpu.SMEM),
            block,
            block,
            block,
            pot,
            whole,
            whole,
        ],
        out_specs=[piece] * (2 * bands),
        out_shape=[shape] * (2 * bands),
        scratch_shapes=[pltpu.VMEM(potential.shape[1:], jnp.bfloat16)] * 2,
        compiler_params=params(2),
        cost_estimate=cost(8 * size * 256, 12 * size),
        name="filtered_step",
    )(me, field, line, start, potential, ky_t, k_z)
    return (list(out[:bands]), list(out[bands:]))


def chunk(refs, tile, plane):
    return jnp.concatenate(
        [split_rows(ref, tile, o, plane) for ref in refs for o in range(ref.shape[1])], axis=0
    )


def owner(place, me, own, bands, sign):
    return lax.rem(me + sign * (place // own) + bands, bands) * own + lax.rem(place, own)


def fold(product, me, out_ref, own, inner):
    rows = product.shape[0]
    count = out_ref.shape[0]
    at = lax.broadcasted_iota(jnp.int32, (rows, rows), 0)
    to = lax.broadcasted_iota(jnp.int32, (rows, rows), 1)
    who = lax.broadcasted_iota(jnp.int32, (count, rows), 0)
    row = lax.broadcasted_iota(jnp.int32, (count, rows), 1)
    if inner:
        same, place = at % ROWS == to % ROWS, row // ROWS
    else:
        same, place = at // ROWS == to // ROWS, row % ROWS
    kept = jnp.where(same, product, 0.0)
    pick = jnp.where(owner(place, me, own, count // own, -1) == who, 1.0, 0.0)
    half = jnp.dot(pick, kept, precision=HIGHEST, preferred_element_type=jnp.float32)
    out_ref[...] = lax.dot_general(
        half, pick, (((1,), (1,)), ((), ())), precision=HIGHEST, preferred_element_type=jnp.float32
    )


def gram_kernel(me_ref, *refs):
    work, out_ref, refs = refs[-1], refs[-2], refs[:-2]
    bands = out_ref.shape[0] // refs[0].shape[1]
    left, right = refs[:bands], refs[-bands:]

    @pl.when(pl.program_id(0) == 0)
    def _():
        work[...] = jnp.zeros_like(work)

    total = work[...]
    for plane in range(left[0].shape[2]):
        for tile in range(0, left[0].shape[0], 2):
            b = chunk(right, tile, plane)
            a = b if len(refs) == bands else chunk(left, tile, plane)
            total = total + dot_nt(a, b)
    work[...] = total

    @pl.when(pl.program_id(0) == pl.num_programs(0) - 1)
    def _():
        fold(work[...], me_ref[0], out_ref, refs[0].shape[1], True)


def gram(me, left, right=None, step=2):
    pieces = tuple(left) + (tuple(right) if right is not None else ())
    tiles, count, planes, rows, lanes = pieces[0].shape
    total = len(left) * count
    block = pl.BlockSpec((tiles, count, step, rows, lanes), lambda x: (0, 0, x, 0, 0))
    size = pieces[0].size * len(left)
    return pl.pallas_call(
        gram_kernel,
        grid=(planes // step,),
        in_specs=[pl.BlockSpec(memory_space=pltpu.SMEM)] + [block] * len(pieces),
        out_specs=pl.BlockSpec((total, total), lambda x: (0, 0)),
        out_shape=jax.ShapeDtypeStruct((total, total), jnp.float32),
        scratch_shapes=[pltpu.VMEM((total * rows, total * rows), jnp.float32)],
        compiler_params=params(1),
        cost_estimate=cost(2 * size * 256, 2 * size * (len(pieces) // len(left))),
        name="gram",
    )(me, *pieces)


def line_gram_kernel(own, me_ref, left_ref, right_ref, out_ref, work):
    @pl.when(pl.program_id(0) == 0)
    def _():
        work[...] = jnp.zeros_like(work)

    blocks, halves, planes, rows, lanes = left_ref.shape
    total = work[...]

    def rows_of(ref, at):
        return jnp.concatenate(
            [ref[at : at + 2, half].reshape(2 * planes * rows, lanes) for half in range(halves)], axis=1
        )

    for at in range(0, blocks, 2):
        total = total + dot_nt(rows_of(left_ref, at), rows_of(right_ref, at))
    work[...] = total

    @pl.when(pl.program_id(0) == pl.num_programs(0) - 1)
    def _():
        fold(work[...], me_ref[0], out_ref, own, False)


def line_gram(me, own, left, right, step=8):
    blocks, halves, planes, rows, lanes = left.shape
    block = pl.BlockSpec((step, halves, planes, rows, lanes), lambda x: (x, 0, 0, 0, 0))
    return pl.pallas_call(
        functools.partial(line_gram_kernel, own),
        grid=(blocks // step,),
        in_specs=[pl.BlockSpec(memory_space=pltpu.SMEM)] + [block] * 2,
        out_specs=pl.BlockSpec((rows, rows), lambda x: (0, 0)),
        out_shape=jax.ShapeDtypeStruct((rows, rows), jnp.float32),
        scratch_shapes=[pltpu.VMEM((2 * planes * rows, 2 * planes * rows), jnp.float32)],
        compiler_params=params(1),
        cost_estimate=cost(2 * left.size * 256, 4 * left.size),
        name="line_gram",
    )(me, left, right)


def regroup_kernel(*refs):
    work, out_ref, refs = refs[-1], refs[-2], refs[:-2]
    tiles, count, planes, rows, lanes = refs[0].shape
    each = planes * rows
    total = len(refs) * count
    for at, ref in enumerate(refs):
        for o in range(count):
            start = (at * count + o) * each
            work[start : start + each, :] = ref[0, o].reshape(each, lanes).astype(jnp.float32)
    half = rows // 2
    for plane in range(planes):
        for row in range(rows):
            value = work[pl.ds(plane * rows + row, total, stride=each), :]
            out_ref[row % half, row // half, plane] = value.astype(jnp.bfloat16)


def regroup(pieces):
    tiles, count, planes, rows, lanes = pieces[0].shape
    total = len(pieces) * count
    half = rows // 2
    block = pl.BlockSpec((1, count, planes, rows, lanes), lambda t: (t, 0, 0, 0, 0))
    size = pieces[0].size * len(pieces)
    return pl.pallas_call(
        regroup_kernel,
        grid=(tiles,),
        in_specs=[block] * len(pieces),
        out_specs=pl.BlockSpec((half, 2, planes, total, lanes), lambda t: (t, 0, 0, 0, 0)),
        out_shape=jax.ShapeDtypeStruct((tiles * half, 2, planes, total, lanes), jnp.bfloat16),
        scratch_shapes=[pltpu.VMEM((total * planes * rows, lanes), jnp.float32)],
        compiler_params=params(1),
        cost_estimate=cost(size, 4 * size),
        name="regroup",
    )(*pieces)


def rotate_kernel(mix_ref, *refs):
    bands = len(refs) // 2
    ins, outs = refs[:bands], refs[bands:]
    tiles, count, planes, rows, lanes = ins[0].shape
    for plane in range(planes):
        for tile in range(0, tiles, 2):
            value = dot(mix_ref[...], chunk(ins, tile, plane)).astype(jnp.bfloat16)
            for at, ref in enumerate(outs):
                for o in range(count):
                    start = (at * count + o) * rows
                    ref[tile, o, plane] = value[start : start + rows, :lanes]
                    ref[tile + 1, o, plane] = value[start : start + rows, lanes:]


def rotate(mix, pieces, step=2):
    tiles, count, planes, rows, lanes = pieces[0].shape
    block = pl.BlockSpec((tiles, count, step, rows, lanes), lambda x: (0, 0, x, 0, 0))
    size = pieces[0].size * len(pieces)
    return pl.pallas_call(
        rotate_kernel,
        grid=(planes // step,),
        in_specs=[pl.BlockSpec(mix.shape, lambda x: (0, 0))] + [block] * len(pieces),
        out_specs=[block] * len(pieces),
        out_shape=[jax.ShapeDtypeStruct(pieces[0].shape, jnp.bfloat16)] * len(pieces),
        compiler_params=params(1),
        cost_estimate=cost(2 * size * 256, 4 * size),
        name="rotate",
    )(mix, *pieces)


def untile_kernel(me_ref, *refs):
    ins, out_ref = refs[:-1], refs[-1]
    for shift, ref in enumerate(ins):

        @pl.when(pl.program_id(0) == shift)
        def _(ref=ref):
            tiles, _, _, rows, lanes = ref.shape
            for tile in range(tiles):
                row, lane = tile // 2 * rows, tile % 2 * lanes
                out_ref[:, :, row : row + rows, lane : lane + lanes] = ref[tile]


def untile(me, pieces, shape):
    bands = len(pieces)
    tiles, count, planes, rows, lanes = pieces[0].shape
    block = pl.BlockSpec(pieces[0].shape, lambda s, me: (0, 0, 0, 0, 0))
    out = pl.BlockSpec(
        (count, planes, tiles // 2 * rows, 2 * lanes),
        lambda s, me: (0, 0, lax.rem(me[0] + bands - s, bands), 0),
    )
    return pl.pallas_call(
        untile_kernel,
        grid_spec=pltpu.PrefetchScalarGridSpec(
            num_scalar_prefetch=1, grid=(bands,), in_specs=[block] * bands, out_specs=out
        ),
        out_shape=jax.ShapeDtypeStruct(shape, jnp.bfloat16),
        compiler_params=params(1),
        cost_estimate=cost(0, 4 * math.prod(shape)),
        name="untile",
    )(me, *pieces)


def exchange(pieces, axis):
    size = lax.axis_size(axis)
    out = [pieces[0]] + [None] * (size - 1)
    order = sorted(range(1, size), key=lambda s: -min(s, size - s))
    for shift in order:
        pairs = [(i, (i + shift) % size) for i in range(size)]
        out[shift] = lax.ppermute(pieces[shift], axis, pairs)
    return out


def over_grid(field):
    return lax.all_to_all(field, "grid", 0, 0, tiled=True)


def spread_sum(matrix, axis):
    flat = matrix.reshape(-1, LANES)
    size = lax.axis_size(axis)
    spread = jnp.broadcast_to(flat[None], (size,) + flat.shape)
    return jnp.sum(lax.all_to_all(spread, axis, 0, 0, tiled=True), axis=0).reshape(matrix.shape)


def mixing_kernel(own, me_ref, corr_ref, root_ref, scale_ref, mix_ref):
    correlation = corr_ref[...]
    count = correlation.shape[0]
    bands = count // own
    scale = jnp.max(jnp.sum(jnp.abs(correlation), axis=1, keepdims=True), axis=0, keepdims=True)
    at = lax.broadcasted_iota(jnp.int32, (count, count), 0)
    to = lax.broadcasted_iota(jnp.int32, (count, count), 1)
    identity = jnp.where(at == to, 1.0, 0.0)

    def full(a, b):
        return jnp.dot(a, b, precision=HIGHEST, preferred_element_type=jnp.float32)

    current = correlation / scale
    root = identity
    for _ in range(NS_ITERS):
        turn = 1.5 * identity - 0.5 * full(root, current)
        current = full(current, turn)
        root = full(turn, root)
    root_ref[...] = root
    scale_ref[...] = jnp.broadcast_to(scale, scale_ref.shape)
    coeff = root.astype(jnp.bfloat16)
    rows = mix_ref.shape[0]
    me = me_ref[0]
    who = lax.broadcasted_iota(jnp.int32, (count, rows), 0)
    place = lax.broadcasted_iota(jnp.int32, (count, rows), 1) // ROWS
    source = jnp.where(owner(place, me, own, bands, -1) == who, 1.0, 0.0).astype(jnp.bfloat16)
    target = jnp.where(owner(place, me, own, bands, 1) == who, 1.0, 0.0).astype(jnp.bfloat16)
    over_target = lax.dot_general(
        coeff, target, (((1,), (0,)), ((), ())), preferred_element_type=jnp.float32
    ).astype(jnp.bfloat16)
    mix = lax.dot_general(
        over_target, source, (((0,), (0,)), ((), ())), preferred_element_type=jnp.float32
    )
    at = lax.broadcasted_iota(jnp.int32, (rows, rows), 0)
    to = lax.broadcasted_iota(jnp.int32, (rows, rows), 1)
    mix_ref[...] = jnp.where(at % ROWS == to % ROWS, mix, 0.0).astype(jnp.bfloat16)


def mixing(me, own, correlation):
    count = correlation.shape[0]
    rows = count * ROWS
    vmem = pl.BlockSpec(memory_space=pltpu.VMEM)
    return pl.pallas_call(
        functools.partial(mixing_kernel, own),
        in_specs=[pl.BlockSpec(memory_space=pltpu.SMEM), vmem],
        out_specs=[vmem] * 3,
        out_shape=[
            jax.ShapeDtypeStruct((count, count), jnp.float32),
            jax.ShapeDtypeStruct((1, LANES), jnp.float32),
            jax.ShapeDtypeStruct((rows, rows), jnp.bfloat16),
        ],
        cost_estimate=cost(1e9, 1e6),
        name="mixing",
    )(me, correlation)


def project(inverse_root, hamil, scale):
    left = jnp.dot(inverse_root.T, hamil, precision=HIGHEST)
    return jnp.dot(left, inverse_root, precision=HIGHEST) / scale


def per_device(orbitals, potential):
    own, planes, height, depth = orbitals.shape
    bands = lax.axis_size("band")
    me = jnp.full((1,), lax.axis_index("band"), jnp.int32)
    kx_t = second_derivative(planes * lax.axis_size("grid")).T
    ky_t = second_derivative(height).T
    k_z = second_derivative(depth)

    tiled = orbitals.reshape(own, planes, height // ROWS, ROWS, depth // LANES, LANES)
    start = tiled.transpose(2, 4, 0, 1, 3, 5).reshape(-1, own, planes, ROWS, LANES)
    line = over_grid(derive_lines(over_grid(start), kx_t))
    first = first_step(start, line, potential, ky_t, k_z)
    line = over_grid(derive_lines(over_grid(first), kx_t))
    f_out, g_out = filtered_step(me, first, line, start, potential, ky_t, k_z, bands)

    arrived = exchange(f_out, "band")
    correlation = spread_sum(gram(me, arrived), "grid")
    late = (1, bands - 1)
    held = lax.optimization_barrier((correlation,) + tuple(g_out[s] for s in late))
    correlation = held[0]
    for s, piece in zip(late, held[1:]):
        g_out[s] = piece
    g_arrived = exchange(g_out, "band")
    correlation = spread_sum(correlation, "band")
    inverse_root, scale, mix = mixing(me, own, correlation)
    back = exchange(rotate(mix, arrived), "band")
    rotated = untile(me, back, orbitals.shape)

    lines = over_grid(regroup(arrived))
    hamil = gram(me, g_arrived, arrived) - 0.5 * line_gram(me, own, derive_lines(lines, kx_t), lines)
    hamil = spread_sum(spread_sum(hamil, "grid"), "band")
    projected = project(inverse_root, hamil, scale[0, 0])
    return (rotated, projected)


def solution(mesh):
    in_specs = (P("band", "grid", None, None), P("grid", None, None))
    out_specs = (P("band", "grid", None, None), P())
    return jax.shard_map(
        per_device, mesh=mesh, in_specs=in_specs, out_specs=out_specs, check_vma=False
    )
```

```python
import functools
import math

import jax
import jax.numpy as jnp
from jax import lax
from jax.experimental import pallas as pl
from jax.experimental.pallas import tpu as pltpu
from jax.sharding import PartitionSpec as P

NS_ITERS = 6

CENTER = 9.5
HALF_WIDTH = 6.5

ROWS = 16
LANES = 128
MOST_MIB = 63
STEP_MIB = 24
HIGHEST = lax.Precision.HIGHEST


def second_derivative(length):
    index = jnp.arange(length, dtype=jnp.int32)
    product = index[:, None] * index[None, :] % length
    angles = product.astype(jnp.float32) * (2.0 * math.pi / length)
    freq = jnp.minimum(index, length - index).astype(jnp.float32)
    weight = -((2.0 * math.pi / length * freq) ** 2) / length
    cosines = jnp.cos(angles)
    sines = jnp.sin(angles)
    matrix = jnp.dot(cosines * weight[None, :], cosines.T, precision=HIGHEST)
    matrix = matrix + jnp.dot(sines * weight[None, :], sines.T, precision=HIGHEST)
    return matrix.astype(jnp.bfloat16)


def dot(a, b):
    return jnp.dot(a, b, preferred_element_type=jnp.float32)


def dot_nt(a, b):
    return lax.dot_general(a, b, (((1,), (1,)), ((), ())), preferred_element_type=jnp.float32)


def params(dims, mib=MOST_MIB):
    return pltpu.CompilerParams(
        dimension_semantics=("arbitrary",) * dims, vmem_limit_bytes=mib * 1024 * 1024
    )


def cost(flops, bytes_accessed):
    return pl.CostEstimate(flops=int(flops), bytes_accessed=int(bytes_accessed), transcendentals=0)


def split_rows(ref, tile, orbital, plane):
    return jnp.concatenate(
        [ref[tile, orbital, plane], ref[tile + 1, orbital, plane]], axis=1
    )


def load_plane(ref, plane):
    tiles = ref.shape[0]
    value = ref[:, 0, plane].reshape(tiles // 2, 2, ROWS, LANES)
    rows = tiles // 2 * ROWS
    return jnp.concatenate(
        [value[:, 0].reshape(rows, LANES), value[:, 1].reshape(rows, LANES)], axis=1
    )


def store_plane(ref, plane, value, orbital=0):
    tiles = ref.shape[0]
    left = value[:, :LANES].reshape(tiles // 2, 1, ROWS, LANES)
    right = value[:, LANES:].reshape(tiles // 2, 1, ROWS, LANES)
    ref[:, orbital, plane] = jnp.concatenate([left, right], axis=1).reshape(tiles, ROWS, LANES)


def lines_kernel(field_ref, k_ref, out_ref, work):
    blocks, _, planes, rows, lanes = field_ref.shape
    total = blocks * planes
    work[...] = field_ref[...].reshape(total * rows, lanes).astype(jnp.float32)
    matrix = k_ref[...]
    for row in range(0, rows, 2):
        here = pl.ds(row, total, stride=rows)
        there = pl.ds(row + 1, total, stride=rows)
        value = jnp.concatenate([work[here, :], work[there, :]], axis=1).astype(jnp.bfloat16)
        result = dot(matrix, value)
        work[here, :] = result[:, :lanes]
        work[there, :] = result[:, lanes:]
    out_ref[...] = work[...].astype(jnp.bfloat16).reshape(blocks, 1, planes, rows, lanes)


def derive_lines(field, k_t):
    blocks, count, planes, rows, lanes = field.shape
    block = pl.BlockSpec((blocks, 1, planes, rows, lanes), lambda i: (0, i, 0, 0, 0))
    size = field.size
    return pl.pallas_call(
        lines_kernel,
        grid=(count,),
        in_specs=[block, pl.BlockSpec(k_t.shape, lambda i: (0, 0))],
        out_specs=block,
        out_shape=jax.ShapeDtypeStruct(field.shape, jnp.bfloat16),
        scratch_shapes=[pltpu.VMEM((blocks * planes * rows, lanes), jnp.float32)],
        compiler_params=params(1, STEP_MIB),
        cost_estimate=cost(2 * size * blocks * planes, 4 * size),
        name="derive_lines",
    )(field, k_t)


def tile_kernel(in_ref, out_ref):
    tiles, count, planes, rows, lanes = out_ref.shape
    for tile in range(tiles):
        row, lane = tile // 2 * rows, tile % 2 * lanes
        out_ref[tile] = in_ref[:, :, row : row + rows, lane : lane + lanes]


def tile(orbitals, step=2):
    own, planes, height, depth = orbitals.shape
    tiles = height // ROWS * (depth // LANES)
    return pl.pallas_call(
        tile_kernel,
        grid=(planes // step,),
        in_specs=[pl.BlockSpec((own, step, height, depth), lambda x: (0, x, 0, 0))],
        out_specs=pl.BlockSpec((tiles, own, step, ROWS, LANES), lambda x: (0, 0, x, 0, 0)),
        out_shape=jax.ShapeDtypeStruct((tiles, own, planes, ROWS, LANES), orbitals.dtype),
        compiler_params=params(1, STEP_MIB),
        cost_estimate=cost(0, 4 * orbitals.size),
        name="tile",
    )(orbitals)


def local_terms(plane, ky_t, k_z):
    return dot(ky_t, plane) + dot(plane, k_z)


def first_kernel(field_ref, line_ref, pot_ref, ky_ref, kz_ref, out_ref):
    for plane in range(field_ref.shape[2]):
        field = load_plane(field_ref, plane)
        wide = field.astype(jnp.float32)
        line = load_plane(line_ref, plane).astype(jnp.float32)
        ham = -0.5 * (line + local_terms(field, ky_ref[...], kz_ref[...])) + pot_ref[plane] * wide
        value = (ham - CENTER * wide) * (1.0 / HALF_WIDTH)
        store_plane(out_ref, plane, value.astype(jnp.bfloat16))


def plane_specs(ky_t, potential, step):
    whole = pl.BlockSpec(ky_t.shape, lambda x: (0, 0))
    pot = pl.BlockSpec((step,) + potential.shape[1:], lambda x: (x, 0, 0))
    return [pot, whole, whole]


def orbital_spec(field, step, orbital):
    tiles, count, _, rows, lanes = field.shape
    return pl.BlockSpec((tiles, 1, step, rows, lanes), lambda x: (0, orbital if count > 1 else 0, x, 0, 0))


def first_step(orbital, field, line, potential, ky_t, k_z, step=2):
    tiles, _, planes, rows, lanes = field.shape
    shape = jax.ShapeDtypeStruct((tiles, 1, planes, rows, lanes), jnp.bfloat16)
    size = math.prod(shape.shape)
    return pl.pallas_call(
        first_kernel,
        grid=(planes // step,),
        in_specs=[orbital_spec(v, step, orbital) for v in (field, line)]
        + plane_specs(ky_t, potential, step),
        out_specs=orbital_spec(shape, step, 0),
        out_shape=shape,
        compiler_params=params(1, STEP_MIB),
        cost_estimate=cost(4 * size * 256, 10 * size),
        name="first_step",
    )(field, line, potential, ky_t, k_z)


def store_pieces(me, refs, orbital, plane, work):
    bands = len(refs)
    span = work.shape[0] // bands
    for shift, ref in enumerate(refs):
        base = pl.multiple_of(lax.rem(me + shift, bands) * span, span)
        store_plane(ref, plane, work[pl.ds(base, span), :], orbital)


def filtered_kernel(me_ref, field_ref, line_ref, start_ref, pot_ref, ky_ref, kz_ref, *rest):
    piece_refs, out_ref, work = rest[:-2], rest[-2], rest[-1]
    for plane in range(field_ref.shape[2]):
        field = load_plane(field_ref, plane)
        wide = field.astype(jnp.float32)
        line = load_plane(line_ref, plane).astype(jnp.float32)
        start = load_plane(start_ref, plane).astype(jnp.float32)
        ham = -0.5 * (line + local_terms(field, ky_ref[...], kz_ref[...])) + pot_ref[plane] * wide
        value = 2.0 * (ham - CENTER * wide) * (1.0 / HALF_WIDTH) - start
        value = value.astype(jnp.bfloat16)
        store_plane(out_ref, plane, value)
        work[...] = value
        store_pieces(me_ref[0], piece_refs, 0, plane, work)


def filtered_step(me, orbital, field, line, start, potential, ky_t, k_z, bands, step=2):
    tiles, _, planes, rows, lanes = field.shape
    shape = jax.ShapeDtypeStruct((tiles // bands, 1, planes, rows, lanes), jnp.bfloat16)
    size = field.size
    out = pl.pallas_call(
        filtered_kernel,
        grid=(planes // step,),
        in_specs=[pl.BlockSpec(memory_space=pltpu.SMEM)]
        + [orbital_spec(v, step, orbital) for v in (field, line, start)]
        + plane_specs(ky_t, potential, step),
        out_specs=[orbital_spec(shape, step, 0)] * bands + [orbital_spec(field, step, 0)],
        out_shape=[shape] * bands + [jax.ShapeDtypeStruct(field.shape, jnp.bfloat16)],
        scratch_shapes=[pltpu.VMEM(potential.shape[1:], jnp.bfloat16)],
        compiler_params=params(1, STEP_MIB),
        cost_estimate=cost(4 * size * 256, 14 * size),
        name="filtered_step",
    )(me, field, line, start, potential, ky_t, k_z)
    return (list(out[:bands]), out[bands])


def local_kernel(own, me_ref, *refs):
    field_refs, (pot_ref, ky_ref, kz_ref), rest = refs[:own], refs[own : own + 3], refs[own + 3 :]
    piece_refs, work = rest[:-1], rest[-1]
    for plane in range(pot_ref.shape[0]):
        pot = pot_ref[plane]
        for orbital, field_ref in enumerate(field_refs):
            field = load_plane(field_ref, plane)
            terms = local_terms(field, ky_ref[...], kz_ref[...])
            part = -0.5 * terms + pot * field.astype(jnp.float32)
            work[...] = part.astype(jnp.bfloat16)
            store_pieces(me_ref[0], piece_refs, orbital, plane, work)


def local_step(me, fields, potential, ky_t, k_z, bands, step=2):
    tiles, _, planes, rows, lanes = fields[0].shape
    own = len(fields)
    shape = jax.ShapeDtypeStruct((tiles // bands, own, planes, rows, lanes), jnp.bfloat16)
    piece = pl.BlockSpec((tiles // bands, own, step, rows, lanes), lambda x: (0, 0, x, 0, 0))
    size = own * fields[0].size
    return list(
        pl.pallas_call(
            functools.partial(local_kernel, own),
            grid=(planes // step,),
            in_specs=[pl.BlockSpec(memory_space=pltpu.SMEM)]
            + [orbital_spec(field, step, 0) for field in fields]
            + plane_specs(ky_t, potential, step),
            out_specs=[piece] * bands,
            out_shape=[shape] * bands,
            scratch_shapes=[pltpu.VMEM(potential.shape[1:], jnp.bfloat16)],
            compiler_params=params(1),
            cost_estimate=cost(4 * size * 256, 8 * size),
            name="local_step",
        )(me, *fields, potential, ky_t, k_z)
    )


def chunk(refs, tile, plane):
    return jnp.concatenate(
        [split_rows(ref, tile, 0, plane) for ref in refs], axis=0
    )


def owner(place, me, own, bands, sign):
    return lax.rem(me + sign * (place // own) + bands, bands) * own + lax.rem(place, own)


def fold(product, me, out_ref, own, inner):
    rows = product.shape[0]
    count = out_ref.shape[0]
    at = lax.broadcasted_iota(jnp.int32, (rows, rows), 0)
    to = lax.broadcasted_iota(jnp.int32, (rows, rows), 1)
    who = lax.broadcasted_iota(jnp.int32, (count, rows), 0)
    row = lax.broadcasted_iota(jnp.int32, (count, rows), 1)
    if inner:
        same, place = at % ROWS == to % ROWS, row // ROWS
    else:
        same, place = at // ROWS == to // ROWS, row % ROWS
    kept = jnp.where(same, product, 0.0)
    pick = jnp.where(owner(place, me, own, count // own, -1) == who, 1.0, 0.0)
    half = jnp.dot(pick, kept, precision=HIGHEST, preferred_element_type=jnp.float32)
    out_ref[...] = lax.dot_general(
        half, pick, (((1,), (1,)), ((), ())), precision=HIGHEST, preferred_element_type=jnp.float32
    )


def gram_kernel(own, count, me_ref, *refs):
    refs, out_ref, work = refs[:-2], refs[-2], refs[-1]
    left, right = refs[:count], refs[-count:]

    @pl.when(pl.program_id(0) == 0)
    def _():
        work[...] = jnp.zeros_like(work)

    total = work[...]
    for plane in range(left[0].shape[2]):
        for tile in range(0, left[0].shape[0], 2):
            b = chunk(right, tile, plane)
            a = b if len(refs) == count else chunk(left, tile, plane)
            total = total + dot_nt(a, b)
    work[...] = total

    @pl.when(pl.program_id(0) == pl.num_programs(0) - 1)
    def _():
        fold(work[...], me_ref[0], out_ref, own, True)


def piece_spec(tiles, view, step):
    array, at = view
    _, _, _, rows, lanes = array.shape
    return pl.BlockSpec((tiles, 1, step, rows, lanes), lambda x: (0, at, x, 0, 0))


def gram(me, own, tiles, left, right=(), step=4):
    views = list(left) + list(right)
    _, _, planes, rows, lanes = views[0][0].shape
    total = len(left)
    size = tiles * planes * rows * lanes * total
    return pl.pallas_call(
        functools.partial(gram_kernel, own, total),
        grid=(planes // step,),
        in_specs=[pl.BlockSpec(memory_space=pltpu.SMEM)]
        + [piece_spec(tiles, view, step) for view in views],
        out_specs=pl.BlockSpec((total, total), lambda x: (0, 0)),
        out_shape=jax.ShapeDtypeStruct((total, total), jnp.float32),
        scratch_shapes=[pltpu.VMEM((total * rows, total * rows), jnp.float32)],
        compiler_params=params(1),
        cost_estimate=cost(2 * size * 256, 2 * size * (len(views) // total)),
        name="gram",
    )(me, *[view[0] for view in views])


def line_gram_kernel(own, me_ref, left_ref, right_ref, out_ref, work):
    @pl.when(pl.program_id(0) == 0)
    def _():
        work[...] = jnp.zeros_like(work)

    blocks, halves, planes, rows, lanes = left_ref.shape
    total = work[...]

    def rows_of(ref, at):
        return jnp.concatenate(
            [ref[at : at + 2, half].reshape(2 * planes * rows, lanes) for half in range(halves)], axis=1
        )

    for at in range(0, blocks, 2):
        total = total + dot_nt(rows_of(left_ref, at), rows_of(right_ref, at))
    work[...] = total

    @pl.when(pl.program_id(0) == pl.num_programs(0) - 1)
    def _():
        fold(work[...], me_ref[0], out_ref, own, False)


def line_gram(me, own, left, right, step=8):
    blocks, halves, planes, rows, lanes = left.shape
    block = pl.BlockSpec((step, halves, planes, rows, lanes), lambda x: (x, 0, 0, 0, 0))
    return pl.pallas_call(
        functools.partial(line_gram_kernel, own),
        grid=(blocks // step,),
        in_specs=[pl.BlockSpec(memory_space=pltpu.SMEM)] + [block] * 2,
        out_specs=pl.BlockSpec((rows, rows), lambda x: (0, 0)),
        out_shape=jax.ShapeDtypeStruct((rows, rows), jnp.float32),
        scratch_shapes=[pltpu.VMEM((2 * planes * rows, 2 * planes * rows), jnp.float32)],
        compiler_params=params(1),
        cost_estimate=cost(2 * left.size * 256, 4 * left.size),
        name="line_gram",
    )(me, left, right)


def regroup_kernel(*refs):
    work, out_ref, refs = refs[-1], refs[-2], refs[:-2]
    _, _, planes, rows, lanes = refs[0].shape
    each = planes * rows
    total = len(refs)
    for at, ref in enumerate(refs):
        work[at * each : (at + 1) * each, :] = ref[0, 0].reshape(each, lanes).astype(jnp.float32)
    half = rows // 2
    for plane in range(planes):
        for row in range(rows):
            value = work[pl.ds(plane * rows + row, total, stride=each), :]
            out_ref[row % half, row // half, plane] = value.astype(jnp.bfloat16)


def regroup(tiles, views):
    _, _, planes, rows, lanes = views[0][0].shape
    total = len(views)
    half = rows // 2

    def spec(at):
        return pl.BlockSpec((1, 1, planes, rows, lanes), lambda t: (t, at, 0, 0, 0))

    size = tiles * planes * rows * lanes * total
    return pl.pallas_call(
        regroup_kernel,
        grid=(tiles,),
        in_specs=[spec(at) for _, at in views],
        out_specs=pl.BlockSpec((half, 2, planes, total, lanes), lambda t: (t, 0, 0, 0, 0)),
        out_shape=jax.ShapeDtypeStruct((tiles * half, 2, planes, total, lanes), jnp.bfloat16),
        scratch_shapes=[pltpu.VMEM((total * planes * rows, lanes), jnp.float32)],
        compiler_params=params(1),
        cost_estimate=cost(size, 4 * size),
        name="regroup",
    )(*[view[0] for view in views])


def rotate_kernel(total, mix_ref, *refs):
    ins, outs = refs[:total], refs[total:]
    tiles, count, planes, rows, lanes = outs[0].shape
    for plane in range(planes):
        for tile in range(0, tiles, 2):
            value = dot(mix_ref[...], chunk(ins, tile, plane)).astype(jnp.bfloat16)
            for at, ref in enumerate(outs):
                for o in range(count):
                    start = (at * count + o) * rows
                    ref[tile, o, plane] = value[start : start + rows, :lanes]
                    ref[tile + 1, o, plane] = value[start : start + rows, lanes:]


def rotate(mix, own, tiles, views, step=4):
    _, _, planes, rows, lanes = views[0][0].shape
    total = len(views)
    out = pl.BlockSpec((tiles, own, step, rows, lanes), lambda x: (0, 0, x, 0, 0))
    shape = jax.ShapeDtypeStruct((tiles, own, planes, rows, lanes), jnp.bfloat16)
    size = tiles * planes * rows * lanes * total
    return pl.pallas_call(
        functools.partial(rotate_kernel, total),
        grid=(planes // step,),
        in_specs=[pl.BlockSpec(mix.shape, lambda x: (0, 0))]
        + [piece_spec(tiles, view, step) for view in views],
        out_specs=[out] * (total // own),
        out_shape=[shape] * (total // own),
        compiler_params=params(1),
        cost_estimate=cost(2 * size * 256, 4 * size),
        name="rotate",
    )(mix, *[view[0] for view in views])


def untile_kernel(me_ref, *refs):
    ins, out_ref = refs[:-1], refs[-1]
    for shift, ref in enumerate(ins):

        @pl.when(pl.program_id(0) == shift)
        def _(ref=ref):
            tiles, _, _, rows, lanes = ref.shape
            for tile in range(tiles):
                row, lane = tile // 2 * rows, tile % 2 * lanes
                out_ref[:, :, row : row + rows, lane : lane + lanes] = ref[tile]


def untile(me, pieces, shape):
    bands = len(pieces)
    tiles, count, planes, rows, lanes = pieces[0].shape
    block = pl.BlockSpec(pieces[0].shape, lambda s, me: (0, 0, 0, 0, 0))
    out = pl.BlockSpec(
        (count, planes, tiles // 2 * rows, 2 * lanes),
        lambda s, me: (0, 0, lax.rem(me[0] + bands - s, bands), 0),
    )
    return pl.pallas_call(
        untile_kernel,
        grid_spec=pltpu.PrefetchScalarGridSpec(
            num_scalar_prefetch=1, grid=(bands,), in_specs=[block] * bands, out_specs=out
        ),
        out_shape=jax.ShapeDtypeStruct(shape, jnp.bfloat16),
        compiler_params=params(1),
        cost_estimate=cost(0, 4 * math.prod(shape)),
        name="untile",
    )(me, *pieces)


def order_of(size):
    return sorted(range(1, size), key=lambda s: -min(s, size - s))


def exchange(pieces, axis):
    size = lax.axis_size(axis)
    out = [pieces[0]] + [None] * (size - 1)
    for shift in order_of(size):
        pairs = [(i, (i + shift) % size) for i in range(size)]
        out[shift] = lax.ppermute(pieces[shift], axis, pairs)
    return out


def after(*values):
    return lax.optimization_barrier(values)


def over_grid(field):
    return lax.all_to_all(field, "grid", 0, 0, tiled=True)


def spread_sum(matrix, axis):
    flat = matrix.reshape(-1, LANES)
    size = lax.axis_size(axis)
    spread = jnp.broadcast_to(flat[None], (size,) + flat.shape)
    return jnp.sum(lax.all_to_all(spread, axis, 0, 0, tiled=True), axis=0).reshape(matrix.shape)


def mixing_kernel(own, me_ref, corr_ref, root_ref, scale_ref, mix_ref):
    correlation = corr_ref[...]
    count = correlation.shape[0]
    bands = count // own
    scale = jnp.max(jnp.sum(jnp.abs(correlation), axis=1, keepdims=True), axis=0, keepdims=True)
    at = lax.broadcasted_iota(jnp.int32, (count, count), 0)
    to = lax.broadcasted_iota(jnp.int32, (count, count), 1)
    identity = jnp.where(at == to, 1.0, 0.0)

    def full(a, b):
        return jnp.dot(a, b, precision=HIGHEST, preferred_element_type=jnp.float32)

    current = correlation / scale
    root = identity
    for _ in range(NS_ITERS):
        turn = 1.5 * identity - 0.5 * full(root, current)
        current = full(current, turn)
        root = full(turn, root)
    root_ref[...] = root
    scale_ref[...] = jnp.broadcast_to(scale, scale_ref.shape)
    coeff = root.astype(jnp.bfloat16)
    rows = mix_ref.shape[0]
    me = me_ref[0]
    who = lax.broadcasted_iota(jnp.int32, (count, rows), 0)
    place = lax.broadcasted_iota(jnp.int32, (count, rows), 1) // ROWS
    source = jnp.where(owner(place, me, own, bands, -1) == who, 1.0, 0.0).astype(jnp.bfloat16)
    target = jnp.where(owner(place, me, own, bands, 1) == who, 1.0, 0.0).astype(jnp.bfloat16)
    over_target = lax.dot_general(
        coeff, target, (((1,), (0,)), ((), ())), preferred_element_type=jnp.float32
    ).astype(jnp.bfloat16)
    mix = lax.dot_general(
        over_target, source, (((0,), (0,)), ((), ())), preferred_element_type=jnp.float32
    )
    at = lax.broadcasted_iota(jnp.int32, (rows, rows), 0)
    to = lax.broadcasted_iota(jnp.int32, (rows, rows), 1)
    mix_ref[...] = jnp.where(at % ROWS == to % ROWS, mix, 0.0).astype(jnp.bfloat16)


def mixing(me, own, correlation):
    count = correlation.shape[0]
    rows = count * ROWS
    vmem = pl.BlockSpec(memory_space=pltpu.VMEM)
    return pl.pallas_call(
        functools.partial(mixing_kernel, own),
        in_specs=[pl.BlockSpec(memory_space=pltpu.SMEM), vmem],
        out_specs=[vmem] * 3,
        out_shape=[
            jax.ShapeDtypeStruct((count, count), jnp.float32),
            jax.ShapeDtypeStruct((1, LANES), jnp.float32),
            jax.ShapeDtypeStruct((rows, rows), jnp.bfloat16),
        ],
        cost_estimate=cost(1e9, 1e6),
        name="mixing",
    )(me, correlation)


def project(inverse_root, hamil, scale):
    left = jnp.dot(inverse_root.T, hamil, precision=HIGHEST)
    return jnp.dot(left, inverse_root, precision=HIGHEST) / scale


def per_device(orbitals, potential):
    own, planes, height, depth = orbitals.shape
    bands = lax.axis_size("band")
    me = jnp.full((1,), lax.axis_index("band"), jnp.int32)
    kx_t = second_derivative(planes * lax.axis_size("grid")).T
    ky_t = second_derivative(height).T
    k_z = second_derivative(depth)

    start = tile(orbitals)
    line = over_grid(derive_lines(over_grid(start), kx_t))
    first = [first_step(o, start, line, potential, ky_t, k_z) for o in range(own)]
    turns, last = [], None
    for o in range(own):
        value = first[o] if last is None else after(first[o], last)[0]
        last = over_grid(value)
        turns.append(last)
    pieces, whole = [], []
    for o in range(own):
        last = over_grid(after(derive_lines(turns[o], kx_t), last)[0])
        cut, field = filtered_step(me, o, first[o], last, start, potential, ky_t, k_z, bands)
        pieces.append(cut)
        whole.append(field)
        last = field
    local = local_step(me, whole, potential, ky_t, k_z, bands)

    tiles = start.shape[0] // bands
    arrived = [exchange(cut, "band") for cut in pieces]
    f_views = [(arrived[o][s], 0) for s in range(bands) for o in range(own)]
    correlation = spread_sum(gram(me, own, tiles, f_views), "grid")
    correlation = spread_sum(correlation, "band")
    inverse_root, scale, mix = mixing(me, own, correlation)
    local = exchange(local, "band")
    g_views = [(local[s], o) for s in range(bands) for o in range(own)]
    back = exchange(rotate(mix, own, tiles, f_views), "band")
    rotated = untile(me, back, orbitals.shape)

    lines, _ = after(regroup(tiles, f_views), correlation)
    lines = over_grid(lines)
    hamil = gram(me, own, tiles, g_views, f_views) - 0.5 * line_gram(
        me, own, derive_lines(lines, kx_t), lines
    )
    hamil = spread_sum(spread_sum(hamil, "grid"), "band")
    projected = project(inverse_root, hamil, scale[0, 0])
    return (rotated, projected)


def solution(mesh):
    in_specs = (P("band", "grid", None, None), P("grid", None, None))
    out_specs = (P("band", "grid", None, None), P())
    return jax.shard_map(
        per_device, mesh=mesh, in_specs=in_specs, out_specs=out_specs, check_vma=False
    )
```

```python
import functools
import math

import jax
import jax.numpy as jnp
from jax import lax
from jax.experimental import pallas as pl
from jax.experimental.pallas import tpu as pltpu
from jax.sharding import PartitionSpec as P

NS_ITERS = 6

CENTER = 9.5
HALF_WIDTH = 6.5

ROWS = 16
LANES = 128
MOST_MIB = 63
STEP_MIB = 24
HIGHEST = lax.Precision.HIGHEST


def second_derivative(length):
    index = jnp.arange(length, dtype=jnp.int32)
    product = index[:, None] * index[None, :] % length
    angles = product.astype(jnp.float32) * (2.0 * math.pi / length)
    freq = jnp.minimum(index, length - index).astype(jnp.float32)
    weight = -((2.0 * math.pi / length * freq) ** 2) / length
    cosines = jnp.cos(angles)
    sines = jnp.sin(angles)
    matrix = jnp.dot(cosines * weight[None, :], cosines.T, precision=HIGHEST)
    matrix = matrix + jnp.dot(sines * weight[None, :], sines.T, precision=HIGHEST)
    return matrix.astype(jnp.bfloat16)


def dot(a, b):
    return jnp.dot(a, b, preferred_element_type=jnp.float32)


def dot_nt(a, b):
    return lax.dot_general(a, b, (((1,), (1,)), ((), ())), preferred_element_type=jnp.float32)


def params(dims, mib=MOST_MIB):
    return pltpu.CompilerParams(
        dimension_semantics=("arbitrary",) * dims, vmem_limit_bytes=mib * 1024 * 1024
    )


def cost(flops, bytes_accessed):
    return pl.CostEstimate(flops=int(flops), bytes_accessed=int(bytes_accessed), transcendentals=0)


def split_rows(ref, tile, orbital, plane):
    return jnp.concatenate(
        [ref[tile, orbital, plane], ref[tile + 1, orbital, plane]], axis=1
    )


def load_plane(ref, plane, orbital):
    tiles = ref.shape[0]
    value = ref[:, orbital, plane].reshape(tiles // 2, 2, ROWS, LANES)
    rows = tiles // 2 * ROWS
    return jnp.concatenate(
        [value[:, 0].reshape(rows, LANES), value[:, 1].reshape(rows, LANES)], axis=1
    )


def store_plane(ref, plane, value, orbital=0):
    tiles = ref.shape[0]
    left = value[:, :LANES].reshape(tiles // 2, 1, ROWS, LANES)
    right = value[:, LANES:].reshape(tiles // 2, 1, ROWS, LANES)
    ref[:, orbital, plane] = jnp.concatenate([left, right], axis=1).reshape(tiles, ROWS, LANES)


def lines_kernel(field_ref, k_ref, out_ref, work):
    blocks, _, planes, rows, lanes = field_ref.shape
    total = blocks * planes
    work[...] = field_ref[...].reshape(total * rows, lanes).astype(jnp.float32)
    matrix = k_ref[...]
    for row in range(0, rows, 2):
        here = pl.ds(row, total, stride=rows)
        there = pl.ds(row + 1, total, stride=rows)
        value = jnp.concatenate([work[here, :], work[there, :]], axis=1).astype(jnp.bfloat16)
        result = dot(matrix, value)
        work[here, :] = result[:, :lanes]
        work[there, :] = result[:, lanes:]
    out_ref[...] = work[...].astype(jnp.bfloat16).reshape(blocks, 1, planes, rows, lanes)


def derive_lines(field, k_t):
    blocks, count, planes, rows, lanes = field.shape
    block = pl.BlockSpec((blocks, 1, planes, rows, lanes), lambda i: (0, i, 0, 0, 0))
    size = field.size
    return pl.pallas_call(
        lines_kernel,
        grid=(count,),
        in_specs=[block, pl.BlockSpec(k_t.shape, lambda i: (0, 0))],
        out_specs=block,
        out_shape=jax.ShapeDtypeStruct(field.shape, jnp.bfloat16),
        scratch_shapes=[pltpu.VMEM((blocks * planes * rows, lanes), jnp.float32)],
        compiler_params=params(1, STEP_MIB),
        cost_estimate=cost(2 * size * blocks * planes, 4 * size),
        name="derive_lines",
    )(field, k_t)


def tile_kernel(in_ref, out_ref):
    tiles, count, planes, rows, lanes = out_ref.shape
    for tile in range(tiles):
        row, lane = tile // 2 * rows, tile % 2 * lanes
        out_ref[tile] = in_ref[:, :, row : row + rows, lane : lane + lanes]


def tile(orbitals, step=2):
    own, planes, height, depth = orbitals.shape
    tiles = height // ROWS * (depth // LANES)
    return pl.pallas_call(
        tile_kernel,
        grid=(planes // step,),
        in_specs=[pl.BlockSpec((own, step, height, depth), lambda x: (0, x, 0, 0))],
        out_specs=pl.BlockSpec((tiles, own, step, ROWS, LANES), lambda x: (0, 0, x, 0, 0)),
        out_shape=jax.ShapeDtypeStruct((tiles, own, planes, ROWS, LANES), orbitals.dtype),
        compiler_params=params(1, STEP_MIB),
        cost_estimate=cost(0, 4 * orbitals.size),
        name="tile",
    )(orbitals)


def local_terms(plane, ky_t, k_z):
    return dot(ky_t, plane) + dot(plane, k_z)


def each_plane(ref):
    return [(plane, o) for plane in range(ref.shape[2]) for o in range(ref.shape[1])]


def first_kernel(field_ref, line_ref, pot_ref, ky_ref, kz_ref, out_ref):
    for plane, o in each_plane(field_ref):
        field = load_plane(field_ref, plane, o)
        wide = field.astype(jnp.float32)
        line = load_plane(line_ref, plane, o).astype(jnp.float32)
        ham = -0.5 * (line + local_terms(field, ky_ref[...], kz_ref[...])) + pot_ref[plane] * wide
        value = (ham - CENTER * wide) * (1.0 / HALF_WIDTH)
        store_plane(out_ref, plane, value.astype(jnp.bfloat16), o)


def plane_specs(ky_t, potential, step):
    whole = pl.BlockSpec(ky_t.shape, lambda x: (0, 0))
    pot = pl.BlockSpec((step,) + potential.shape[1:], lambda x: (x, 0, 0))
    return [pot, whole, whole]


def planes_spec(field, step):
    tiles, count, _, rows, lanes = field.shape
    return pl.BlockSpec((tiles, count, step, rows, lanes), lambda x: (0, 0, x, 0, 0))


def first_step(field, line, potential, ky_t, k_z, step=2):
    size = field.size
    return pl.pallas_call(
        first_kernel,
        grid=(field.shape[2] // step,),
        in_specs=[planes_spec(field, step)] * 2 + plane_specs(ky_t, potential, step),
        out_specs=planes_spec(field, step),
        out_shape=jax.ShapeDtypeStruct(field.shape, jnp.bfloat16),
        compiler_params=params(1, STEP_MIB),
        cost_estimate=cost(4 * size * 256, 10 * size),
        name="first_step",
    )(field, line, potential, ky_t, k_z)


def store_pieces(me, refs, orbital, plane, work):
    bands = len(refs)
    span = work.shape[0] // bands
    for shift, ref in enumerate(refs):
        base = pl.multiple_of(lax.rem(me + shift, bands) * span, span)
        store_plane(ref, plane, work[pl.ds(base, span), :], orbital)


def filtered_kernel(me_ref, field_ref, line_ref, start_ref, pot_ref, ky_ref, kz_ref, *rest):
    piece_refs, out_ref, work = rest[:-2], rest[-2], rest[-1]
    for plane, o in each_plane(field_ref):
        field = load_plane(field_ref, plane, o)
        wide = field.astype(jnp.float32)
        line = load_plane(line_ref, plane, o).astype(jnp.float32)
        start = load_plane(start_ref, plane, o).astype(jnp.float32)
        ham = -0.5 * (line + local_terms(field, ky_ref[...], kz_ref[...])) + pot_ref[plane] * wide
        value = 2.0 * (ham - CENTER * wide) * (1.0 / HALF_WIDTH) - start
        value = value.astype(jnp.bfloat16)
        store_plane(out_ref, plane, value, o)
        work[...] = value
        store_pieces(me_ref[0], piece_refs, o, plane, work)


def pieces_of(field, bands):
    tiles, count, planes, rows, lanes = field.shape
    return jax.ShapeDtypeStruct((tiles // bands, count, planes, rows, lanes), jnp.bfloat16)


def filtered_step(me, field, line, start, potential, ky_t, k_z, bands, step=2):
    piece = pieces_of(field, bands)
    size = field.size
    out = pl.pallas_call(
        filtered_kernel,
        grid=(field.shape[2] // step,),
        in_specs=[pl.BlockSpec(memory_space=pltpu.SMEM)]
        + [planes_spec(field, step)] * 3
        + plane_specs(ky_t, potential, step),
        out_specs=[planes_spec(piece, step)] * bands + [planes_spec(field, step)],
        out_shape=[piece] * bands + [jax.ShapeDtypeStruct(field.shape, jnp.bfloat16)],
        scratch_shapes=[pltpu.VMEM(potential.shape[1:], jnp.bfloat16)],
        compiler_params=params(1),
        cost_estimate=cost(4 * size * 256, 14 * size),
        name="filtered_step",
    )(me, field, line, start, potential, ky_t, k_z)
    return (list(out[:bands]), out[bands])


def local_kernel(me_ref, field_ref, pot_ref, ky_ref, kz_ref, *rest):
    piece_refs, work = rest[:-1], rest[-1]
    for plane, o in each_plane(field_ref):
        field = load_plane(field_ref, plane, o)
        terms = local_terms(field, ky_ref[...], kz_ref[...])
        part = -0.5 * terms + pot_ref[plane] * field.astype(jnp.float32)
        work[...] = part.astype(jnp.bfloat16)
        store_pieces(me_ref[0], piece_refs, o, plane, work)


def local_step(me, field, potential, ky_t, k_z, bands, step=2):
    piece = pieces_of(field, bands)
    size = field.size
    out = pl.pallas_call(
        local_kernel,
        grid=(field.shape[2] // step,),
        in_specs=[pl.BlockSpec(memory_space=pltpu.SMEM), planes_spec(field, step)]
        + plane_specs(ky_t, potential, step),
        out_specs=[planes_spec(piece, step)] * bands,
        out_shape=[piece] * bands,
        scratch_shapes=[pltpu.VMEM(potential.shape[1:], jnp.bfloat16)],
        compiler_params=params(1),
        cost_estimate=cost(4 * size * 256, 8 * size),
        name="local_step",
    )(me, field, potential, ky_t, k_z)
    return list(out)


def chunk(refs, tile, plane):
    return jnp.concatenate(
        [split_rows(ref, tile, 0, plane) for ref in refs], axis=0
    )


def owner(place, me, own, bands, sign):
    return lax.rem(me + sign * (place // own) + bands, bands) * own + lax.rem(place, own)


def fold(product, me, out_ref, own, inner):
    rows = product.shape[0]
    count = out_ref.shape[0]
    at = lax.broadcasted_iota(jnp.int32, (rows, rows), 0)
    to = lax.broadcasted_iota(jnp.int32, (rows, rows), 1)
    who = lax.broadcasted_iota(jnp.int32, (count, rows), 0)
    row = lax.broadcasted_iota(jnp.int32, (count, rows), 1)
    if inner:
        same, place = at % ROWS == to % ROWS, row // ROWS
    else:
        same, place = at // ROWS == to // ROWS, row % ROWS
    kept = jnp.where(same, product, 0.0)
    pick = jnp.where(owner(place, me, own, count // own, -1) == who, 1.0, 0.0)
    half = jnp.dot(pick, kept, precision=HIGHEST, preferred_element_type=jnp.float32)
    out_ref[...] = lax.dot_general(
        half, pick, (((1,), (1,)), ((), ())), precision=HIGHEST, preferred_element_type=jnp.float32
    )


def gram_kernel(own, count, me_ref, *refs):
    refs, out_ref, work = refs[:-2], refs[-2], refs[-1]
    left, right = refs[:count], refs[-count:]

    @pl.when(pl.program_id(0) == 0)
    def _():
        work[...] = jnp.zeros_like(work)

    total = work[...]
    for plane in range(left[0].shape[2]):
        for tile in range(0, left[0].shape[0], 2):
            b = chunk(right, tile, plane)
            a = b if len(refs) == count else chunk(left, tile, plane)
            total = total + dot_nt(a, b)
    work[...] = total

    @pl.when(pl.program_id(0) == pl.num_programs(0) - 1)
    def _():
        fold(work[...], me_ref[0], out_ref, own, True)


def piece_spec(tiles, view, step):
    array, at = view
    _, _, _, rows, lanes = array.shape
    return pl.BlockSpec((tiles, 1, step, rows, lanes), lambda x: (0, at, x, 0, 0))


def gram(me, own, tiles, left, right=(), step=4):
    views = list(left) + list(right)
    _, _, planes, rows, lanes = views[0][0].shape
    total = len(left)
    size = tiles * planes * rows * lanes * total
    return pl.pallas_call(
        functools.partial(gram_kernel, own, total),
        grid=(planes // step,),
        in_specs=[pl.BlockSpec(memory_space=pltpu.SMEM)]
        + [piece_spec(tiles, view, step) for view in views],
        out_specs=pl.BlockSpec((total, total), lambda x: (0, 0)),
        out_shape=jax.ShapeDtypeStruct((total, total), jnp.float32),
        scratch_shapes=[pltpu.VMEM((total * rows, total * rows), jnp.float32)],
        compiler_params=params(1),
        cost_estimate=cost(2 * size * 256, 2 * size * (len(views) // total)),
        name="gram",
    )(me, *[view[0] for view in views])


def line_gram_kernel(own, me_ref, left_ref, right_ref, out_ref, work):
    @pl.when(pl.program_id(0) == 0)
    def _():
        work[...] = jnp.zeros_like(work)

    blocks, halves, planes, rows, lanes = left_ref.shape
    total = work[...]

    def rows_of(ref, at):
        return jnp.concatenate(
            [ref[at : at + 2, half].reshape(2 * planes * rows, lanes) for half in range(halves)], axis=1
        )

    for at in range(0, blocks, 2):
        total = total + dot_nt(rows_of(left_ref, at), rows_of(right_ref, at))
    work[...] = total

    @pl.when(pl.program_id(0) == pl.num_programs(0) - 1)
    def _():
        fold(work[...], me_ref[0], out_ref, own, False)


def line_gram(me, own, left, right, step=8):
    blocks, halves, planes, rows, lanes = left.shape
    block = pl.BlockSpec((step, halves, planes, rows, lanes), lambda x: (x, 0, 0, 0, 0))
    return pl.pallas_call(
        functools.partial(line_gram_kernel, own),
        grid=(blocks // step,),
        in_specs=[pl.BlockSpec(memory_space=pltpu.SMEM)] + [block] * 2,
        out_specs=pl.BlockSpec((rows, rows), lambda x: (0, 0)),
        out_shape=jax.ShapeDtypeStruct((rows, rows), jnp.float32),
        scratch_shapes=[pltpu.VMEM((2 * planes * rows, 2 * planes * rows), jnp.float32)],
        compiler_params=params(1),
        cost_estimate=cost(2 * left.size * 256, 4 * left.size),
        name="line_gram",
    )(me, left, right)


def regroup_kernel(*refs):
    work, out_ref, refs = refs[-1], refs[-2], refs[:-2]
    _, _, planes, rows, lanes = refs[0].shape
    each = planes * rows
    total = len(refs)
    for at, ref in enumerate(refs):
        work[at * each : (at + 1) * each, :] = ref[0, 0].reshape(each, lanes).astype(jnp.float32)
    half = rows // 2
    for plane in range(planes):
        for row in range(rows):
            value = work[pl.ds(plane * rows + row, total, stride=each), :]
            out_ref[row % half, row // half, plane] = value.astype(jnp.bfloat16)


def regroup(tiles, views):
    _, _, planes, rows, lanes = views[0][0].shape
    total = len(views)
    half = rows // 2

    def spec(at):
        return pl.BlockSpec((1, 1, planes, rows, lanes), lambda t: (t, at, 0, 0, 0))

    size = tiles * planes * rows * lanes * total
    return pl.pallas_call(
        regroup_kernel,
        grid=(tiles,),
        in_specs=[spec(at) for _, at in views],
        out_specs=pl.BlockSpec((half, 2, planes, total, lanes), lambda t: (t, 0, 0, 0, 0)),
        out_shape=jax.ShapeDtypeStruct((tiles * half, 2, planes, total, lanes), jnp.bfloat16),
        scratch_shapes=[pltpu.VMEM((total * planes * rows, lanes), jnp.float32)],
        compiler_params=params(1),
        cost_estimate=cost(size, 4 * size),
        name="regroup",
    )(*[view[0] for view in views])


def rotate_kernel(total, mix_ref, *refs):
    ins, outs = refs[:total], refs[total:]
    tiles, count, planes, rows, lanes = outs[0].shape
    for plane in range(planes):
        for tile in range(0, tiles, 2):
            value = dot(mix_ref[...], chunk(ins, tile, plane)).astype(jnp.bfloat16)
            for at, ref in enumerate(outs):
                for o in range(count):
                    start = (at * count + o) * rows
                    ref[tile, o, plane] = value[start : start + rows, :lanes]
                    ref[tile + 1, o, plane] = value[start : start + rows, lanes:]


def rotate(mix, own, tiles, views, step=4):
    _, _, planes, rows, lanes = views[0][0].shape
    total = len(views)
    out = pl.BlockSpec((tiles, own, step, rows, lanes), lambda x: (0, 0, x, 0, 0))
    shape = jax.ShapeDtypeStruct((tiles, own, planes, rows, lanes), jnp.bfloat16)
    size = tiles * planes * rows * lanes * total
    return pl.pallas_call(
        functools.partial(rotate_kernel, total),
        grid=(planes // step,),
        in_specs=[pl.BlockSpec(mix.shape, lambda x: (0, 0))]
        + [piece_spec(tiles, view, step) for view in views],
        out_specs=[out] * (total // own),
        out_shape=[shape] * (total // own),
        compiler_params=params(1),
        cost_estimate=cost(2 * size * 256, 4 * size),
        name="rotate",
    )(mix, *[view[0] for view in views])


def untile_kernel(me_ref, *refs):
    ins, out_ref = refs[:-1], refs[-1]
    for shift, ref in enumerate(ins):

        @pl.when(pl.program_id(0) == shift)
        def _(ref=ref):
            tiles, _, _, rows, lanes = ref.shape
            for tile in range(tiles):
                row, lane = tile // 2 * rows, tile % 2 * lanes
                out_ref[:, :, row : row + rows, lane : lane + lanes] = ref[tile]


def untile(me, pieces, shape):
    bands = len(pieces)
    tiles, count, planes, rows, lanes = pieces[0].shape
    block = pl.BlockSpec(pieces[0].shape, lambda s, me: (0, 0, 0, 0, 0))
    out = pl.BlockSpec(
        (count, planes, tiles // 2 * rows, 2 * lanes),
        lambda s, me: (0, 0, lax.rem(me[0] + bands - s, bands), 0),
    )
    return pl.pallas_call(
        untile_kernel,
        grid_spec=pltpu.PrefetchScalarGridSpec(
            num_scalar_prefetch=1, grid=(bands,), in_specs=[block] * bands, out_specs=out
        ),
        out_shape=jax.ShapeDtypeStruct(shape, jnp.bfloat16),
        compiler_params=params(1),
        cost_estimate=cost(0, 4 * math.prod(shape)),
        name="untile",
    )(me, *pieces)


def order_of(size):
    return sorted(range(1, size), key=lambda s: -min(s, size - s))


def exchange(pieces, axis):
    size = lax.axis_size(axis)
    out = [pieces[0]] + [None] * (size - 1)
    for shift in order_of(size):
        pairs = [(i, (i + shift) % size) for i in range(size)]
        out[shift] = lax.ppermute(pieces[shift], axis, pairs)
    return out


def after(*values):
    return lax.optimization_barrier(values)


def over_grid(field):
    return lax.all_to_all(field, "grid", 0, 0, tiled=True)


def small_sum(matrix):
    axes = ("band", "grid")
    flat = matrix.reshape(-1, LANES)
    spread = jnp.broadcast_to(flat[None], (lax.axis_size(axes),) + flat.shape)
    return jnp.sum(lax.all_to_all(spread, axes, 0, 0, tiled=True), axis=0).reshape(matrix.shape)


def mixing_kernel(own, me_ref, corr_ref, root_ref, scale_ref, mix_ref):
    correlation = corr_ref[...]
    count = correlation.shape[0]
    bands = count // own
    scale = jnp.max(jnp.sum(jnp.abs(correlation), axis=1, keepdims=True), axis=0, keepdims=True)
    at = lax.broadcasted_iota(jnp.int32, (count, count), 0)
    to = lax.broadcasted_iota(jnp.int32, (count, count), 1)
    identity = jnp.where(at == to, 1.0, 0.0)

    def full(a, b):
        return jnp.dot(a, b, precision=HIGHEST, preferred_element_type=jnp.float32)

    current = correlation / scale
    root = identity
    for _ in range(NS_ITERS):
        turn = 1.5 * identity - 0.5 * full(root, current)
        current = full(current, turn)
        root = full(turn, root)
    root_ref[...] = root
    scale_ref[...] = jnp.broadcast_to(scale, scale_ref.shape)
    coeff = root.astype(jnp.bfloat16)
    rows = mix_ref.shape[0]
    me = me_ref[0]
    who = lax.broadcasted_iota(jnp.int32, (count, rows), 0)
    place = lax.broadcasted_iota(jnp.int32, (count, rows), 1) // ROWS
    source = jnp.where(owner(place, me, own, bands, -1) == who, 1.0, 0.0).astype(jnp.bfloat16)
    target = jnp.where(owner(place, me, own, bands, 1) == who, 1.0, 0.0).astype(jnp.bfloat16)
    over_target = lax.dot_general(
        coeff, target, (((1,), (0,)), ((), ())), preferred_element_type=jnp.float32
    ).astype(jnp.bfloat16)
    mix = lax.dot_general(
        over_target, source, (((0,), (0,)), ((), ())), preferred_element_type=jnp.float32
    )
    at = lax.broadcasted_iota(jnp.int32, (rows, rows), 0)
    to = lax.broadcasted_iota(jnp.int32, (rows, rows), 1)
    mix_ref[...] = jnp.where(at % ROWS == to % ROWS, mix, 0.0).astype(jnp.bfloat16)


def mixing(me, own, correlation):
    count = correlation.shape[0]
    rows = count * ROWS
    vmem = pl.BlockSpec(memory_space=pltpu.VMEM)
    return pl.pallas_call(
        functools.partial(mixing_kernel, own),
        in_specs=[pl.BlockSpec(memory_space=pltpu.SMEM), vmem],
        out_specs=[vmem] * 3,
        out_shape=[
            jax.ShapeDtypeStruct((count, count), jnp.float32),
            jax.ShapeDtypeStruct((1, LANES), jnp.float32),
            jax.ShapeDtypeStruct((rows, rows), jnp.bfloat16),
        ],
        cost_estimate=cost(1e9, 1e6),
        name="mixing",
    )(me, correlation)


def project(inverse_root, hamil, scale):
    left = jnp.dot(inverse_root.T, hamil, precision=HIGHEST)
    return jnp.dot(left, inverse_root, precision=HIGHEST) / scale


def per_device(orbitals, potential):
    own, planes, height, depth = orbitals.shape
    bands = lax.axis_size("band")
    me = jnp.full((1,), lax.axis_index("band"), jnp.int32)
    kx_t = second_derivative(planes * lax.axis_size("grid")).T
    ky_t = second_derivative(height).T
    k_z = second_derivative(depth)

    start = tile(orbitals)
    line = over_grid(derive_lines(over_grid(start), kx_t))
    first = first_step(start, line, potential, ky_t, k_z)
    line = over_grid(derive_lines(over_grid(first), kx_t))
    pieces, whole = filtered_step(me, first, line, start, potential, ky_t, k_z, bands)

    tiles = start.shape[0] // bands
    arrived = exchange(pieces, "band")
    local = exchange(local_step(me, whole, potential, ky_t, k_z, bands), "band")
    f_views = [(arrived[s], o) for s in range(bands) for o in range(own)]
    correlation = small_sum(gram(me, own, tiles, f_views))
    far = order_of(bands)[: bands // 2 - 1]
    tied = after(correlation, *[local[s] for s in far])
    correlation = tied[0]
    for s, piece in zip(far, tied[1:]):
        local[s] = piece
    inverse_root, scale, mix = mixing(me, own, correlation)
    g_views = [(local[s], o) for s in range(bands) for o in range(own)]
    back = exchange(rotate(mix, own, tiles, f_views), "band")
    rotated = untile(me, back, orbitals.shape)

    lines, _ = after(regroup(tiles, f_views), correlation)
    lines, _ = after(over_grid(lines), back[far[0]])
    hamil = gram(me, own, tiles, g_views, f_views) - 0.5 * line_gram(
        me, own, derive_lines(lines, kx_t), lines
    )
    projected = project(inverse_root, small_sum(hamil), scale[0, 0])
    return (rotated, projected)


def solution(mesh):
    in_specs = (P("band", "grid", None, None), P("grid", None, None))
    out_specs = (P("band", "grid", None, None), P())
    return jax.shard_map(
        per_device, mesh=mesh, in_specs=in_specs, out_specs=out_specs, check_vma=False
    )
```

```python
import functools
import math

import jax
import jax.numpy as jnp
from jax import lax
from jax.experimental import pallas as pl
from jax.experimental.pallas import tpu as pltpu
from jax.sharding import PartitionSpec as P

NS_ITERS = 6

CENTER = 9.5
HALF_WIDTH = 6.5

ROWS = 16
LANES = 128
MOST_MIB = 63
STEP_MIB = 24
HIGHEST = lax.Precision.HIGHEST


def second_derivative(length):
    index = jnp.arange(length, dtype=jnp.int32)
    product = index[:, None] * index[None, :] % length
    angles = product.astype(jnp.float32) * (2.0 * math.pi / length)
    freq = jnp.minimum(index, length - index).astype(jnp.float32)
    weight = -((2.0 * math.pi / length * freq) ** 2) / length
    cosines = jnp.cos(angles)
    sines = jnp.sin(angles)
    matrix = jnp.dot(cosines * weight[None, :], cosines.T, precision=HIGHEST)
    matrix = matrix + jnp.dot(sines * weight[None, :], sines.T, precision=HIGHEST)
    return matrix.astype(jnp.bfloat16)


def dot(a, b):
    return jnp.dot(a, b, preferred_element_type=jnp.float32)


def dot_nt(a, b):
    return lax.dot_general(a, b, (((1,), (1,)), ((), ())), preferred_element_type=jnp.float32)


def params(dims, mib=MOST_MIB):
    return pltpu.CompilerParams(
        dimension_semantics=("arbitrary",) * dims, vmem_limit_bytes=mib * 1024 * 1024
    )


def cost(flops, bytes_accessed):
    return pl.CostEstimate(flops=int(flops), bytes_accessed=int(bytes_accessed), transcendentals=0)


def split_rows(ref, tile, orbital, plane):
    return jnp.concatenate(
        [ref[tile, orbital, plane], ref[tile + 1, orbital, plane]], axis=1
    )


def load_plane(ref, plane, orbital):
    tiles = ref.shape[0]
    value = ref[:, orbital, plane].reshape(tiles // 2, 2, ROWS, LANES)
    rows = tiles // 2 * ROWS
    return jnp.concatenate(
        [value[:, 0].reshape(rows, LANES), value[:, 1].reshape(rows, LANES)], axis=1
    )


def store_plane(ref, plane, value, orbital=0):
    tiles = ref.shape[0]
    left = value[:, :LANES].reshape(tiles // 2, 1, ROWS, LANES)
    right = value[:, LANES:].reshape(tiles // 2, 1, ROWS, LANES)
    ref[:, orbital, plane] = jnp.concatenate([left, right], axis=1).reshape(tiles, ROWS, LANES)


def derive_rows(work, matrix, rows):
    total = work.shape[0] // rows
    lanes = work.shape[1]
    for row in range(0, rows, 2):
        here = pl.ds(row, total, stride=rows)
        there = pl.ds(row + 1, total, stride=rows)
        value = jnp.concatenate([work[here, :], work[there, :]], axis=1).astype(jnp.bfloat16)
        result = dot(matrix, value)
        work[here, :] = result[:, :lanes]
        work[there, :] = result[:, lanes:]


def lines_kernel(field_ref, k_ref, out_ref, work):
    blocks, _, planes, rows, lanes = field_ref.shape
    work[...] = field_ref[...].reshape(blocks * planes * rows, lanes).astype(jnp.float32)
    derive_rows(work, k_ref[...], rows)
    out_ref[...] = work[...].astype(jnp.bfloat16).reshape(blocks, 1, planes, rows, lanes)


def derive_lines(field, k_t):
    blocks, count, planes, rows, lanes = field.shape
    block = pl.BlockSpec((blocks, 1, planes, rows, lanes), lambda i: (0, i, 0, 0, 0))
    size = field.size
    return pl.pallas_call(
        lines_kernel,
        grid=(count,),
        in_specs=[block, pl.BlockSpec(k_t.shape, lambda i: (0, 0))],
        out_specs=block,
        out_shape=jax.ShapeDtypeStruct(field.shape, jnp.bfloat16),
        scratch_shapes=[pltpu.VMEM((blocks * planes * rows, lanes), jnp.float32)],
        compiler_params=params(1, STEP_MIB),
        cost_estimate=cost(2 * size * blocks * planes, 4 * size),
        name="derive_lines",
    )(field, k_t)


def tile_kernel(in_ref, out_ref):
    tiles, count, planes, rows, lanes = out_ref.shape
    for tile in range(tiles):
        row, lane = tile // 2 * rows, tile % 2 * lanes
        out_ref[tile] = in_ref[:, :, row : row + rows, lane : lane + lanes]


def tile(orbitals, step=2):
    own, planes, height, depth = orbitals.shape
    tiles = height // ROWS * (depth // LANES)
    return pl.pallas_call(
        tile_kernel,
        grid=(planes // step,),
        in_specs=[pl.BlockSpec((own, step, height, depth), lambda x: (0, x, 0, 0))],
        out_specs=pl.BlockSpec((tiles, own, step, ROWS, LANES), lambda x: (0, 0, x, 0, 0)),
        out_shape=jax.ShapeDtypeStruct((tiles, own, planes, ROWS, LANES), orbitals.dtype),
        compiler_params=params(1, STEP_MIB),
        cost_estimate=cost(0, 4 * orbitals.size),
        name="tile",
    )(orbitals)


def local_terms(plane, ky_t, k_z):
    return dot(ky_t, plane) + dot(plane, k_z)


def each_plane(ref):
    return [(plane, o) for plane in range(ref.shape[2]) for o in range(ref.shape[1])]


def first_kernel(field_ref, line_ref, pot_ref, ky_ref, kz_ref, out_ref):
    for plane, o in each_plane(field_ref):
        field = load_plane(field_ref, plane, o)
        wide = field.astype(jnp.float32)
        line = load_plane(line_ref, plane, o).astype(jnp.float32)
        ham = -0.5 * (line + local_terms(field, ky_ref[...], kz_ref[...])) + pot_ref[plane] * wide
        value = (ham - CENTER * wide) * (1.0 / HALF_WIDTH)
        store_plane(out_ref, plane, value.astype(jnp.bfloat16), o)


def plane_specs(ky_t, potential, step):
    whole = pl.BlockSpec(ky_t.shape, lambda x: (0, 0))
    pot = pl.BlockSpec((step,) + potential.shape[1:], lambda x: (x, 0, 0))
    return [pot, whole, whole]


def planes_spec(field, step):
    tiles, count, _, rows, lanes = field.shape
    return pl.BlockSpec((tiles, count, step, rows, lanes), lambda x: (0, 0, x, 0, 0))


def first_step(field, line, potential, ky_t, k_z, step=2):
    size = field.size
    return pl.pallas_call(
        first_kernel,
        grid=(field.shape[2] // step,),
        in_specs=[planes_spec(field, step)] * 2 + plane_specs(ky_t, potential, step),
        out_specs=planes_spec(field, step),
        out_shape=jax.ShapeDtypeStruct(field.shape, jnp.bfloat16),
        compiler_params=params(1, STEP_MIB),
        cost_estimate=cost(4 * size * 256, 10 * size),
        name="first_step",
    )(field, line, potential, ky_t, k_z)


def store_pieces(me, refs, orbital, plane, work):
    bands = len(refs)
    span = work.shape[0] // bands
    for shift, ref in enumerate(refs):
        base = pl.multiple_of(lax.rem(me + shift, bands) * span, span)
        store_plane(ref, plane, work[pl.ds(base, span), :], orbital)


def filtered_kernel(me_ref, field_ref, line_ref, start_ref, pot_ref, ky_ref, kz_ref, *rest):
    piece_refs, out_ref, work = rest[:-2], rest[-2], rest[-1]
    for plane, o in each_plane(field_ref):
        field = load_plane(field_ref, plane, o)
        wide = field.astype(jnp.float32)
        line = load_plane(line_ref, plane, o).astype(jnp.float32)
        start = load_plane(start_ref, plane, o).astype(jnp.float32)
        ham = -0.5 * (line + local_terms(field, ky_ref[...], kz_ref[...])) + pot_ref[plane] * wide
        value = 2.0 * (ham - CENTER * wide) * (1.0 / HALF_WIDTH) - start
        value = value.astype(jnp.bfloat16)
        store_plane(out_ref, plane, value, o)
        work[...] = value
        store_pieces(me_ref[0], piece_refs, o, plane, work)


def pieces_of(field, bands):
    tiles, count, planes, rows, lanes = field.shape
    return jax.ShapeDtypeStruct((tiles // bands, count, planes, rows, lanes), jnp.bfloat16)


def filtered_step(me, field, line, start, potential, ky_t, k_z, bands, step=2):
    piece = pieces_of(field, bands)
    size = field.size
    out = pl.pallas_call(
        filtered_kernel,
        grid=(field.shape[2] // step,),
        in_specs=[pl.BlockSpec(memory_space=pltpu.SMEM)]
        + [planes_spec(field, step)] * 3
        + plane_specs(ky_t, potential, step),
        out_specs=[planes_spec(piece, step)] * bands + [planes_spec(field, step)],
        out_shape=[piece] * bands + [jax.ShapeDtypeStruct(field.shape, jnp.bfloat16)],
        scratch_shapes=[pltpu.VMEM(potential.shape[1:], jnp.bfloat16)],
        compiler_params=params(1),
        cost_estimate=cost(4 * size * 256, 14 * size),
        name="filtered_step",
    )(me, field, line, start, potential, ky_t, k_z)
    return (list(out[:bands]), out[bands])


def local_kernel(me_ref, field_ref, pot_ref, ky_ref, kz_ref, *rest):
    piece_refs, work = rest[:-1], rest[-1]
    for plane, o in each_plane(field_ref):
        field = load_plane(field_ref, plane, o)
        terms = local_terms(field, ky_ref[...], kz_ref[...])
        part = -0.5 * terms + pot_ref[plane] * field.astype(jnp.float32)
        work[...] = part.astype(jnp.bfloat16)
        store_pieces(me_ref[0], piece_refs, o, plane, work)


def local_step(me, field, potential, ky_t, k_z, bands, step=2):
    piece = pieces_of(field, bands)
    size = field.size
    out = pl.pallas_call(
        local_kernel,
        grid=(field.shape[2] // step,),
        in_specs=[pl.BlockSpec(memory_space=pltpu.SMEM), planes_spec(field, step)]
        + plane_specs(ky_t, potential, step),
        out_specs=[planes_spec(piece, step)] * bands,
        out_shape=[piece] * bands,
        scratch_shapes=[pltpu.VMEM(potential.shape[1:], jnp.bfloat16)],
        compiler_params=params(1),
        cost_estimate=cost(4 * size * 256, 8 * size),
        name="local_step",
    )(me, field, potential, ky_t, k_z)
    return list(out)


def chunk(refs, tile, plane):
    return jnp.concatenate(
        [split_rows(ref, tile, 0, plane) for ref in refs], axis=0
    )


def owner(place, me, own, bands, sign):
    return lax.rem(me + sign * (place // own) + bands, bands) * own + lax.rem(place, own)


def fold(product, me, out_ref, own, inner):
    rows = product.shape[0]
    count = out_ref.shape[0]
    at = lax.broadcasted_iota(jnp.int32, (rows, rows), 0)
    to = lax.broadcasted_iota(jnp.int32, (rows, rows), 1)
    who = lax.broadcasted_iota(jnp.int32, (count, rows), 0)
    row = lax.broadcasted_iota(jnp.int32, (count, rows), 1)
    if inner:
        same, place = at % ROWS == to % ROWS, row // ROWS
    else:
        same, place = at // ROWS == to // ROWS, row % ROWS
    kept = jnp.where(same, product, 0.0)
    pick = jnp.where(owner(place, me, own, count // own, -1) == who, 1.0, 0.0)
    half = jnp.dot(pick, kept, precision=HIGHEST, preferred_element_type=jnp.float32)
    out_ref[...] = lax.dot_general(
        half, pick, (((1,), (1,)), ((), ())), precision=HIGHEST, preferred_element_type=jnp.float32
    )


def gram_kernel(own, count, me_ref, *refs):
    refs, out_ref, work = refs[:-2], refs[-2], refs[-1]
    left, right = refs[:count], refs[-count:]

    @pl.when(pl.program_id(0) == 0)
    def _():
        work[...] = jnp.zeros_like(work)

    total = work[...]
    for plane in range(left[0].shape[2]):
        for tile in range(0, left[0].shape[0], 2):
            b = chunk(right, tile, plane)
            a = b if len(refs) == count else chunk(left, tile, plane)
            total = total + dot_nt(a, b)
    work[...] = total

    @pl.when(pl.program_id(0) == pl.num_programs(0) - 1)
    def _():
        fold(work[...], me_ref[0], out_ref, own, True)


def piece_spec(tiles, view, step):
    array, at = view
    _, _, _, rows, lanes = array.shape
    return pl.BlockSpec((tiles, 1, step, rows, lanes), lambda x: (0, at, x, 0, 0))


def gram(me, own, tiles, left, right=(), step=4):
    views = list(left) + list(right)
    _, _, planes, rows, lanes = views[0][0].shape
    total = len(left)
    size = tiles * planes * rows * lanes * total
    return pl.pallas_call(
        functools.partial(gram_kernel, own, total),
        grid=(planes // step,),
        in_specs=[pl.BlockSpec(memory_space=pltpu.SMEM)]
        + [piece_spec(tiles, view, step) for view in views],
        out_specs=pl.BlockSpec((total, total), lambda x: (0, 0)),
        out_shape=jax.ShapeDtypeStruct((total, total), jnp.float32),
        scratch_shapes=[pltpu.VMEM((total * rows, total * rows), jnp.float32)],
        compiler_params=params(1),
        cost_estimate=cost(2 * size * 256, 2 * size * (len(views) // total)),
        name="gram",
    )(me, *[view[0] for view in views])


def line_gram_kernel(own, me_ref, field_ref, k_ref, out_ref, work, derived):
    blocks, halves, planes, rows, lanes = field_ref.shape
    for half in range(halves):
        work[...] = field_ref[:, half].reshape(blocks * planes * rows, lanes).astype(jnp.float32)
        derive_rows(work, k_ref[...], rows)
        derived[half] = work[...].astype(jnp.bfloat16)
    step = rows * rows
    total = jnp.zeros((step, step), jnp.float32)
    each = step // (planes * rows)
    for at in range(0, blocks, each):
        start = at * planes * rows
        left = [derived[half, start : start + step] for half in range(halves)]
        right = [field_ref[at : at + each, half].reshape(step, lanes) for half in range(halves)]
        total = total + dot_nt(jnp.concatenate(left, axis=1), jnp.concatenate(right, axis=1))
    fold(total, me_ref[0], out_ref, own, False)


def line_gram(me, own, field, k_t):
    blocks, halves, planes, rows, lanes = field.shape
    vmem = pl.BlockSpec(memory_space=pltpu.VMEM)
    size = blocks * planes * rows
    return pl.pallas_call(
        functools.partial(line_gram_kernel, own),
        in_specs=[pl.BlockSpec(memory_space=pltpu.SMEM), vmem, vmem],
        out_specs=vmem,
        out_shape=jax.ShapeDtypeStruct((rows, rows), jnp.float32),
        scratch_shapes=[
            pltpu.VMEM((size, lanes), jnp.float32),
            pltpu.VMEM((halves, size, lanes), jnp.bfloat16),
        ],
        compiler_params=pltpu.CompilerParams(vmem_limit_bytes=STEP_MIB * 1024 * 1024),
        cost_estimate=cost(4 * field.size * 256, 2 * field.size),
        name="line_gram",
    )(me, field, k_t)


def regroup_kernel(*refs):
    work, out_ref, refs = refs[-1], refs[-2], refs[:-2]
    _, _, planes, rows, lanes = refs[0].shape
    each = planes * rows
    total = len(refs)
    for at, ref in enumerate(refs):
        work[at * each : (at + 1) * each, :] = ref[0, 0].reshape(each, lanes).astype(jnp.float32)
    half = rows // 2
    for plane in range(planes):
        for row in range(rows):
            value = work[pl.ds(plane * rows + row, total, stride=each), :]
            out_ref[row % half, row // half, plane] = value.astype(jnp.bfloat16)


def regroup(tiles, views):
    _, _, planes, rows, lanes = views[0][0].shape
    total = len(views)
    half = rows // 2

    def spec(at):
        return pl.BlockSpec((1, 1, planes, rows, lanes), lambda t: (t, at, 0, 0, 0))

    size = tiles * planes * rows * lanes * total
    return pl.pallas_call(
        regroup_kernel,
        grid=(tiles,),
        in_specs=[spec(at) for _, at in views],
        out_specs=pl.BlockSpec((half, 2, planes, total, lanes), lambda t: (t, 0, 0, 0, 0)),
        out_shape=jax.ShapeDtypeStruct((tiles * half, 2, planes, total, lanes), jnp.bfloat16),
        scratch_shapes=[pltpu.VMEM((total * planes * rows, lanes), jnp.float32)],
        compiler_params=params(1),
        cost_estimate=cost(size, 4 * size),
        name="regroup",
    )(*[view[0] for view in views])


def rotate_kernel(total, mix_ref, *refs):
    ins, outs = refs[:total], refs[total:]
    tiles, count, planes, rows, lanes = outs[0].shape
    for plane in range(planes):
        for tile in range(0, tiles, 2):
            value = dot(mix_ref[...], chunk(ins, tile, plane)).astype(jnp.bfloat16)
            for at, ref in enumerate(outs):
                for o in range(count):
                    start = (at * count + o) * rows
                    ref[tile, o, plane] = value[start : start + rows, :lanes]
                    ref[tile + 1, o, plane] = value[start : start + rows, lanes:]


def rotate(mix, own, tiles, views, step=4):
    _, _, planes, rows, lanes = views[0][0].shape
    total = len(views)
    out = pl.BlockSpec((tiles, own, step, rows, lanes), lambda x: (0, 0, x, 0, 0))
    shape = jax.ShapeDtypeStruct((tiles, own, planes, rows, lanes), jnp.bfloat16)
    size = tiles * planes * rows * lanes * total
    return pl.pallas_call(
        functools.partial(rotate_kernel, total),
        grid=(planes // step,),
        in_specs=[pl.BlockSpec(mix.shape, lambda x: (0, 0))]
        + [piece_spec(tiles, view, step) for view in views],
        out_specs=[out] * (total // own),
        out_shape=[shape] * (total // own),
        compiler_params=params(1),
        cost_estimate=cost(2 * size * 256, 4 * size),
        name="rotate",
    )(mix, *[view[0] for view in views])


def untile_kernel(me_ref, *refs):
    ins, out_ref = refs[:-1], refs[-1]
    for shift, ref in enumerate(ins):

        @pl.when(pl.program_id(0) == shift)
        def _(ref=ref):
            tiles, _, _, rows, lanes = ref.shape
            for tile in range(tiles):
                row, lane = tile // 2 * rows, tile % 2 * lanes
                out_ref[:, :, row : row + rows, lane : lane + lanes] = ref[tile]


def untile(me, pieces, shape):
    bands = len(pieces)
    tiles, count, planes, rows, lanes = pieces[0].shape
    block = pl.BlockSpec(pieces[0].shape, lambda s, me: (0, 0, 0, 0, 0))
    out = pl.BlockSpec(
        (count, planes, tiles // 2 * rows, 2 * lanes),
        lambda s, me: (0, 0, lax.rem(me[0] + bands - s, bands), 0),
    )
    return pl.pallas_call(
        untile_kernel,
        grid_spec=pltpu.PrefetchScalarGridSpec(
            num_scalar_prefetch=1, grid=(bands,), in_specs=[block] * bands, out_specs=out
        ),
        out_shape=jax.ShapeDtypeStruct(shape, jnp.bfloat16),
        compiler_params=params(1),
        cost_estimate=cost(0, 4 * math.prod(shape)),
        name="untile",
    )(me, *pieces)


def order_of(size):
    return sorted(range(1, size), key=lambda s: -min(s, size - s))


def exchange(pieces, axis):
    size = lax.axis_size(axis)
    out = [pieces[0]] + [None] * (size - 1)
    for shift in order_of(size):
        pairs = [(i, (i + shift) % size) for i in range(size)]
        out[shift] = lax.ppermute(pieces[shift], axis, pairs)
    return out


def after(*values):
    return lax.optimization_barrier(values)


def over_grid(field):
    return lax.all_to_all(field, "grid", 0, 0, tiled=True)


def small_sum(matrix):
    axes = ("band", "grid")
    flat = matrix.reshape(-1, LANES)
    spread = jnp.broadcast_to(flat[None], (lax.axis_size(axes),) + flat.shape)
    return jnp.sum(lax.all_to_all(spread, axes, 0, 0, tiled=True), axis=0).reshape(matrix.shape)


def spread_sum(matrix, axis):
    flat = matrix.reshape(-1, LANES)
    spread = jnp.broadcast_to(flat[None], (lax.axis_size(axis),) + flat.shape)
    return jnp.sum(lax.all_to_all(spread, axis, 0, 0, tiled=True), axis=0).reshape(matrix.shape)


def mixing_kernel(own, me_ref, corr_ref, root_ref, scale_ref, mix_ref):
    correlation = corr_ref[...]
    count = correlation.shape[0]
    bands = count // own
    scale = jnp.max(jnp.sum(jnp.abs(correlation), axis=1, keepdims=True), axis=0, keepdims=True)
    at = lax.broadcasted_iota(jnp.int32, (count, count), 0)
    to = lax.broadcasted_iota(jnp.int32, (count, count), 1)
    identity = jnp.where(at == to, 1.0, 0.0)

    def full(a, b):
        return jnp.dot(a, b, precision=HIGHEST, preferred_element_type=jnp.float32)

    current = correlation / scale
    root = identity
    for _ in range(NS_ITERS):
        turn = 1.5 * identity - 0.5 * full(root, current)
        current = full(current, turn)
        root = full(turn, root)
    root_ref[...] = root
    scale_ref[...] = jnp.broadcast_to(scale, scale_ref.shape)
    coeff = root.astype(jnp.bfloat16)
    rows = mix_ref.shape[0]
    me = me_ref[0]
    who = lax.broadcasted_iota(jnp.int32, (count, rows), 0)
    place = lax.broadcasted_iota(jnp.int32, (count, rows), 1) // ROWS
    source = jnp.where(owner(place, me, own, bands, -1) == who, 1.0, 0.0).astype(jnp.bfloat16)
    target = jnp.where(owner(place, me, own, bands, 1) == who, 1.0, 0.0).astype(jnp.bfloat16)
    over_target = lax.dot_general(
        coeff, target, (((1,), (0,)), ((), ())), preferred_element_type=jnp.float32
    ).astype(jnp.bfloat16)
    mix = lax.dot_general(
        over_target, source, (((0,), (0,)), ((), ())), preferred_element_type=jnp.float32
    )
    at = lax.broadcasted_iota(jnp.int32, (rows, rows), 0)
    to = lax.broadcasted_iota(jnp.int32, (rows, rows), 1)
    mix_ref[...] = jnp.where(at % ROWS == to % ROWS, mix, 0.0).astype(jnp.bfloat16)


def mixing(me, own, correlation):
    count = correlation.shape[0]
    rows = count * ROWS
    vmem = pl.BlockSpec(memory_space=pltpu.VMEM)
    return pl.pallas_call(
        functools.partial(mixing_kernel, own),
        in_specs=[pl.BlockSpec(memory_space=pltpu.SMEM), vmem],
        out_specs=[vmem] * 3,
        out_shape=[
            jax.ShapeDtypeStruct((count, count), jnp.float32),
            jax.ShapeDtypeStruct((1, LANES), jnp.float32),
            jax.ShapeDtypeStruct((rows, rows), jnp.bfloat16),
        ],
        cost_estimate=cost(1e9, 1e6),
        name="mixing",
    )(me, correlation)


def project(inverse_root, hamil, scale):
    left = jnp.dot(inverse_root.T, hamil, precision=HIGHEST)
    return jnp.dot(left, inverse_root, precision=HIGHEST) / scale


def per_device(orbitals, potential):
    own, planes, height, depth = orbitals.shape
    bands = lax.axis_size("band")
    me = jnp.full((1,), lax.axis_index("band"), jnp.int32)
    kx_t = second_derivative(planes * lax.axis_size("grid")).T
    ky_t = second_derivative(height).T
    k_z = second_derivative(depth)

    start = tile(orbitals)
    line = over_grid(derive_lines(over_grid(start), kx_t))
    first = first_step(start, line, potential, ky_t, k_z)
    line = over_grid(derive_lines(over_grid(first), kx_t))
    pieces, whole = filtered_step(me, first, line, start, potential, ky_t, k_z, bands)

    tiles = start.shape[0] // bands
    order = order_of(bands)
    far, near = order[: bands // 2 - 1], order[bands // 2 - 1 :]
    arrived = exchange(pieces, "band")
    local_pieces = local_step(me, whole, potential, ky_t, k_z, bands)
    arrived[far[0]] = after(arrived[far[0]], *local_pieces)[0]
    local = exchange(local_pieces, "band")
    f_views = [(arrived[s], o) for s in range(bands) for o in range(own)]
    correlation = spread_sum(gram(me, own, tiles, f_views), "grid")
    tied = after(correlation, *[local[s] for s in far])
    correlation = tied[0]
    for s, piece in zip(far, tied[1:]):
        local[s] = piece
    correlation = spread_sum(correlation, "band")
    tied = after(correlation, *[local[s] for s in near])
    correlation = tied[0]
    for s, piece in zip(near, tied[1:]):
        local[s] = piece
    inverse_root, scale, mix = mixing(me, own, correlation)
    back = exchange(rotate(mix, own, tiles, f_views), "band")
    rotated = untile(me, back, orbitals.shape)
    g_views = [(local[s], o) for s in range(bands) for o in range(own)]
    lines, _ = after(regroup(tiles, f_views), correlation)
    lines = after(over_grid(lines), back[far[0]], back[far[1]])[0]
    hamil = gram(me, own, tiles, g_views, f_views) - 0.5 * line_gram(me, own, lines, kx_t)
    hamil = after(hamil, *[back[s] for s in order[: bands // 2 + 1]])[0]
    projected = project(inverse_root, small_sum(hamil), scale[0, 0])
    return (rotated, projected)


def solution(mesh):
    in_specs = (P("band", "grid", None, None), P("grid", None, None))
    out_specs = (P("band", "grid", None, None), P())
    return jax.shard_map(
        per_device, mesh=mesh, in_specs=in_specs, out_specs=out_specs, check_vma=False
    )
```

```python
import functools
import math

import jax
import jax.numpy as jnp
from jax import lax
from jax.experimental import pallas as pl
from jax.experimental.pallas import tpu as pltpu
from jax.sharding import PartitionSpec as P

NS_ITERS = 6

CENTER = 9.5
HALF_WIDTH = 6.5

ROWS = 16
LANES = 128
MOST_MIB = 63
STEP_MIB = 24
HIGHEST = lax.Precision.HIGHEST


def second_derivative(length):
    index = jnp.arange(length, dtype=jnp.int32)
    product = index[:, None] * index[None, :] % length
    angles = product.astype(jnp.float32) * (2.0 * math.pi / length)
    freq = jnp.minimum(index, length - index).astype(jnp.float32)
    weight = -((2.0 * math.pi / length * freq) ** 2) / length
    cosines = jnp.cos(angles)
    sines = jnp.sin(angles)
    matrix = jnp.dot(cosines * weight[None, :], cosines.T, precision=HIGHEST)
    matrix = matrix + jnp.dot(sines * weight[None, :], sines.T, precision=HIGHEST)
    return matrix.astype(jnp.bfloat16)


def dot(a, b):
    return jnp.dot(a, b, preferred_element_type=jnp.float32)


def dot_nt(a, b):
    return lax.dot_general(a, b, (((1,), (1,)), ((), ())), preferred_element_type=jnp.float32)


def params(dims, mib=MOST_MIB):
    return pltpu.CompilerParams(
        dimension_semantics=("arbitrary",) * dims, vmem_limit_bytes=mib * 1024 * 1024
    )


def cost(flops, bytes_accessed):
    return pl.CostEstimate(flops=int(flops), bytes_accessed=int(bytes_accessed), transcendentals=0)


def split_rows(ref, tile, orbital, plane):
    return jnp.concatenate(
        [ref[tile, orbital, plane], ref[tile + 1, orbital, plane]], axis=1
    )


def load_plane(ref, plane, orbital):
    tiles = ref.shape[0]
    value = ref[:, orbital, plane].reshape(tiles // 2, 2, ROWS, LANES)
    rows = tiles // 2 * ROWS
    return jnp.concatenate(
        [value[:, 0].reshape(rows, LANES), value[:, 1].reshape(rows, LANES)], axis=1
    )


def store_plane(ref, plane, value, orbital=0):
    tiles = ref.shape[0]
    left = value[:, :LANES].reshape(tiles // 2, 1, ROWS, LANES)
    right = value[:, LANES:].reshape(tiles // 2, 1, ROWS, LANES)
    ref[:, orbital, plane] = jnp.concatenate([left, right], axis=1).reshape(tiles, ROWS, LANES)


def derive_rows(work, matrix, rows):
    total = work.shape[0] // rows
    lanes = work.shape[1]
    for row in range(0, rows, 2):
        here = pl.ds(row, total, stride=rows)
        there = pl.ds(row + 1, total, stride=rows)
        value = jnp.concatenate([work[here, :], work[there, :]], axis=1).astype(jnp.bfloat16)
        result = dot(matrix, value)
        work[here, :] = result[:, :lanes]
        work[there, :] = result[:, lanes:]


def lines_kernel(field_ref, k_ref, out_ref, work):
    blocks, _, planes, rows, lanes = field_ref.shape
    work[...] = field_ref[...].reshape(blocks * planes * rows, lanes).astype(jnp.float32)
    derive_rows(work, k_ref[...], rows)
    out_ref[...] = work[...].astype(jnp.bfloat16).reshape(blocks, 1, planes, rows, lanes)


def derive_lines(field, k_t):
    blocks, count, planes, rows, lanes = field.shape
    block = pl.BlockSpec((blocks, 1, planes, rows, lanes), lambda i: (0, i, 0, 0, 0))
    size = field.size
    return pl.pallas_call(
        lines_kernel,
        grid=(count,),
        in_specs=[block, pl.BlockSpec(k_t.shape, lambda i: (0, 0))],
        out_specs=block,
        out_shape=jax.ShapeDtypeStruct(field.shape, jnp.bfloat16),
        scratch_shapes=[pltpu.VMEM((blocks * planes * rows, lanes), jnp.float32)],
        compiler_params=params(1, STEP_MIB),
        cost_estimate=cost(2 * size * blocks * planes, 4 * size),
        name="derive_lines",
    )(field, k_t)


def tile_kernel(in_ref, out_ref):
    tiles, count, planes, rows, lanes = out_ref.shape
    for tile in range(tiles):
        row, lane = tile // 2 * rows, tile % 2 * lanes
        out_ref[tile] = in_ref[:, :, row : row + rows, lane : lane + lanes]


def tile(orbitals, step=2):
    own, planes, height, depth = orbitals.shape
    tiles = height // ROWS * (depth // LANES)
    return pl.pallas_call(
        tile_kernel,
        grid=(planes // step,),
        in_specs=[pl.BlockSpec((own, step, height, depth), lambda x: (0, x, 0, 0))],
        out_specs=pl.BlockSpec((tiles, own, step, ROWS, LANES), lambda x: (0, 0, x, 0, 0)),
        out_shape=jax.ShapeDtypeStruct((tiles, own, planes, ROWS, LANES), orbitals.dtype),
        compiler_params=params(1),
        cost_estimate=cost(0, 4 * orbitals.size),
        name="tile",
    )(orbitals)


def local_terms(plane, ky_t, k_z):
    return dot(ky_t, plane) + dot(plane, k_z)


def each_plane(ref):
    return [(plane, o) for plane in range(ref.shape[2]) for o in range(ref.shape[1])]


def first_kernel(field_ref, line_ref, pot_ref, ky_ref, kz_ref, out_ref):
    for plane, o in each_plane(field_ref):
        field = load_plane(field_ref, plane, o)
        wide = field.astype(jnp.float32)
        line = load_plane(line_ref, plane, o).astype(jnp.float32)
        ham = -0.5 * (line + local_terms(field, ky_ref[...], kz_ref[...])) + pot_ref[plane] * wide
        value = (ham - CENTER * wide) * (1.0 / HALF_WIDTH)
        store_plane(out_ref, plane, value.astype(jnp.bfloat16), o)


def plane_specs(ky_t, potential, step):
    whole = pl.BlockSpec(ky_t.shape, lambda x: (0, 0))
    pot = pl.BlockSpec((step,) + potential.shape[1:], lambda x: (x, 0, 0))
    return [pot, whole, whole]


def planes_spec(field, step):
    tiles, count, _, rows, lanes = field.shape
    return pl.BlockSpec((tiles, count, step, rows, lanes), lambda x: (0, 0, x, 0, 0))


def first_step(field, line, potential, ky_t, k_z, step=2):
    size = field.size
    return pl.pallas_call(
        first_kernel,
        grid=(field.shape[2] // step,),
        in_specs=[planes_spec(field, step)] * 2 + plane_specs(ky_t, potential, step),
        out_specs=planes_spec(field, step),
        out_shape=jax.ShapeDtypeStruct(field.shape, jnp.bfloat16),
        compiler_params=params(1, STEP_MIB),
        cost_estimate=cost(4 * size * 256, 10 * size),
        name="first_step",
    )(field, line, potential, ky_t, k_z)


def store_pieces(me, refs, orbital, plane, work):
    bands = len(refs)
    span = work.shape[0] // bands
    for shift, ref in enumerate(refs):
        base = pl.multiple_of(lax.rem(me + shift, bands) * span, span)
        store_plane(ref, plane, work[pl.ds(base, span), :], orbital)


def filtered_kernel(me_ref, field_ref, line_ref, start_ref, pot_ref, ky_ref, kz_ref, *rest):
    piece_refs, f_work, g_work = rest[:-2], rest[-2], rest[-1]
    own = field_ref.shape[1]
    for plane, o in each_plane(field_ref):
        field = load_plane(field_ref, plane, o)
        wide = field.astype(jnp.float32)
        line = load_plane(line_ref, plane, o).astype(jnp.float32)
        start = load_plane(start_ref, plane, o).astype(jnp.float32)
        ham = -0.5 * (line + local_terms(field, ky_ref[...], kz_ref[...])) + pot_ref[plane] * wide
        value = 2.0 * (ham - CENTER * wide) * (1.0 / HALF_WIDTH) - start
        value = value.astype(jnp.bfloat16)
        part = -0.5 * local_terms(value, ky_ref[...], kz_ref[...])
        part = part + pot_ref[plane] * value.astype(jnp.float32)
        f_work[...] = value
        g_work[...] = part.astype(jnp.bfloat16)
        store_pieces(me_ref[0], piece_refs, o, plane, f_work)
        store_pieces(me_ref[0], piece_refs, own + o, plane, g_work)


def filtered_step(me, field, line, start, potential, ky_t, k_z, bands, step=2):
    tiles, own, planes, rows, lanes = field.shape
    piece = jax.ShapeDtypeStruct((tiles // bands, 2 * own, planes, rows, lanes), jnp.bfloat16)
    size = field.size
    out = pl.pallas_call(
        filtered_kernel,
        grid=(planes // step,),
        in_specs=[pl.BlockSpec(memory_space=pltpu.SMEM)]
        + [planes_spec(field, step)] * 3
        + plane_specs(ky_t, potential, step),
        out_specs=[planes_spec(piece, step)] * bands,
        out_shape=[piece] * bands,
        scratch_shapes=[pltpu.VMEM(potential.shape[1:], jnp.bfloat16)] * 2,
        compiler_params=params(1),
        cost_estimate=cost(8 * size * 256, 14 * size),
        name="filtered_step",
    )(me, field, line, start, potential, ky_t, k_z)
    return list(out)


def chunk(refs, tile, plane):
    return jnp.concatenate(
        [split_rows(ref, tile, 0, plane) for ref in refs], axis=0
    )


def owner(place, me, own, bands, sign):
    return lax.rem(me + sign * (place // own) + bands, bands) * own + lax.rem(place, own)


def fold(product, me, out_ref, own, inner):
    rows = product.shape[0]
    count = out_ref.shape[0]
    at = lax.broadcasted_iota(jnp.int32, (rows, rows), 0)
    to = lax.broadcasted_iota(jnp.int32, (rows, rows), 1)
    who = lax.broadcasted_iota(jnp.int32, (count, rows), 0)
    row = lax.broadcasted_iota(jnp.int32, (count, rows), 1)
    if inner:
        same, place = at % ROWS == to % ROWS, row // ROWS
    else:
        same, place = at // ROWS == to // ROWS, row % ROWS
    kept = jnp.where(same, product, 0.0)
    pick = jnp.where(owner(place, me, own, count // own, -1) == who, 1.0, 0.0)
    half = jnp.dot(pick, kept, precision=HIGHEST, preferred_element_type=jnp.float32)
    out_ref[...] = lax.dot_general(
        half, pick, (((1,), (1,)), ((), ())), precision=HIGHEST, preferred_element_type=jnp.float32
    )


def gram_kernel(own, count, me_ref, *refs):
    refs, out_ref, work = refs[:-2], refs[-2], refs[-1]
    left, right = refs[:count], refs[-count:]

    @pl.when(pl.program_id(0) == 0)
    def _():
        work[...] = jnp.zeros_like(work)

    total = work[...]
    for plane in range(left[0].shape[2]):
        for tile in range(0, left[0].shape[0], 2):
            b = chunk(right, tile, plane)
            a = b if len(refs) == count else chunk(left, tile, plane)
            total = total + dot_nt(a, b)
    work[...] = total

    @pl.when(pl.program_id(0) == pl.num_programs(0) - 1)
    def _():
        fold(work[...], me_ref[0], out_ref, own, True)


def piece_spec(tiles, view, step):
    array, at = view
    _, _, _, rows, lanes = array.shape
    return pl.BlockSpec((tiles, 1, step, rows, lanes), lambda x: (0, at, x, 0, 0))


def gram(me, own, tiles, left, right=(), step=4):
    views = list(left) + list(right)
    _, _, planes, rows, lanes = views[0][0].shape
    total = len(left)
    size = tiles * planes * rows * lanes * total
    return pl.pallas_call(
        functools.partial(gram_kernel, own, total),
        grid=(planes // step,),
        in_specs=[pl.BlockSpec(memory_space=pltpu.SMEM)]
        + [piece_spec(tiles, view, step) for view in views],
        out_specs=pl.BlockSpec((total, total), lambda x: (0, 0)),
        out_shape=jax.ShapeDtypeStruct((total, total), jnp.float32),
        scratch_shapes=[pltpu.VMEM((total * rows, total * rows), jnp.float32)],
        compiler_params=params(1),
        cost_estimate=cost(2 * size * 256, 2 * size * (len(views) // total)),
        name="gram",
    )(me, *[view[0] for view in views])


def line_gram_kernel(own, me_ref, field_ref, k_ref, out_ref, work, derived):
    blocks, halves, planes, rows, lanes = field_ref.shape
    for half in range(halves):
        work[...] = field_ref[:, half].reshape(blocks * planes * rows, lanes).astype(jnp.float32)
        derive_rows(work, k_ref[...], rows)
        derived[half] = work[...].astype(jnp.bfloat16)
    step = rows * rows
    total = jnp.zeros((step, step), jnp.float32)
    each = step // (planes * rows)
    for at in range(0, blocks, each):
        start = at * planes * rows
        left = [derived[half, start : start + step] for half in range(halves)]
        right = [field_ref[at : at + each, half].reshape(step, lanes) for half in range(halves)]
        total = total + dot_nt(jnp.concatenate(left, axis=1), jnp.concatenate(right, axis=1))
    fold(total, me_ref[0], out_ref, own, False)


def line_gram(me, own, field, k_t):
    blocks, halves, planes, rows, lanes = field.shape
    vmem = pl.BlockSpec(memory_space=pltpu.VMEM)
    size = blocks * planes * rows
    return pl.pallas_call(
        functools.partial(line_gram_kernel, own),
        in_specs=[pl.BlockSpec(memory_space=pltpu.SMEM), vmem, vmem],
        out_specs=vmem,
        out_shape=jax.ShapeDtypeStruct((rows, rows), jnp.float32),
        scratch_shapes=[
            pltpu.VMEM((size, lanes), jnp.float32),
            pltpu.VMEM((halves, size, lanes), jnp.bfloat16),
        ],
        compiler_params=pltpu.CompilerParams(vmem_limit_bytes=STEP_MIB * 1024 * 1024),
        cost_estimate=cost(4 * field.size * 256, 2 * field.size),
        name="line_gram",
    )(me, field, k_t)


def regroup_kernel(*refs):
    work, out_ref, refs = refs[-1], refs[-2], refs[:-2]
    _, _, planes, rows, lanes = refs[0].shape
    each = planes * rows
    total = len(refs)
    for at, ref in enumerate(refs):
        work[at * each : (at + 1) * each, :] = ref[0, 0].reshape(each, lanes).astype(jnp.float32)
    half = rows // 2
    for plane in range(planes):
        for row in range(rows):
            value = work[pl.ds(plane * rows + row, total, stride=each), :]
            out_ref[row % half, row // half, plane] = value.astype(jnp.bfloat16)


def regroup(tiles, views):
    _, _, planes, rows, lanes = views[0][0].shape
    total = len(views)
    half = rows // 2

    def spec(at):
        return pl.BlockSpec((1, 1, planes, rows, lanes), lambda t: (t, at, 0, 0, 0))

    size = tiles * planes * rows * lanes * total
    return pl.pallas_call(
        regroup_kernel,
        grid=(tiles,),
        in_specs=[spec(at) for _, at in views],
        out_specs=pl.BlockSpec((half, 2, planes, total, lanes), lambda t: (t, 0, 0, 0, 0)),
        out_shape=jax.ShapeDtypeStruct((tiles * half, 2, planes, total, lanes), jnp.bfloat16),
        scratch_shapes=[pltpu.VMEM((total * planes * rows, lanes), jnp.float32)],
        compiler_params=params(1),
        cost_estimate=cost(size, 4 * size),
        name="regroup",
    )(*[view[0] for view in views])


def rotate_kernel(total, mix_ref, *refs):
    ins, outs = refs[:total], refs[total:]
    tiles, count, planes, rows, lanes = outs[0].shape
    for plane in range(planes):
        for tile in range(0, tiles, 2):
            value = dot(mix_ref[...], chunk(ins, tile, plane)).astype(jnp.bfloat16)
            for at, ref in enumerate(outs):
                for o in range(count):
                    start = (at * count + o) * rows
                    ref[tile, o, plane] = value[start : start + rows, :lanes]
                    ref[tile + 1, o, plane] = value[start : start + rows, lanes:]


def rotate(mix, own, tiles, views, step=4):
    _, _, planes, rows, lanes = views[0][0].shape
    total = len(views)
    out = pl.BlockSpec((tiles, own, step, rows, lanes), lambda x: (0, 0, x, 0, 0))
    shape = jax.ShapeDtypeStruct((tiles, own, planes, rows, lanes), jnp.bfloat16)
    size = tiles * planes * rows * lanes * total
    return pl.pallas_call(
        functools.partial(rotate_kernel, total),
        grid=(planes // step,),
        in_specs=[pl.BlockSpec(mix.shape, lambda x: (0, 0))]
        + [piece_spec(tiles, view, step) for view in views],
        out_specs=[out] * (total // own),
        out_shape=[shape] * (total // own),
        compiler_params=params(1),
        cost_estimate=cost(2 * size * 256, 4 * size),
        name="rotate",
    )(mix, *[view[0] for view in views])


def untile_kernel(me_ref, *refs):
    ins, out_ref = refs[:-1], refs[-1]
    bands = len(ins)
    tiles, _, _, rows, lanes = ins[0].shape
    for shift, ref in enumerate(ins):
        band = lax.rem(me_ref[0] + (bands - shift), bands)
        for tile in range(tiles):
            row = pl.multiple_of(band * (tiles // 2 * rows) + tile // 2 * rows, rows)
            lane = tile % 2 * lanes
            out_ref[:, :, pl.ds(row, rows), lane : lane + lanes] = ref[tile]


def untile(me, pieces, shape, step=2):
    own, planes, height, depth = shape
    return pl.pallas_call(
        untile_kernel,
        grid=(planes // step,),
        in_specs=[pl.BlockSpec(memory_space=pltpu.SMEM)] + [planes_spec(pieces[0], step)] * len(pieces),
        out_specs=pl.BlockSpec((own, step, height, depth), lambda x: (0, x, 0, 0)),
        out_shape=jax.ShapeDtypeStruct(shape, jnp.bfloat16),
        compiler_params=params(1),
        cost_estimate=cost(0, 4 * math.prod(shape)),
        name="untile",
    )(me, *pieces)


def order_of(size):
    return sorted(range(1, size), key=lambda s: -min(s, size - s))


def exchange(pieces, axis):
    size = lax.axis_size(axis)
    out = [pieces[0]] + [None] * (size - 1)
    for shift in order_of(size):
        pairs = [(i, (i + shift) % size) for i in range(size)]
        out[shift] = lax.ppermute(pieces[shift], axis, pairs)
    return out


def after(*values):
    return lax.optimization_barrier(values)


def over_grid(field):
    return lax.all_to_all(field, "grid", 0, 0, tiled=True)


def small_sum(matrix):
    axes = ("band", "grid")
    flat = matrix.reshape(-1, LANES)
    spread = jnp.broadcast_to(flat[None], (lax.axis_size(axes),) + flat.shape)
    return jnp.sum(lax.all_to_all(spread, axes, 0, 0, tiled=True), axis=0).reshape(matrix.shape)


def spread_sum(matrix, axis):
    flat = matrix.reshape(-1, LANES)
    spread = jnp.broadcast_to(flat[None], (lax.axis_size(axis),) + flat.shape)
    return jnp.sum(lax.all_to_all(spread, axis, 0, 0, tiled=True), axis=0).reshape(matrix.shape)


def mixing_kernel(own, me_ref, corr_ref, root_ref, scale_ref, mix_ref):
    correlation = corr_ref[...]
    count = correlation.shape[0]
    bands = count // own
    scale = jnp.max(jnp.sum(jnp.abs(correlation), axis=1, keepdims=True), axis=0, keepdims=True)
    at = lax.broadcasted_iota(jnp.int32, (count, count), 0)
    to = lax.broadcasted_iota(jnp.int32, (count, count), 1)
    identity = jnp.where(at == to, 1.0, 0.0)

    def full(a, b):
        return jnp.dot(a, b, precision=HIGHEST, preferred_element_type=jnp.float32)

    current = correlation / scale
    root = identity
    for _ in range(NS_ITERS):
        turn = 1.5 * identity - 0.5 * full(root, current)
        current = full(current, turn)
        root = full(turn, root)
    root_ref[...] = root
    scale_ref[...] = jnp.broadcast_to(scale, scale_ref.shape)
    coeff = root.astype(jnp.bfloat16)
    rows = mix_ref.shape[0]
    me = me_ref[0]
    who = lax.broadcasted_iota(jnp.int32, (count, rows), 0)
    place = lax.broadcasted_iota(jnp.int32, (count, rows), 1) // ROWS
    source = jnp.where(owner(place, me, own, bands, -1) == who, 1.0, 0.0).astype(jnp.bfloat16)
    target = jnp.where(owner(place, me, own, bands, 1) == who, 1.0, 0.0).astype(jnp.bfloat16)
    over_target = lax.dot_general(
        coeff, target, (((1,), (0,)), ((), ())), preferred_element_type=jnp.float32
    ).astype(jnp.bfloat16)
    mix = lax.dot_general(
        over_target, source, (((0,), (0,)), ((), ())), preferred_element_type=jnp.float32
    )
    at = lax.broadcasted_iota(jnp.int32, (rows, rows), 0)
    to = lax.broadcasted_iota(jnp.int32, (rows, rows), 1)
    mix_ref[...] = jnp.where(at % ROWS == to % ROWS, mix, 0.0).astype(jnp.bfloat16)


def mixing(me, own, correlation):
    count = correlation.shape[0]
    rows = count * ROWS
    vmem = pl.BlockSpec(memory_space=pltpu.VMEM)
    return pl.pallas_call(
        functools.partial(mixing_kernel, own),
        in_specs=[pl.BlockSpec(memory_space=pltpu.SMEM), vmem],
        out_specs=[vmem] * 3,
        out_shape=[
            jax.ShapeDtypeStruct((count, count), jnp.float32),
            jax.ShapeDtypeStruct((1, LANES), jnp.float32),
            jax.ShapeDtypeStruct((rows, rows), jnp.bfloat16),
        ],
        cost_estimate=cost(1e9, 1e6),
        name="mixing",
    )(me, correlation)


def project(inverse_root, hamil, scale):
    left = jnp.dot(inverse_root.T, hamil, precision=HIGHEST)
    return jnp.dot(left, inverse_root, precision=HIGHEST) / scale


def per_device(orbitals, potential):
    own, planes, height, depth = orbitals.shape
    bands = lax.axis_size("band")
    me = jnp.full((1,), lax.axis_index("band"), jnp.int32)
    kx_t = second_derivative(planes * lax.axis_size("grid")).T
    ky_t = second_derivative(height).T
    k_z = second_derivative(depth)

    start = tile(orbitals)
    line = over_grid(derive_lines(over_grid(start), kx_t))
    first = first_step(start, line, potential, ky_t, k_z)
    line = over_grid(derive_lines(over_grid(first), kx_t))
    pieces = filtered_step(me, first, line, start, potential, ky_t, k_z, bands)

    tiles = start.shape[0] // bands
    arrived = exchange(pieces, "band")
    f_views = [(arrived[s], o) for s in range(bands) for o in range(own)]
    g_views = [(arrived[s], own + o) for s in range(bands) for o in range(own)]
    correlation = spread_sum(spread_sum(gram(me, own, tiles, f_views), "grid"), "band")
    inverse_root, scale, mix = mixing(me, own, correlation)
    back = exchange(rotate(mix, own, tiles, f_views), "band")
    rotated = untile(me, back, orbitals.shape)

    lines, _ = after(regroup(tiles, f_views), correlation)
    order = order_of(bands)
    lines = after(over_grid(lines), back[order[0]], back[order[1]])[0]
    hamil = gram(me, own, tiles, g_views, f_views) - 0.5 * line_gram(me, own, lines, kx_t)
    hamil = spread_sum(spread_sum(hamil, "grid"), "band")
    projected = project(inverse_root, hamil, scale[0, 0])
    return (rotated, projected)


def solution(mesh):
    in_specs = (P("band", "grid", None, None), P("grid", None, None))
    out_specs = (P("band", "grid", None, None), P())
    return jax.shard_map(
        per_device, mesh=mesh, in_specs=in_specs, out_specs=out_specs, check_vma=False
    )
```

```python
import functools
import math

import jax
import jax.numpy as jnp
from jax import lax
from jax.experimental import pallas as pl
from jax.experimental.pallas import tpu as pltpu
from jax.sharding import PartitionSpec as P

NS_ITERS = 6

CENTER = 9.5
HALF_WIDTH = 6.5

ROWS = 16
LANES = 128
MOST_MIB = 63
STEP_MIB = 24
HIGHEST = lax.Precision.HIGHEST


def second_derivative(length):
    index = jnp.arange(length, dtype=jnp.int32)
    product = index[:, None] * index[None, :] % length
    angles = product.astype(jnp.float32) * (2.0 * math.pi / length)
    freq = jnp.minimum(index, length - index).astype(jnp.float32)
    weight = -((2.0 * math.pi / length * freq) ** 2) / length
    cosines = jnp.cos(angles)
    sines = jnp.sin(angles)
    matrix = jnp.dot(cosines * weight[None, :], cosines.T, precision=HIGHEST)
    matrix = matrix + jnp.dot(sines * weight[None, :], sines.T, precision=HIGHEST)
    return matrix.astype(jnp.bfloat16)


def dot(a, b):
    return jnp.dot(a, b, preferred_element_type=jnp.float32)


def dot_nt(a, b):
    return lax.dot_general(a, b, (((1,), (1,)), ((), ())), preferred_element_type=jnp.float32)


def params(dims, mib=MOST_MIB):
    return pltpu.CompilerParams(
        dimension_semantics=("arbitrary",) * dims, vmem_limit_bytes=mib * 1024 * 1024
    )


def cost(flops, bytes_accessed):
    return pl.CostEstimate(flops=int(flops), bytes_accessed=int(bytes_accessed), transcendentals=0)


def split_rows(ref, tile, orbital, plane):
    return jnp.concatenate(
        [ref[tile, orbital, plane], ref[tile + 1, orbital, plane]], axis=1
    )


def load_plane(ref, plane, orbital):
    tiles = ref.shape[0]
    value = ref[:, orbital, plane].reshape(tiles // 2, 2, ROWS, LANES)
    rows = tiles // 2 * ROWS
    return jnp.concatenate(
        [value[:, 0].reshape(rows, LANES), value[:, 1].reshape(rows, LANES)], axis=1
    )


def store_plane(ref, plane, value, orbital=0):
    tiles = ref.shape[0]
    left = value[:, :LANES].reshape(tiles // 2, 1, ROWS, LANES)
    right = value[:, LANES:].reshape(tiles // 2, 1, ROWS, LANES)
    ref[:, orbital, plane] = jnp.concatenate([left, right], axis=1).reshape(tiles, ROWS, LANES)


def derive_rows(work, matrix, rows):
    total = work.shape[0] // rows
    lanes = work.shape[1]
    for row in range(0, rows, 2):
        here = pl.ds(row, total, stride=rows)
        there = pl.ds(row + 1, total, stride=rows)
        value = jnp.concatenate([work[here, :], work[there, :]], axis=1).astype(jnp.bfloat16)
        result = dot(matrix, value)
        work[here, :] = result[:, :lanes]
        work[there, :] = result[:, lanes:]


def lines_kernel(field_ref, k_ref, out_ref, work):
    blocks, _, planes, rows, lanes = field_ref.shape
    work[...] = field_ref[...].reshape(blocks * planes * rows, lanes).astype(jnp.float32)
    derive_rows(work, k_ref[...], rows)
    out_ref[...] = work[...].astype(jnp.bfloat16).reshape(blocks, 1, planes, rows, lanes)


def derive_lines(field, k_t):
    blocks, count, planes, rows, lanes = field.shape
    block = pl.BlockSpec((blocks, 1, planes, rows, lanes), lambda i: (0, i, 0, 0, 0))
    size = field.size
    return pl.pallas_call(
        lines_kernel,
        grid=(count,),
        in_specs=[block, pl.BlockSpec(k_t.shape, lambda i: (0, 0))],
        out_specs=block,
        out_shape=jax.ShapeDtypeStruct(field.shape, jnp.bfloat16),
        scratch_shapes=[pltpu.VMEM((blocks * planes * rows, lanes), jnp.float32)],
        compiler_params=params(1, STEP_MIB),
        cost_estimate=cost(2 * size * blocks * planes, 4 * size),
        name="derive_lines",
    )(field, k_t)


def tile_kernel(in_ref, out_ref):
    tiles, count, planes, rows, lanes = out_ref.shape
    for tile in range(tiles):
        row, lane = tile // 2 * rows, tile % 2 * lanes
        out_ref[tile] = in_ref[:, :, row : row + rows, lane : lane + lanes]


def tile(orbitals, step=2):
    own, planes, height, depth = orbitals.shape
    tiles = height // ROWS * (depth // LANES)
    return pl.pallas_call(
        tile_kernel,
        grid=(planes // step,),
        in_specs=[pl.BlockSpec((own, step, height, depth), lambda x: (0, x, 0, 0))],
        out_specs=pl.BlockSpec((tiles, own, step, ROWS, LANES), lambda x: (0, 0, x, 0, 0)),
        out_shape=jax.ShapeDtypeStruct((tiles, own, planes, ROWS, LANES), orbitals.dtype),
        compiler_params=params(1),
        cost_estimate=cost(0, 4 * orbitals.size),
        name="tile",
    )(orbitals)


def local_terms(plane, ky_t, k_z):
    return dot(ky_t, plane) + dot(plane, k_z)


def each_plane(ref):
    return [(plane, o) for plane in range(ref.shape[2]) for o in range(ref.shape[1])]


def first_kernel(field_ref, line_ref, pot_ref, ky_ref, kz_ref, out_ref):
    for plane, o in each_plane(field_ref):
        field = load_plane(field_ref, plane, o)
        wide = field.astype(jnp.float32)
        line = load_plane(line_ref, plane, o).astype(jnp.float32)
        ham = -0.5 * (line + local_terms(field, ky_ref[...], kz_ref[...])) + pot_ref[plane] * wide
        value = (ham - CENTER * wide) * (1.0 / HALF_WIDTH)
        store_plane(out_ref, plane, value.astype(jnp.bfloat16), o)


def plane_specs(ky_t, potential, step):
    whole = pl.BlockSpec(ky_t.shape, lambda x: (0, 0))
    pot = pl.BlockSpec((step,) + potential.shape[1:], lambda x: (x, 0, 0))
    return [pot, whole, whole]


def planes_spec(field, step):
    tiles, count, _, rows, lanes = field.shape
    return pl.BlockSpec((tiles, count, step, rows, lanes), lambda x: (0, 0, x, 0, 0))


def first_step(field, line, potential, ky_t, k_z, step=2):
    size = field.size
    return pl.pallas_call(
        first_kernel,
        grid=(field.shape[2] // step,),
        in_specs=[planes_spec(field, step)] * 2 + plane_specs(ky_t, potential, step),
        out_specs=planes_spec(field, step),
        out_shape=jax.ShapeDtypeStruct(field.shape, jnp.bfloat16),
        compiler_params=params(1, STEP_MIB),
        cost_estimate=cost(4 * size * 256, 10 * size),
        name="first_step",
    )(field, line, potential, ky_t, k_z)


def store_pieces(me, refs, orbital, plane, work):
    bands = len(refs)
    span = work.shape[0] // bands
    for shift, ref in enumerate(refs):
        base = pl.multiple_of(lax.rem(me + shift, bands) * span, span)
        store_plane(ref, plane, work[pl.ds(base, span), :], orbital)


def filtered_kernel(me_ref, field_ref, line_ref, start_ref, pot_ref, ky_ref, kz_ref, *rest):
    piece_refs, out_ref, work = rest[:-2], rest[-2], rest[-1]
    for plane, o in each_plane(field_ref):
        field = load_plane(field_ref, plane, o)
        wide = field.astype(jnp.float32)
        line = load_plane(line_ref, plane, o).astype(jnp.float32)
        start = load_plane(start_ref, plane, o).astype(jnp.float32)
        ham = -0.5 * (line + local_terms(field, ky_ref[...], kz_ref[...])) + pot_ref[plane] * wide
        value = 2.0 * (ham - CENTER * wide) * (1.0 / HALF_WIDTH) - start
        value = value.astype(jnp.bfloat16)
        store_plane(out_ref, plane, value, o)
        work[...] = value
        store_pieces(me_ref[0], piece_refs, o, plane, work)


def pieces_of(field, bands):
    tiles, count, planes, rows, lanes = field.shape
    return jax.ShapeDtypeStruct((tiles // bands, count, planes, rows, lanes), jnp.bfloat16)


def filtered_step(me, field, line, start, potential, ky_t, k_z, bands, step=2):
    piece = pieces_of(field, bands)
    size = field.size
    out = pl.pallas_call(
        filtered_kernel,
        grid=(field.shape[2] // step,),
        in_specs=[pl.BlockSpec(memory_space=pltpu.SMEM)]
        + [planes_spec(field, step)] * 3
        + plane_specs(ky_t, potential, step),
        out_specs=[planes_spec(piece, step)] * bands + [planes_spec(field, step)],
        out_shape=[piece] * bands + [jax.ShapeDtypeStruct(field.shape, jnp.bfloat16)],
        scratch_shapes=[pltpu.VMEM(potential.shape[1:], jnp.bfloat16)],
        compiler_params=params(1),
        cost_estimate=cost(4 * size * 256, 14 * size),
        name="filtered_step",
    )(me, field, line, start, potential, ky_t, k_z)
    return (list(out[:bands]), out[bands])


def local_kernel(me_ref, field_ref, pot_ref, ky_ref, kz_ref, *rest):
    piece_refs, work = rest[:-1], rest[-1]
    for plane, o in each_plane(field_ref):
        field = load_plane(field_ref, plane, o)
        terms = local_terms(field, ky_ref[...], kz_ref[...])
        part = -0.5 * terms + pot_ref[plane] * field.astype(jnp.float32)
        work[...] = part.astype(jnp.bfloat16)
        store_pieces(me_ref[0], piece_refs, o, plane, work)


def local_step(me, field, potential, ky_t, k_z, bands, step=2):
    piece = pieces_of(field, bands)
    size = field.size
    out = pl.pallas_call(
        local_kernel,
        grid=(field.shape[2] // step,),
        in_specs=[pl.BlockSpec(memory_space=pltpu.SMEM), planes_spec(field, step)]
        + plane_specs(ky_t, potential, step),
        out_specs=[planes_spec(piece, step)] * bands,
        out_shape=[piece] * bands,
        scratch_shapes=[pltpu.VMEM(potential.shape[1:], jnp.bfloat16)],
        compiler_params=params(1),
        cost_estimate=cost(4 * size * 256, 8 * size),
        name="local_step",
    )(me, field, potential, ky_t, k_z)
    return list(out)


def chunk(refs, tile, plane):
    return jnp.concatenate(
        [split_rows(ref, tile, 0, plane) for ref in refs], axis=0
    )


def owner(place, me, own, bands, sign):
    return lax.rem(me + sign * (place // own) + bands, bands) * own + lax.rem(place, own)


def fold(product, me, out_ref, own, inner):
    rows = product.shape[0]
    count = out_ref.shape[0]
    at = lax.broadcasted_iota(jnp.int32, (rows, rows), 0)
    to = lax.broadcasted_iota(jnp.int32, (rows, rows), 1)
    who = lax.broadcasted_iota(jnp.int32, (count, rows), 0)
    row = lax.broadcasted_iota(jnp.int32, (count, rows), 1)
    if inner:
        same, place = at % ROWS == to % ROWS, row // ROWS
    else:
        same, place = at // ROWS == to // ROWS, row % ROWS
    kept = jnp.where(same, product, 0.0)
    pick = jnp.where(owner(place, me, own, count // own, -1) == who, 1.0, 0.0)
    half = jnp.dot(pick, kept, precision=HIGHEST, preferred_element_type=jnp.float32)
    out_ref[...] = lax.dot_general(
        half, pick, (((1,), (1,)), ((), ())), precision=HIGHEST, preferred_element_type=jnp.float32
    )


def gram_kernel(own, count, me_ref, *refs):
    refs, out_ref, work = refs[:-2], refs[-2], refs[-1]
    left, right = refs[:count], refs[-count:]

    @pl.when(pl.program_id(0) == 0)
    def _():
        work[...] = jnp.zeros_like(work)

    total = work[...]
    for plane in range(left[0].shape[2]):
        for tile in range(0, left[0].shape[0], 2):
            b = chunk(right, tile, plane)
            a = b if len(refs) == count else chunk(left, tile, plane)
            total = total + dot_nt(a, b)
    work[...] = total

    @pl.when(pl.program_id(0) == pl.num_programs(0) - 1)
    def _():
        fold(work[...], me_ref[0], out_ref, own, True)


def piece_spec(tiles, view, step):
    array, at = view
    _, _, _, rows, lanes = array.shape
    return pl.BlockSpec((tiles, 1, step, rows, lanes), lambda x: (0, at, x, 0, 0))


def gram(me, own, tiles, left, right=(), step=4):
    views = list(left) + list(right)
    _, _, planes, rows, lanes = views[0][0].shape
    total = len(left)
    size = tiles * planes * rows * lanes * total
    return pl.pallas_call(
        functools.partial(gram_kernel, own, total),
        grid=(planes // step,),
        in_specs=[pl.BlockSpec(memory_space=pltpu.SMEM)]
        + [piece_spec(tiles, view, step) for view in views],
        out_specs=pl.BlockSpec((total, total), lambda x: (0, 0)),
        out_shape=jax.ShapeDtypeStruct((total, total), jnp.float32),
        scratch_shapes=[pltpu.VMEM((total * rows, total * rows), jnp.float32)],
        compiler_params=params(1),
        cost_estimate=cost(2 * size * 256, 2 * size * (len(views) // total)),
        name="gram",
    )(me, *[view[0] for view in views])


def line_gram_kernel(own, me_ref, field_ref, k_ref, out_ref, work, derived):
    blocks, halves, planes, rows, lanes = field_ref.shape
    for half in range(halves):
        work[...] = field_ref[:, half].reshape(blocks * planes * rows, lanes).astype(jnp.float32)
        derive_rows(work, k_ref[...], rows)
        derived[half] = work[...].astype(jnp.bfloat16)
    step = rows * rows
    total = jnp.zeros((step, step), jnp.float32)
    each = step // (planes * rows)
    for at in range(0, blocks, each):
        start = at * planes * rows
        left = [derived[half, start : start + step] for half in range(halves)]
        right = [field_ref[at : at + each, half].reshape(step, lanes) for half in range(halves)]
        total = total + dot_nt(jnp.concatenate(left, axis=1), jnp.concatenate(right, axis=1))
    fold(total, me_ref[0], out_ref, own, False)


def line_gram(me, own, field, k_t):
    blocks, halves, planes, rows, lanes = field.shape
    vmem = pl.BlockSpec(memory_space=pltpu.VMEM)
    size = blocks * planes * rows
    return pl.pallas_call(
        functools.partial(line_gram_kernel, own),
        in_specs=[pl.BlockSpec(memory_space=pltpu.SMEM), vmem, vmem],
        out_specs=vmem,
        out_shape=jax.ShapeDtypeStruct((rows, rows), jnp.float32),
        scratch_shapes=[
            pltpu.VMEM((size, lanes), jnp.float32),
            pltpu.VMEM((halves, size, lanes), jnp.bfloat16),
        ],
        compiler_params=pltpu.CompilerParams(vmem_limit_bytes=STEP_MIB * 1024 * 1024),
        cost_estimate=cost(4 * field.size * 256, 2 * field.size),
        name="line_gram",
    )(me, field, k_t)


def regroup_kernel(*refs):
    work, out_ref, refs = refs[-1], refs[-2], refs[:-2]
    _, _, planes, rows, lanes = refs[0].shape
    each = planes * rows
    total = len(refs)
    for at, ref in enumerate(refs):
        work[at * each : (at + 1) * each, :] = ref[0, 0].reshape(each, lanes).astype(jnp.float32)
    half = rows // 2
    for plane in range(planes):
        for row in range(rows):
            value = work[pl.ds(plane * rows + row, total, stride=each), :]
            out_ref[row % half, row // half, plane] = value.astype(jnp.bfloat16)


def regroup(tiles, views):
    _, _, planes, rows, lanes = views[0][0].shape
    total = len(views)
    half = rows // 2

    def spec(at):
        return pl.BlockSpec((1, 1, planes, rows, lanes), lambda t: (t, at, 0, 0, 0))

    size = tiles * planes * rows * lanes * total
    return pl.pallas_call(
        regroup_kernel,
        grid=(tiles,),
        in_specs=[spec(at) for _, at in views],
        out_specs=pl.BlockSpec((half, 2, planes, total, lanes), lambda t: (t, 0, 0, 0, 0)),
        out_shape=jax.ShapeDtypeStruct((tiles * half, 2, planes, total, lanes), jnp.bfloat16),
        scratch_shapes=[pltpu.VMEM((total * planes * rows, lanes), jnp.float32)],
        compiler_params=params(1),
        cost_estimate=cost(size, 4 * size),
        name="regroup",
    )(*[view[0] for view in views])


def rotate_kernel(total, mix_ref, *refs):
    ins, outs = refs[:total], refs[total:]
    tiles, count, planes, rows, lanes = outs[0].shape
    for plane in range(planes):
        for tile in range(0, tiles, 2):
            value = dot(mix_ref[...], chunk(ins, tile, plane)).astype(jnp.bfloat16)
            for at, ref in enumerate(outs):
                for o in range(count):
                    start = (at * count + o) * rows
                    ref[tile, o, plane] = value[start : start + rows, :lanes]
                    ref[tile + 1, o, plane] = value[start : start + rows, lanes:]


def rotate(mix, own, tiles, views, step=4):
    _, _, planes, rows, lanes = views[0][0].shape
    total = len(views)
    out = pl.BlockSpec((tiles, own, step, rows, lanes), lambda x: (0, 0, x, 0, 0))
    shape = jax.ShapeDtypeStruct((tiles, own, planes, rows, lanes), jnp.bfloat16)
    size = tiles * planes * rows * lanes * total
    return pl.pallas_call(
        functools.partial(rotate_kernel, total),
        grid=(planes // step,),
        in_specs=[pl.BlockSpec(mix.shape, lambda x: (0, 0))]
        + [piece_spec(tiles, view, step) for view in views],
        out_specs=[out] * (total // own),
        out_shape=[shape] * (total // own),
        compiler_params=params(1),
        cost_estimate=cost(2 * size * 256, 4 * size),
        name="rotate",
    )(mix, *[view[0] for view in views])


def untile_kernel(me_ref, *refs):
    ins, out_ref = refs[:-1], refs[-1]
    bands = len(ins)
    tiles, _, _, rows, lanes = ins[0].shape
    for shift, ref in enumerate(ins):
        band = lax.rem(me_ref[0] + (bands - shift), bands)
        for tile in range(tiles):
            row = pl.multiple_of(band * (tiles // 2 * rows) + tile // 2 * rows, rows)
            lane = tile % 2 * lanes
            out_ref[:, :, pl.ds(row, rows), lane : lane + lanes] = ref[tile]


def untile(me, pieces, shape, step=2):
    own, planes, height, depth = shape
    return pl.pallas_call(
        untile_kernel,
        grid=(planes // step,),
        in_specs=[pl.BlockSpec(memory_space=pltpu.SMEM)] + [planes_spec(pieces[0], step)] * len(pieces),
        out_specs=pl.BlockSpec((own, step, height, depth), lambda x: (0, x, 0, 0)),
        out_shape=jax.ShapeDtypeStruct(shape, jnp.bfloat16),
        compiler_params=params(1),
        cost_estimate=cost(0, 4 * math.prod(shape)),
        name="untile",
    )(me, *pieces)


def order_of(size):
    return sorted(range(1, size), key=lambda s: -min(s, size - s))


def exchange(pieces, axis):
    size = lax.axis_size(axis)
    out = [pieces[0]] + [None] * (size - 1)

    def send(shift, piece):
        pairs = [(i, (i + shift) % size) for i in range(size)]
        out[shift % size] = lax.ppermute(piece, axis, pairs)

    for shift in order_of(size):
        if min(shift, size - shift) != 2:
            send(shift, pieces[shift])
    for shift, first in ((2, 1), (size - 2, size - 1)):
        send(shift, after(pieces[shift], out[first])[0])
    return out


def after(*values):
    return lax.optimization_barrier(values)


def over_grid(field):
    return lax.all_to_all(field, "grid", 0, 0, tiled=True)


def small_sum(matrix):
    axes = ("band", "grid")
    flat = matrix.reshape(-1, LANES)
    spread = jnp.broadcast_to(flat[None], (lax.axis_size(axes),) + flat.shape)
    return jnp.sum(lax.all_to_all(spread, axes, 0, 0, tiled=True), axis=0).reshape(matrix.shape)


def spread_sum(matrix, axis):
    flat = matrix.reshape(-1, LANES)
    spread = jnp.broadcast_to(flat[None], (lax.axis_size(axis),) + flat.shape)
    return jnp.sum(lax.all_to_all(spread, axis, 0, 0, tiled=True), axis=0).reshape(matrix.shape)


def mixing_kernel(own, me_ref, corr_ref, root_ref, scale_ref, mix_ref):
    correlation = corr_ref[...]
    count = correlation.shape[0]
    bands = count // own
    scale = jnp.max(jnp.sum(jnp.abs(correlation), axis=1, keepdims=True), axis=0, keepdims=True)
    at = lax.broadcasted_iota(jnp.int32, (count, count), 0)
    to = lax.broadcasted_iota(jnp.int32, (count, count), 1)
    identity = jnp.where(at == to, 1.0, 0.0)

    def full(a, b):
        return jnp.dot(a, b, precision=HIGHEST, preferred_element_type=jnp.float32)

    current = correlation / scale
    root = identity
    for _ in range(NS_ITERS):
        turn = 1.5 * identity - 0.5 * full(root, current)
        current = full(current, turn)
        root = full(turn, root)
    root_ref[...] = root
    scale_ref[...] = jnp.broadcast_to(scale, scale_ref.shape)
    coeff = root.astype(jnp.bfloat16)
    rows = mix_ref.shape[0]
    me = me_ref[0]
    who = lax.broadcasted_iota(jnp.int32, (count, rows), 0)
    place = lax.broadcasted_iota(jnp.int32, (count, rows), 1) // ROWS
    source = jnp.where(owner(place, me, own, bands, -1) == who, 1.0, 0.0).astype(jnp.bfloat16)
    target = jnp.where(owner(place, me, own, bands, 1) == who, 1.0, 0.0).astype(jnp.bfloat16)
    over_target = lax.dot_general(
        coeff, target, (((1,), (0,)), ((), ())), preferred_element_type=jnp.float32
    ).astype(jnp.bfloat16)
    mix = lax.dot_general(
        over_target, source, (((0,), (0,)), ((), ())), preferred_element_type=jnp.float32
    )
    at = lax.broadcasted_iota(jnp.int32, (rows, rows), 0)
    to = lax.broadcasted_iota(jnp.int32, (rows, rows), 1)
    mix_ref[...] = jnp.where(at % ROWS == to % ROWS, mix, 0.0).astype(jnp.bfloat16)


def mixing(me, own, correlation):
    count = correlation.shape[0]
    rows = count * ROWS
    vmem = pl.BlockSpec(memory_space=pltpu.VMEM)
    return pl.pallas_call(
        functools.partial(mixing_kernel, own),
        in_specs=[pl.BlockSpec(memory_space=pltpu.SMEM), vmem],
        out_specs=[vmem] * 3,
        out_shape=[
            jax.ShapeDtypeStruct((count, count), jnp.float32),
            jax.ShapeDtypeStruct((1, LANES), jnp.float32),
            jax.ShapeDtypeStruct((rows, rows), jnp.bfloat16),
        ],
        cost_estimate=cost(1e9, 1e6),
        name="mixing",
    )(me, correlation)


def project(inverse_root, hamil, scale):
    left = jnp.dot(inverse_root.T, hamil, precision=HIGHEST)
    return jnp.dot(left, inverse_root, precision=HIGHEST) / scale


def per_device(orbitals, potential):
    own, planes, height, depth = orbitals.shape
    bands = lax.axis_size("band")
    me = jnp.full((1,), lax.axis_index("band"), jnp.int32)
    kx_t = second_derivative(planes * lax.axis_size("grid")).T
    ky_t = second_derivative(height).T
    k_z = second_derivative(depth)

    start = tile(orbitals)
    line = over_grid(derive_lines(over_grid(start), kx_t))
    first = first_step(start, line, potential, ky_t, k_z)
    line = over_grid(derive_lines(over_grid(first), kx_t))
    pieces, whole = filtered_step(me, first, line, start, potential, ky_t, k_z, bands)

    tiles = start.shape[0] // bands
    arrived = exchange(pieces, "band")
    f_views = [(arrived[s], o) for s in range(bands) for o in range(own)]
    local = local_step(me, whole, potential, ky_t, k_z, bands)
    arrived[4] = after(arrived[4], *local)[0]
    f_views = [(arrived[s], o) for s in range(bands) for o in range(own)]
    local = exchange(local, "band")
    g_views = [(local[s], o) for s in range(bands) for o in range(own)]
    correlation = gram(me, own, tiles, f_views)
    lines = over_grid(regroup(tiles, f_views))
    hamil = gram(me, own, tiles, g_views, f_views) - 0.5 * line_gram(me, own, lines, kx_t)
    both = jnp.stack([correlation, hamil])
    both = spread_sum(spread_sum(both, "grid"), "band")
    inverse_root, scale, mix = mixing(me, own, both[0])
    back = exchange(rotate(mix, own, tiles, f_views), "band")
    projected = project(inverse_root, both[1], scale[0, 0])
    return (untile(me, back, orbitals.shape), projected)


def solution(mesh):
    in_specs = (P("band", "grid", None, None), P("grid", None, None))
    out_specs = (P("band", "grid", None, None), P())
    return jax.shard_map(
        per_device, mesh=mesh, in_specs=in_specs, out_specs=out_specs, check_vma=False
    )
```

```python
import functools
import math

import jax
import jax.numpy as jnp
from jax import lax
from jax.experimental import pallas as pl
from jax.experimental.pallas import tpu as pltpu
from jax.sharding import PartitionSpec as P

NS_ITERS = 6

CENTER = 9.5
HALF_WIDTH = 6.5

ROWS = 16
LANES = 128
MOST_MIB = 63
STEP_MIB = 24
HIGHEST = lax.Precision.HIGHEST


def second_derivative(length):
    index = jnp.arange(length, dtype=jnp.int32)
    product = index[:, None] * index[None, :] % length
    angles = product.astype(jnp.float32) * (2.0 * math.pi / length)
    freq = jnp.minimum(index, length - index).astype(jnp.float32)
    weight = -((2.0 * math.pi / length * freq) ** 2) / length
    cosines = jnp.cos(angles)
    sines = jnp.sin(angles)
    matrix = jnp.dot(cosines * weight[None, :], cosines.T, precision=HIGHEST)
    matrix = matrix + jnp.dot(sines * weight[None, :], sines.T, precision=HIGHEST)
    return matrix.astype(jnp.bfloat16)


def dot(a, b):
    return jnp.dot(a, b, preferred_element_type=jnp.float32)


def dot_nt(a, b):
    return lax.dot_general(a, b, (((1,), (1,)), ((), ())), preferred_element_type=jnp.float32)


def params(dims, mib=MOST_MIB):
    return pltpu.CompilerParams(
        dimension_semantics=("arbitrary",) * dims, vmem_limit_bytes=mib * 1024 * 1024
    )


def cost(flops, bytes_accessed):
    return pl.CostEstimate(flops=int(flops), bytes_accessed=int(bytes_accessed), transcendentals=0)


def split_rows(ref, tile, orbital, plane):
    return jnp.concatenate(
        [ref[tile, orbital, plane], ref[tile + 1, orbital, plane]], axis=1
    )


def load_plane(ref, plane, orbital):
    tiles = ref.shape[0]
    value = ref[:, orbital, plane].reshape(tiles // 2, 2, ROWS, LANES)
    rows = tiles // 2 * ROWS
    return jnp.concatenate(
        [value[:, 0].reshape(rows, LANES), value[:, 1].reshape(rows, LANES)], axis=1
    )


def store_plane(ref, plane, value, orbital=0):
    tiles = ref.shape[0]
    left = value[:, :LANES].reshape(tiles // 2, 1, ROWS, LANES)
    right = value[:, LANES:].reshape(tiles // 2, 1, ROWS, LANES)
    ref[:, orbital, plane] = jnp.concatenate([left, right], axis=1).reshape(tiles, ROWS, LANES)


def derive_rows(work, matrix, rows):
    total = work.shape[0] // rows
    lanes = work.shape[1]
    for row in range(0, rows, 2):
        here = pl.ds(row, total, stride=rows)
        there = pl.ds(row + 1, total, stride=rows)
        value = jnp.concatenate([work[here, :], work[there, :]], axis=1).astype(jnp.bfloat16)
        result = dot(matrix, value)
        work[here, :] = result[:, :lanes]
        work[there, :] = result[:, lanes:]


def lines_kernel(field_ref, k_ref, out_ref, work):
    blocks, _, planes, rows, lanes = field_ref.shape
    work[...] = field_ref[...].reshape(blocks * planes * rows, lanes).astype(jnp.float32)
    derive_rows(work, k_ref[...], rows)
    out_ref[...] = work[...].astype(jnp.bfloat16).reshape(blocks, 1, planes, rows, lanes)


def derive_lines(field, k_t):
    blocks, count, planes, rows, lanes = field.shape
    block = pl.BlockSpec((blocks, 1, planes, rows, lanes), lambda i: (0, i, 0, 0, 0))
    size = field.size
    return pl.pallas_call(
        lines_kernel,
        grid=(count,),
        in_specs=[block, pl.BlockSpec(k_t.shape, lambda i: (0, 0))],
        out_specs=block,
        out_shape=jax.ShapeDtypeStruct(field.shape, jnp.bfloat16),
        scratch_shapes=[pltpu.VMEM((blocks * planes * rows, lanes), jnp.float32)],
        compiler_params=params(1, STEP_MIB),
        cost_estimate=cost(2 * size * blocks * planes, 4 * size),
        name="derive_lines",
    )(field, k_t)


def tile_kernel(in_ref, out_ref):
    tiles, count, planes, rows, lanes = out_ref.shape
    for tile in range(tiles):
        row, lane = tile // 2 * rows, tile % 2 * lanes
        out_ref[tile] = in_ref[:, :, row : row + rows, lane : lane + lanes]


def tile(orbitals, step=2):
    own, planes, height, depth = orbitals.shape
    tiles = height // ROWS * (depth // LANES)
    return pl.pallas_call(
        tile_kernel,
        grid=(planes // step,),
        in_specs=[pl.BlockSpec((own, step, height, depth), lambda x: (0, x, 0, 0))],
        out_specs=pl.BlockSpec((tiles, own, step, ROWS, LANES), lambda x: (0, 0, x, 0, 0)),
        out_shape=jax.ShapeDtypeStruct((tiles, own, planes, ROWS, LANES), orbitals.dtype),
        compiler_params=params(1),
        cost_estimate=cost(0, 4 * orbitals.size),
        name="tile",
    )(orbitals)


def local_terms(plane, ky_t, k_z):
    return dot(ky_t, plane) + dot(plane, k_z)


def each_plane(ref):
    return [(plane, o) for plane in range(ref.shape[2]) for o in range(ref.shape[1])]


def first_kernel(field_ref, line_ref, pot_ref, ky_ref, kz_ref, out_ref):
    for plane, o in each_plane(field_ref):
        field = load_plane(field_ref, plane, o)
        wide = field.astype(jnp.float32)
        line = load_plane(line_ref, plane, o).astype(jnp.float32)
        ham = -0.5 * (line + local_terms(field, ky_ref[...], kz_ref[...])) + pot_ref[plane] * wide
        value = (ham - CENTER * wide) * (1.0 / HALF_WIDTH)
        store_plane(out_ref, plane, value.astype(jnp.bfloat16), o)


def plane_specs(ky_t, potential, step):
    whole = pl.BlockSpec(ky_t.shape, lambda x: (0, 0))
    pot = pl.BlockSpec((step,) + potential.shape[1:], lambda x: (x, 0, 0))
    return [pot, whole, whole]


def planes_spec(field, step):
    tiles, count, _, rows, lanes = field.shape
    return pl.BlockSpec((tiles, count, step, rows, lanes), lambda x: (0, 0, x, 0, 0))


def first_step(field, line, potential, ky_t, k_z, step=2):
    size = field.size
    return pl.pallas_call(
        first_kernel,
        grid=(field.shape[2] // step,),
        in_specs=[planes_spec(field, step)] * 2 + plane_specs(ky_t, potential, step),
        out_specs=planes_spec(field, step),
        out_shape=jax.ShapeDtypeStruct(field.shape, jnp.bfloat16),
        compiler_params=params(1, STEP_MIB),
        cost_estimate=cost(4 * size * 256, 10 * size),
        name="first_step",
    )(field, line, potential, ky_t, k_z)


def store_pieces(me, refs, orbital, plane, work):
    bands = len(refs)
    span = work.shape[0] // bands
    for shift, ref in enumerate(refs):
        base = pl.multiple_of(lax.rem(me + shift, bands) * span, span)
        store_plane(ref, plane, work[pl.ds(base, span), :], orbital)


def filtered_kernel(me_ref, field_ref, line_ref, start_ref, pot_ref, ky_ref, kz_ref, *rest):
    piece_refs, out_ref, work = rest[:-2], rest[-2], rest[-1]
    for plane, o in each_plane(field_ref):
        field = load_plane(field_ref, plane, o)
        wide = field.astype(jnp.float32)
        line = load_plane(line_ref, plane, o).astype(jnp.float32)
        start = load_plane(start_ref, plane, o).astype(jnp.float32)
        ham = -0.5 * (line + local_terms(field, ky_ref[...], kz_ref[...])) + pot_ref[plane] * wide
        value = 2.0 * (ham - CENTER * wide) * (1.0 / HALF_WIDTH) - start
        value = value.astype(jnp.bfloat16)
        store_plane(out_ref, plane, value, o)
        work[...] = value
        store_pieces(me_ref[0], piece_refs, o, plane, work)


def pieces_of(field, bands):
    tiles, count, planes, rows, lanes = field.shape
    return jax.ShapeDtypeStruct((tiles // bands, count, planes, rows, lanes), jnp.bfloat16)


def filtered_step(me, field, line, start, potential, ky_t, k_z, bands, step=2):
    piece = pieces_of(field, bands)
    size = field.size
    out = pl.pallas_call(
        filtered_kernel,
        grid=(field.shape[2] // step,),
        in_specs=[pl.BlockSpec(memory_space=pltpu.SMEM)]
        + [planes_spec(field, step)] * 3
        + plane_specs(ky_t, potential, step),
        out_specs=[planes_spec(piece, step)] * bands + [planes_spec(field, step)],
        out_shape=[piece] * bands + [jax.ShapeDtypeStruct(field.shape, jnp.bfloat16)],
        scratch_shapes=[pltpu.VMEM(potential.shape[1:], jnp.bfloat16)],
        compiler_params=params(1),
        cost_estimate=cost(4 * size * 256, 14 * size),
        name="filtered_step",
    )(me, field, line, start, potential, ky_t, k_z)
    return (list(out[:bands]), out[bands])


def local_kernel(me_ref, field_ref, pot_ref, ky_ref, kz_ref, *rest):
    piece_refs, work = rest[:-1], rest[-1]
    for plane, o in each_plane(field_ref):
        field = load_plane(field_ref, plane, o)
        terms = local_terms(field, ky_ref[...], kz_ref[...])
        part = -0.5 * terms + pot_ref[plane] * field.astype(jnp.float32)
        work[...] = part.astype(jnp.bfloat16)
        store_pieces(me_ref[0], piece_refs, o, plane, work)


def local_step(me, field, potential, ky_t, k_z, bands, step=2):
    piece = pieces_of(field, bands)
    size = field.size
    out = pl.pallas_call(
        local_kernel,
        grid=(field.shape[2] // step,),
        in_specs=[pl.BlockSpec(memory_space=pltpu.SMEM), planes_spec(field, step)]
        + plane_specs(ky_t, potential, step),
        out_specs=[planes_spec(piece, step)] * bands,
        out_shape=[piece] * bands,
        scratch_shapes=[pltpu.VMEM(potential.shape[1:], jnp.bfloat16)],
        compiler_params=params(1),
        cost_estimate=cost(4 * size * 256, 8 * size),
        name="local_step",
    )(me, field, potential, ky_t, k_z)
    return list(out)


def chunk(refs, tile, plane):
    return jnp.concatenate(
        [split_rows(ref, tile, 0, plane) for ref in refs], axis=0
    )


def owner(place, me, own, bands, sign):
    return lax.rem(me + sign * (place // own) + bands, bands) * own + lax.rem(place, own)


def fold(product, me, out_ref, own, inner):
    rows = product.shape[0]
    count = out_ref.shape[0]
    at = lax.broadcasted_iota(jnp.int32, (rows, rows), 0)
    to = lax.broadcasted_iota(jnp.int32, (rows, rows), 1)
    who = lax.broadcasted_iota(jnp.int32, (count, rows), 0)
    row = lax.broadcasted_iota(jnp.int32, (count, rows), 1)
    if inner:
        same, place = at % ROWS == to % ROWS, row // ROWS
    else:
        same, place = at // ROWS == to // ROWS, row % ROWS
    kept = jnp.where(same, product, 0.0)
    pick = jnp.where(owner(place, me, own, count // own, -1) == who, 1.0, 0.0)
    half = jnp.dot(pick, kept, precision=HIGHEST, preferred_element_type=jnp.float32)
    out_ref[...] = lax.dot_general(
        half, pick, (((1,), (1,)), ((), ())), precision=HIGHEST, preferred_element_type=jnp.float32
    )


def gram_kernel(own, count, me_ref, *refs):
    refs, out_ref, work = refs[:-2], refs[-2], refs[-1]
    left, right = refs[:count], refs[-count:]

    @pl.when(pl.program_id(0) == 0)
    def _():
        work[...] = jnp.zeros_like(work)

    total = work[...]
    for plane in range(left[0].shape[2]):
        for tile in range(0, left[0].shape[0], 2):
            b = chunk(right, tile, plane)
            a = b if len(refs) == count else chunk(left, tile, plane)
            total = total + dot_nt(a, b)
    work[...] = total

    @pl.when(pl.program_id(0) == pl.num_programs(0) - 1)
    def _():
        fold(work[...], me_ref[0], out_ref, own, True)


def piece_spec(tiles, view, step):
    array, at = view
    _, _, _, rows, lanes = array.shape
    return pl.BlockSpec((tiles, 1, step, rows, lanes), lambda x: (0, at, x, 0, 0))


def gram(me, own, tiles, left, right=(), step=4):
    views = list(left) + list(right)
    _, _, planes, rows, lanes = views[0][0].shape
    total = len(left)
    size = tiles * planes * rows * lanes * total
    return pl.pallas_call(
        functools.partial(gram_kernel, own, total),
        grid=(planes // step,),
        in_specs=[pl.BlockSpec(memory_space=pltpu.SMEM)]
        + [piece_spec(tiles, view, step) for view in views],
        out_specs=pl.BlockSpec((total, total), lambda x: (0, 0)),
        out_shape=jax.ShapeDtypeStruct((total, total), jnp.float32),
        scratch_shapes=[pltpu.VMEM((total * rows, total * rows), jnp.float32)],
        compiler_params=params(1),
        cost_estimate=cost(2 * size * 256, 2 * size * (len(views) // total)),
        name="gram",
    )(me, *[view[0] for view in views])


def line_gram_kernel(own, me_ref, field_ref, k_ref, out_ref, work, derived):
    blocks, halves, planes, rows, lanes = field_ref.shape
    for half in range(halves):
        work[...] = field_ref[:, half].reshape(blocks * planes * rows, lanes).astype(jnp.float32)
        derive_rows(work, k_ref[...], rows)
        derived[half] = work[...].astype(jnp.bfloat16)
    step = rows * rows
    total = jnp.zeros((step, step), jnp.float32)
    each = step // (planes * rows)
    for at in range(0, blocks, each):
        start = at * planes * rows
        left = [derived[half, start : start + step] for half in range(halves)]
        right = [field_ref[at : at + each, half].reshape(step, lanes) for half in range(halves)]
        total = total + dot_nt(jnp.concatenate(left, axis=1), jnp.concatenate(right, axis=1))
    fold(total, me_ref[0], out_ref, own, False)


def line_gram(me, own, field, k_t):
    blocks, halves, planes, rows, lanes = field.shape
    vmem = pl.BlockSpec(memory_space=pltpu.VMEM)
    size = blocks * planes * rows
    return pl.pallas_call(
        functools.partial(line_gram_kernel, own),
        in_specs=[pl.BlockSpec(memory_space=pltpu.SMEM), vmem, vmem],
        out_specs=vmem,
        out_shape=jax.ShapeDtypeStruct((rows, rows), jnp.float32),
        scratch_shapes=[
            pltpu.VMEM((size, lanes), jnp.float32),
            pltpu.VMEM((halves, size, lanes), jnp.bfloat16),
        ],
        compiler_params=pltpu.CompilerParams(vmem_limit_bytes=STEP_MIB * 1024 * 1024),
        cost_estimate=cost(4 * field.size * 256, 2 * field.size),
        name="line_gram",
    )(me, field, k_t)


def regroup_kernel(*refs):
    work, out_ref, refs = refs[-1], refs[-2], refs[:-2]
    _, _, planes, rows, lanes = refs[0].shape
    each = planes * rows
    total = len(refs)
    for at, ref in enumerate(refs):
        work[at * each : (at + 1) * each, :] = ref[0, 0].reshape(each, lanes).astype(jnp.float32)
    half = rows // 2
    for plane in range(planes):
        for row in range(rows):
            value = work[pl.ds(plane * rows + row, total, stride=each), :]
            out_ref[row % half, row // half, plane] = value.astype(jnp.bfloat16)


def regroup(tiles, views):
    _, _, planes, rows, lanes = views[0][0].shape
    total = len(views)
    half = rows // 2

    def spec(at):
        return pl.BlockSpec((1, 1, planes, rows, lanes), lambda t: (t, at, 0, 0, 0))

    size = tiles * planes * rows * lanes * total
    return pl.pallas_call(
        regroup_kernel,
        grid=(tiles,),
        in_specs=[spec(at) for _, at in views],
        out_specs=pl.BlockSpec((half, 2, planes, total, lanes), lambda t: (t, 0, 0, 0, 0)),
        out_shape=jax.ShapeDtypeStruct((tiles * half, 2, planes, total, lanes), jnp.bfloat16),
        scratch_shapes=[pltpu.VMEM((total * planes * rows, lanes), jnp.float32)],
        compiler_params=params(1),
        cost_estimate=cost(size, 4 * size),
        name="regroup",
    )(*[view[0] for view in views])


def rotate_kernel(total, mix_ref, *refs):
    ins, outs = refs[:total], refs[total:]
    tiles, count, planes, rows, lanes = outs[0].shape
    for plane in range(planes):
        for tile in range(0, tiles, 2):
            value = dot(mix_ref[...], chunk(ins, tile, plane)).astype(jnp.bfloat16)
            for at, ref in enumerate(outs):
                for o in range(count):
                    start = (at * count + o) * rows
                    ref[tile, o, plane] = value[start : start + rows, :lanes]
                    ref[tile + 1, o, plane] = value[start : start + rows, lanes:]


def rotate(mix, own, tiles, views, step=4):
    _, _, planes, rows, lanes = views[0][0].shape
    total = len(views)
    out = pl.BlockSpec((tiles, own, step, rows, lanes), lambda x: (0, 0, x, 0, 0))
    shape = jax.ShapeDtypeStruct((tiles, own, planes, rows, lanes), jnp.bfloat16)
    size = tiles * planes * rows * lanes * total
    return pl.pallas_call(
        functools.partial(rotate_kernel, total),
        grid=(planes // step,),
        in_specs=[pl.BlockSpec(mix.shape, lambda x: (0, 0))]
        + [piece_spec(tiles, view, step) for view in views],
        out_specs=[out] * (total // own),
        out_shape=[shape] * (total // own),
        compiler_params=params(1),
        cost_estimate=cost(2 * size * 256, 4 * size),
        name="rotate",
    )(mix, *[view[0] for view in views])


def untile_kernel(me_ref, *refs):
    ins, out_ref = refs[:-1], refs[-1]
    bands = len(ins)
    tiles, _, _, rows, lanes = ins[0].shape
    for shift, ref in enumerate(ins):
        band = lax.rem(me_ref[0] + (bands - shift), bands)
        for tile in range(tiles):
            row = pl.multiple_of(band * (tiles // 2 * rows) + tile // 2 * rows, rows)
            lane = tile % 2 * lanes
            out_ref[:, :, pl.ds(row, rows), lane : lane + lanes] = ref[tile]


def untile(me, pieces, shape, step=2):
    own, planes, height, depth = shape
    return pl.pallas_call(
        untile_kernel,
        grid=(planes // step,),
        in_specs=[pl.BlockSpec(memory_space=pltpu.SMEM)] + [planes_spec(pieces[0], step)] * len(pieces),
        out_specs=pl.BlockSpec((own, step, height, depth), lambda x: (0, x, 0, 0)),
        out_shape=jax.ShapeDtypeStruct(shape, jnp.bfloat16),
        compiler_params=params(1),
        cost_estimate=cost(0, 4 * math.prod(shape)),
        name="untile",
    )(me, *pieces)


def order_of(size):
    return sorted(range(1, size), key=lambda s: -min(s, size - s))


def exchange(pieces, axis):
    size = lax.axis_size(axis)
    out = [pieces[0]] + [None] * (size - 1)

    def send(shift, piece):
        pairs = [(i, (i + shift) % size) for i in range(size)]
        out[shift % size] = lax.ppermute(piece, axis, pairs)

    for shift in order_of(size):
        if min(shift, size - shift) != 2:
            send(shift, pieces[shift])
    for shift, first in ((2, 1), (size - 2, size - 1)):
        send(shift, after(pieces[shift], out[first])[0])
    return out


def after(*values):
    return lax.optimization_barrier(values)


def over_grid(field):
    return lax.all_to_all(field, "grid", 0, 0, tiled=True)


def small_sum(matrix):
    axes = ("band", "grid")
    flat = matrix.reshape(-1, LANES)
    spread = jnp.broadcast_to(flat[None], (lax.axis_size(axes),) + flat.shape)
    return jnp.sum(lax.all_to_all(spread, axes, 0, 0, tiled=True), axis=0).reshape(matrix.shape)


def spread_sum(matrix, axis):
    flat = matrix.reshape(-1, LANES)
    spread = jnp.broadcast_to(flat[None], (lax.axis_size(axis),) + flat.shape)
    return jnp.sum(lax.all_to_all(spread, axis, 0, 0, tiled=True), axis=0).reshape(matrix.shape)


def mixing_kernel(own, me_ref, corr_ref, root_ref, scale_ref, mix_ref):
    correlation = corr_ref[...]
    count = correlation.shape[0]
    bands = count // own
    scale = jnp.max(jnp.sum(jnp.abs(correlation), axis=1, keepdims=True), axis=0, keepdims=True)
    at = lax.broadcasted_iota(jnp.int32, (count, count), 0)
    to = lax.broadcasted_iota(jnp.int32, (count, count), 1)
    identity = jnp.where(at == to, 1.0, 0.0)

    def full(a, b):
        return jnp.dot(a, b, precision=HIGHEST, preferred_element_type=jnp.float32)

    current = correlation / scale
    root = identity
    for _ in range(NS_ITERS):
        turn = 1.5 * identity - 0.5 * full(root, current)
        current = full(current, turn)
        root = full(turn, root)
    root_ref[...] = root
    scale_ref[...] = jnp.broadcast_to(scale, scale_ref.shape)
    coeff = root.astype(jnp.bfloat16)
    rows = mix_ref.shape[0]
    me = me_ref[0]
    who = lax.broadcasted_iota(jnp.int32, (count, rows), 0)
    place = lax.broadcasted_iota(jnp.int32, (count, rows), 1) // ROWS
    source = jnp.where(owner(place, me, own, bands, -1) == who, 1.0, 0.0).astype(jnp.bfloat16)
    target = jnp.where(owner(place, me, own, bands, 1) == who, 1.0, 0.0).astype(jnp.bfloat16)
    over_target = lax.dot_general(
        coeff, target, (((1,), (0,)), ((), ())), preferred_element_type=jnp.float32
    ).astype(jnp.bfloat16)
    mix = lax.dot_general(
        over_target, source, (((0,), (0,)), ((), ())), preferred_element_type=jnp.float32
    )
    at = lax.broadcasted_iota(jnp.int32, (rows, rows), 0)
    to = lax.broadcasted_iota(jnp.int32, (rows, rows), 1)
    mix_ref[...] = jnp.where(at % ROWS == to % ROWS, mix, 0.0).astype(jnp.bfloat16)


def mixing(me, own, correlation):
    count = correlation.shape[0]
    rows = count * ROWS
    vmem = pl.BlockSpec(memory_space=pltpu.VMEM)
    return pl.pallas_call(
        functools.partial(mixing_kernel, own),
        in_specs=[pl.BlockSpec(memory_space=pltpu.SMEM), vmem],
        out_specs=[vmem] * 3,
        out_shape=[
            jax.ShapeDtypeStruct((count, count), jnp.float32),
            jax.ShapeDtypeStruct((1, LANES), jnp.float32),
            jax.ShapeDtypeStruct((rows, rows), jnp.bfloat16),
        ],
        cost_estimate=cost(1e9, 1e6),
        name="mixing",
    )(me, correlation)


def project(inverse_root, hamil, scale):
    left = jnp.dot(inverse_root.T, hamil, precision=HIGHEST)
    return jnp.dot(left, inverse_root, precision=HIGHEST) / scale


def per_device(orbitals, potential):
    own, planes, height, depth = orbitals.shape
    bands = lax.axis_size("band")
    me = jnp.full((1,), lax.axis_index("band"), jnp.int32)
    kx_t = second_derivative(planes * lax.axis_size("grid")).T
    ky_t = second_derivative(height).T
    k_z = second_derivative(depth)

    start = tile(orbitals)
    line = over_grid(derive_lines(over_grid(start), kx_t))
    first = first_step(start, line, potential, ky_t, k_z)
    line = over_grid(derive_lines(over_grid(first), kx_t))
    pieces, whole = filtered_step(me, first, line, start, potential, ky_t, k_z, bands)

    tiles = start.shape[0] // bands
    arrived = exchange(pieces, "band")
    local = local_step(me, whole, potential, ky_t, k_z, bands)
    arrived[4] = after(arrived[4], *local)[0]
    f_views = [(arrived[s], o) for s in range(bands) for o in range(own)]
    local = exchange(local, "band")
    ends, second = (1, bands - 1), (2, bands - 2)
    far = tuple(range(3, bands - 2))
    correlation = gram(me, own, tiles, f_views)
    correlation = spread_sum(correlation, "grid")
    held = after(correlation, *[local[s] for s in ends])
    correlation = held[0]
    for s, piece in zip(ends, held[1:]):
        local[s] = piece
    correlation = spread_sum(correlation, "band")
    held = after(correlation, *[local[s] for s in second + far])
    correlation = held[0]
    for s, piece in zip(second + far, held[1:]):
        local[s] = piece
    inverse_root, scale, mix = mixing(me, own, correlation)
    g_views = [(local[s], o) for s in range(bands) for o in range(own)]
    back = exchange(rotate(mix, own, tiles, f_views), "band")
    lines = over_grid(after(regroup(tiles, f_views), correlation)[0])
    lines = after(lines, *[back[s] for s in ends])[0]
    hamil = gram(me, own, tiles, g_views, f_views) - 0.5 * line_gram(me, own, lines, kx_t)
    hamil = spread_sum(spread_sum(hamil, "grid"), "band")
    projected = project(inverse_root, hamil, scale[0, 0])
    return (untile(me, back, orbitals.shape), projected)


def solution(mesh):
    in_specs = (P("band", "grid", None, None), P("grid", None, None))
    out_specs = (P("band", "grid", None, None), P())
    return jax.shard_map(
        per_device, mesh=mesh, in_specs=in_specs, out_specs=out_specs, check_vma=False
    )
```

```python
import functools
import math

import jax
import jax.numpy as jnp
from jax import lax
from jax.experimental import pallas as pl
from jax.experimental.pallas import tpu as pltpu
from jax.sharding import PartitionSpec as P

NS_ITERS = 6

CENTER = 9.5
HALF_WIDTH = 6.5

ROWS = 16
LANES = 128
MOST_MIB = 63
STEP_MIB = 24
HIGHEST = lax.Precision.HIGHEST


def second_derivative(length):
    index = jnp.arange(length, dtype=jnp.int32)
    product = index[:, None] * index[None, :] % length
    angles = product.astype(jnp.float32) * (2.0 * math.pi / length)
    freq = jnp.minimum(index, length - index).astype(jnp.float32)
    weight = -((2.0 * math.pi / length * freq) ** 2) / length
    cosines = jnp.cos(angles)
    sines = jnp.sin(angles)
    matrix = jnp.dot(cosines * weight[None, :], cosines.T, precision=HIGHEST)
    matrix = matrix + jnp.dot(sines * weight[None, :], sines.T, precision=HIGHEST)
    return matrix.astype(jnp.bfloat16)


def dot(a, b):
    return jnp.dot(a, b, preferred_element_type=jnp.float32)


def dot_nt(a, b):
    return lax.dot_general(a, b, (((1,), (1,)), ((), ())), preferred_element_type=jnp.float32)


def params(dims, mib=MOST_MIB):
    return pltpu.CompilerParams(
        dimension_semantics=("arbitrary",) * dims, vmem_limit_bytes=mib * 1024 * 1024
    )


def cost(flops, bytes_accessed):
    return pl.CostEstimate(flops=int(flops), bytes_accessed=int(bytes_accessed), transcendentals=0)


def split_rows(ref, tile, orbital, plane):
    return jnp.concatenate(
        [ref[tile, orbital, plane], ref[tile + 1, orbital, plane]], axis=1
    )


def load_plane(ref, plane, orbital):
    tiles = ref.shape[0]
    value = ref[:, orbital, plane].reshape(tiles // 2, 2, ROWS, LANES)
    rows = tiles // 2 * ROWS
    return jnp.concatenate(
        [value[:, 0].reshape(rows, LANES), value[:, 1].reshape(rows, LANES)], axis=1
    )


def store_plane(ref, plane, value, orbital=0):
    tiles = ref.shape[0]
    left = value[:, :LANES].reshape(tiles // 2, 1, ROWS, LANES)
    right = value[:, LANES:].reshape(tiles // 2, 1, ROWS, LANES)
    ref[:, orbital, plane] = jnp.concatenate([left, right], axis=1).reshape(tiles, ROWS, LANES)


def derive_rows(work, matrix, rows):
    total = work.shape[0] // rows
    lanes = work.shape[1]
    for row in range(0, rows, 2):
        here = pl.ds(row, total, stride=rows)
        there = pl.ds(row + 1, total, stride=rows)
        value = jnp.concatenate([work[here, :], work[there, :]], axis=1).astype(jnp.bfloat16)
        result = dot(matrix, value)
        work[here, :] = result[:, :lanes]
        work[there, :] = result[:, lanes:]


def lines_kernel(field_ref, k_ref, out_ref, work):
    blocks, _, planes, rows, lanes = field_ref.shape
    work[...] = field_ref[...].reshape(blocks * planes * rows, lanes).astype(jnp.float32)
    derive_rows(work, k_ref[...], rows)
    out_ref[...] = work[...].astype(jnp.bfloat16).reshape(blocks, 1, planes, rows, lanes)


def derive_lines(field, k_t):
    blocks, count, planes, rows, lanes = field.shape
    block = pl.BlockSpec((blocks, 1, planes, rows, lanes), lambda i: (0, i, 0, 0, 0))
    size = field.size
    return pl.pallas_call(
        lines_kernel,
        grid=(count,),
        in_specs=[block, pl.BlockSpec(k_t.shape, lambda i: (0, 0))],
        out_specs=block,
        out_shape=jax.ShapeDtypeStruct(field.shape, jnp.bfloat16),
        scratch_shapes=[pltpu.VMEM((blocks * planes * rows, lanes), jnp.float32)],
        compiler_params=params(1, STEP_MIB),
        cost_estimate=cost(2 * size * blocks * planes, 4 * size),
        name="derive_lines",
    )(field, k_t)


def tile_kernel(in_ref, out_ref):
    tiles, count, planes, rows, lanes = out_ref.shape
    for tile in range(tiles):
        row, lane = tile // 2 * rows, tile % 2 * lanes
        out_ref[tile] = in_ref[:, :, row : row + rows, lane : lane + lanes]


def tile(orbitals, step=2):
    own, planes, height, depth = orbitals.shape
    tiles = height // ROWS * (depth // LANES)
    return pl.pallas_call(
        tile_kernel,
        grid=(planes // step,),
        in_specs=[pl.BlockSpec((own, step, height, depth), lambda x: (0, x, 0, 0))],
        out_specs=pl.BlockSpec((tiles, own, step, ROWS, LANES), lambda x: (0, 0, x, 0, 0)),
        out_shape=jax.ShapeDtypeStruct((tiles, own, planes, ROWS, LANES), orbitals.dtype),
        compiler_params=params(1),
        cost_estimate=cost(0, 4 * orbitals.size),
        name="tile",
    )(orbitals)


def local_terms(plane, ky_t, k_z):
    return dot(ky_t, plane) + dot(plane, k_z)


def each_plane(ref):
    return [(plane, o) for plane in range(ref.shape[2]) for o in range(ref.shape[1])]


def first_kernel(field_ref, line_ref, pot_ref, ky_ref, kz_ref, out_ref):
    for plane, o in each_plane(field_ref):
        field = load_plane(field_ref, plane, o)
        wide = field.astype(jnp.float32)
        line = load_plane(line_ref, plane, o).astype(jnp.float32)
        ham = -0.5 * (line + local_terms(field, ky_ref[...], kz_ref[...])) + pot_ref[plane] * wide
        value = (ham - CENTER * wide) * (1.0 / HALF_WIDTH)
        store_plane(out_ref, plane, value.astype(jnp.bfloat16), o)


def plane_specs(ky_t, potential, step):
    whole = pl.BlockSpec(ky_t.shape, lambda x: (0, 0))
    pot = pl.BlockSpec((step,) + potential.shape[1:], lambda x: (x, 0, 0))
    return [pot, whole, whole]


def planes_spec(field, step):
    tiles, count, _, rows, lanes = field.shape
    return pl.BlockSpec((tiles, count, step, rows, lanes), lambda x: (0, 0, x, 0, 0))


def first_step(field, line, potential, ky_t, k_z, step=2):
    size = field.size
    return pl.pallas_call(
        first_kernel,
        grid=(field.shape[2] // step,),
        in_specs=[planes_spec(field, step)] * 2 + plane_specs(ky_t, potential, step),
        out_specs=planes_spec(field, step),
        out_shape=jax.ShapeDtypeStruct(field.shape, jnp.bfloat16),
        compiler_params=params(1, STEP_MIB),
        cost_estimate=cost(4 * size * 256, 10 * size),
        name="first_step",
    )(field, line, potential, ky_t, k_z)


def store_pieces(me, refs, orbital, plane, work):
    bands = len(refs)
    span = work.shape[0] // bands
    for shift, ref in enumerate(refs):
        base = pl.multiple_of(lax.rem(me + shift, bands) * span, span)
        store_plane(ref, plane, work[pl.ds(base, span), :], orbital)


def filtered_kernel(me_ref, field_ref, line_ref, start_ref, pot_ref, ky_ref, kz_ref, *rest):
    piece_refs, out_ref, work = rest[:-2], rest[-2], rest[-1]
    for plane, o in each_plane(field_ref):
        field = load_plane(field_ref, plane, o)
        wide = field.astype(jnp.float32)
        line = load_plane(line_ref, plane, o).astype(jnp.float32)
        start = load_plane(start_ref, plane, o).astype(jnp.float32)
        ham = -0.5 * (line + local_terms(field, ky_ref[...], kz_ref[...])) + pot_ref[plane] * wide
        value = 2.0 * (ham - CENTER * wide) * (1.0 / HALF_WIDTH) - start
        value = value.astype(jnp.bfloat16)
        store_plane(out_ref, plane, value, o)
        work[...] = value
        store_pieces(me_ref[0], piece_refs, o, plane, work)


def pieces_of(field, bands):
    tiles, count, planes, rows, lanes = field.shape
    return jax.ShapeDtypeStruct((tiles // bands, count, planes, rows, lanes), jnp.bfloat16)


def filtered_step(me, field, line, start, potential, ky_t, k_z, bands, step=2):
    piece = pieces_of(field, bands)
    size = field.size
    out = pl.pallas_call(
        filtered_kernel,
        grid=(field.shape[2] // step,),
        in_specs=[pl.BlockSpec(memory_space=pltpu.SMEM)]
        + [planes_spec(field, step)] * 3
        + plane_specs(ky_t, potential, step),
        out_specs=[planes_spec(piece, step)] * bands + [planes_spec(field, step)],
        out_shape=[piece] * bands + [jax.ShapeDtypeStruct(field.shape, jnp.bfloat16)],
        scratch_shapes=[pltpu.VMEM(potential.shape[1:], jnp.bfloat16)],
        compiler_params=params(1),
        cost_estimate=cost(4 * size * 256, 14 * size),
        name="filtered_step",
    )(me, field, line, start, potential, ky_t, k_z)
    return (list(out[:bands]), out[bands])


def local_kernel(me_ref, field_ref, pot_ref, ky_ref, kz_ref, *rest):
    piece_refs, work = rest[:-1], rest[-1]
    for plane, o in each_plane(field_ref):
        field = load_plane(field_ref, plane, o)
        terms = local_terms(field, ky_ref[...], kz_ref[...])
        part = -0.5 * terms + pot_ref[plane] * field.astype(jnp.float32)
        work[...] = part.astype(jnp.bfloat16)
        store_pieces(me_ref[0], piece_refs, o, plane, work)


def local_step(me, field, potential, ky_t, k_z, bands, step=2):
    piece = pieces_of(field, bands)
    size = field.size
    out = pl.pallas_call(
        local_kernel,
        grid=(field.shape[2] // step,),
        in_specs=[pl.BlockSpec(memory_space=pltpu.SMEM), planes_spec(field, step)]
        + plane_specs(ky_t, potential, step),
        out_specs=[planes_spec(piece, step)] * bands,
        out_shape=[piece] * bands,
        scratch_shapes=[pltpu.VMEM(potential.shape[1:], jnp.bfloat16)],
        compiler_params=params(1),
        cost_estimate=cost(4 * size * 256, 8 * size),
        name="local_step",
    )(me, field, potential, ky_t, k_z)
    return list(out)


def chunk(refs, tile, plane):
    return jnp.concatenate(
        [split_rows(ref, tile, 0, plane) for ref in refs], axis=0
    )


def owner(place, me, own, bands, sign):
    return lax.rem(me + sign * (place // own) + bands, bands) * own + lax.rem(place, own)


def fold(product, me, out_ref, own, inner):
    rows = product.shape[0]
    count = out_ref.shape[0]
    at = lax.broadcasted_iota(jnp.int32, (rows, rows), 0)
    to = lax.broadcasted_iota(jnp.int32, (rows, rows), 1)
    who = lax.broadcasted_iota(jnp.int32, (count, rows), 0)
    row = lax.broadcasted_iota(jnp.int32, (count, rows), 1)
    if inner:
        same, place = at % ROWS == to % ROWS, row // ROWS
    else:
        same, place = at // ROWS == to // ROWS, row % ROWS
    kept = jnp.where(same, product, 0.0)
    pick = jnp.where(owner(place, me, own, count // own, -1) == who, 1.0, 0.0)
    half = jnp.dot(pick, kept, precision=HIGHEST, preferred_element_type=jnp.float32)
    out_ref[...] = lax.dot_general(
        half, pick, (((1,), (1,)), ((), ())), precision=HIGHEST, preferred_element_type=jnp.float32
    )


def gram_kernel(own, count, me_ref, *refs):
    refs, out_ref, work = refs[:-2], refs[-2], refs[-1]
    left, right = refs[:count], refs[-count:]

    @pl.when(pl.program_id(0) == 0)
    def _():
        work[...] = jnp.zeros_like(work)

    total = work[...]
    for plane in range(left[0].shape[2]):
        for tile in range(0, left[0].shape[0], 2):
            b = chunk(right, tile, plane)
            a = b if len(refs) == count else chunk(left, tile, plane)
            total = total + dot_nt(a, b)
    work[...] = total

    @pl.when(pl.program_id(0) == pl.num_programs(0) - 1)
    def _():
        fold(work[...], me_ref[0], out_ref, own, True)


def piece_spec(tiles, view, step):
    array, at = view
    _, _, _, rows, lanes = array.shape
    return pl.BlockSpec((tiles, 1, step, rows, lanes), lambda x: (0, at, x, 0, 0))


def gram(me, own, tiles, left, right=(), step=4):
    views = list(left) + list(right)
    _, _, planes, rows, lanes = views[0][0].shape
    total = len(left)
    size = tiles * planes * rows * lanes * total
    return pl.pallas_call(
        functools.partial(gram_kernel, own, total),
        grid=(planes // step,),
        in_specs=[pl.BlockSpec(memory_space=pltpu.SMEM)]
        + [piece_spec(tiles, view, step) for view in views],
        out_specs=pl.BlockSpec((total, total), lambda x: (0, 0)),
        out_shape=jax.ShapeDtypeStruct((total, total), jnp.float32),
        scratch_shapes=[pltpu.VMEM((total * rows, total * rows), jnp.float32)],
        compiler_params=params(1),
        cost_estimate=cost(2 * size * 256, 2 * size * (len(views) // total)),
        name="gram",
    )(me, *[view[0] for view in views])


def line_gram_kernel(own, me_ref, field_ref, k_ref, out_ref, work, derived):
    blocks, halves, planes, rows, lanes = field_ref.shape
    for half in range(halves):
        work[...] = field_ref[:, half].reshape(blocks * planes * rows, lanes).astype(jnp.float32)
        derive_rows(work, k_ref[...], rows)
        derived[half] = work[...].astype(jnp.bfloat16)
    step = rows * rows
    total = jnp.zeros((step, step), jnp.float32)
    each = step // (planes * rows)
    for at in range(0, blocks, each):
        start = at * planes * rows
        left = [derived[half, start : start + step] for half in range(halves)]
        right = [field_ref[at : at + each, half].reshape(step, lanes) for half in range(halves)]
        total = total + dot_nt(jnp.concatenate(left, axis=1), jnp.concatenate(right, axis=1))
    fold(total, me_ref[0], out_ref, own, False)


def line_gram(me, own, field, k_t):
    blocks, halves, planes, rows, lanes = field.shape
    vmem = pl.BlockSpec(memory_space=pltpu.VMEM)
    size = blocks * planes * rows
    return pl.pallas_call(
        functools.partial(line_gram_kernel, own),
        in_specs=[pl.BlockSpec(memory_space=pltpu.SMEM), vmem, vmem],
        out_specs=vmem,
        out_shape=jax.ShapeDtypeStruct((rows, rows), jnp.float32),
        scratch_shapes=[
            pltpu.VMEM((size, lanes), jnp.float32),
            pltpu.VMEM((halves, size, lanes), jnp.bfloat16),
        ],
        compiler_params=pltpu.CompilerParams(vmem_limit_bytes=STEP_MIB * 1024 * 1024),
        cost_estimate=cost(4 * field.size * 256, 2 * field.size),
        name="line_gram",
    )(me, field, k_t)


def regroup_kernel(*refs):
    work, out_ref, refs = refs[-1], refs[-2], refs[:-2]
    _, _, planes, rows, lanes = refs[0].shape
    each = planes * rows
    total = len(refs)
    for at, ref in enumerate(refs):
        work[at * each : (at + 1) * each, :] = ref[0, 0].reshape(each, lanes).astype(jnp.float32)
    half = rows // 2
    for plane in range(planes):
        for row in range(rows):
            value = work[pl.ds(plane * rows + row, total, stride=each), :]
            out_ref[row % half, row // half, plane] = value.astype(jnp.bfloat16)


def regroup(tiles, views):
    _, _, planes, rows, lanes = views[0][0].shape
    total = len(views)
    half = rows // 2

    def spec(at):
        return pl.BlockSpec((1, 1, planes, rows, lanes), lambda t: (t, at, 0, 0, 0))

    size = tiles * planes * rows * lanes * total
    return pl.pallas_call(
        regroup_kernel,
        grid=(tiles,),
        in_specs=[spec(at) for _, at in views],
        out_specs=pl.BlockSpec((half, 2, planes, total, lanes), lambda t: (t, 0, 0, 0, 0)),
        out_shape=jax.ShapeDtypeStruct((tiles * half, 2, planes, total, lanes), jnp.bfloat16),
        scratch_shapes=[pltpu.VMEM((total * planes * rows, lanes), jnp.float32)],
        compiler_params=params(1),
        cost_estimate=cost(size, 4 * size),
        name="regroup",
    )(*[view[0] for view in views])


def rotate_kernel(total, mix_ref, *refs):
    ins, outs = refs[:total], refs[total:]
    tiles, count, planes, rows, lanes = outs[0].shape
    for plane in range(planes):
        for tile in range(0, tiles, 2):
            value = dot(mix_ref[...], chunk(ins, tile, plane)).astype(jnp.bfloat16)
            for at, ref in enumerate(outs):
                for o in range(count):
                    start = (at * count + o) * rows
                    ref[tile, o, plane] = value[start : start + rows, :lanes]
                    ref[tile + 1, o, plane] = value[start : start + rows, lanes:]


def rotate(mix, own, tiles, views, step=4):
    _, _, planes, rows, lanes = views[0][0].shape
    total = len(views)
    out = pl.BlockSpec((tiles, own, step, rows, lanes), lambda x: (0, 0, x, 0, 0))
    shape = jax.ShapeDtypeStruct((tiles, own, planes, rows, lanes), jnp.bfloat16)
    size = tiles * planes * rows * lanes * total
    return pl.pallas_call(
        functools.partial(rotate_kernel, total),
        grid=(planes // step,),
        in_specs=[pl.BlockSpec(mix.shape, lambda x: (0, 0))]
        + [piece_spec(tiles, view, step) for view in views],
        out_specs=[out] * (total // own),
        out_shape=[shape] * (total // own),
        compiler_params=params(1),
        cost_estimate=cost(2 * size * 256, 4 * size),
        name="rotate",
    )(mix, *[view[0] for view in views])


def untile_kernel(me_ref, *refs):
    ins, out_ref = refs[:-1], refs[-1]
    bands = len(ins)
    tiles, _, _, rows, lanes = ins[0].shape
    for shift, ref in enumerate(ins):
        band = lax.rem(me_ref[0] + (bands - shift), bands)
        for tile in range(tiles):
            row = pl.multiple_of(band * (tiles // 2 * rows) + tile // 2 * rows, rows)
            lane = tile % 2 * lanes
            out_ref[:, :, pl.ds(row, rows), lane : lane + lanes] = ref[tile]


def untile(me, pieces, shape, step=2):
    own, planes, height, depth = shape
    return pl.pallas_call(
        untile_kernel,
        grid=(planes // step,),
        in_specs=[pl.BlockSpec(memory_space=pltpu.SMEM)] + [planes_spec(pieces[0], step)] * len(pieces),
        out_specs=pl.BlockSpec((own, step, height, depth), lambda x: (0, x, 0, 0)),
        out_shape=jax.ShapeDtypeStruct(shape, jnp.bfloat16),
        compiler_params=params(1),
        cost_estimate=cost(0, 4 * math.prod(shape)),
        name="untile",
    )(me, *pieces)


def order_of(size):
    return sorted(range(1, size), key=lambda s: -min(s, size - s))


def send(piece, shift, axis):
    size = lax.axis_size(axis)
    return lax.ppermute(piece, axis, [(i, (i + shift) % size) for i in range(size)])


def exchange(pieces, axis):
    size = lax.axis_size(axis)
    out = [pieces[0]] + [None] * (size - 1)
    for shift in order_of(size):
        if min(shift, size - shift) != 2:
            out[shift] = send(pieces[shift], shift, axis)
    for shift, first in ((2, 1), (size - 2, size - 1)):
        out[shift] = send(after(pieces[shift], out[first])[0], shift, axis)
    return out


def after(*values):
    return lax.optimization_barrier(values)


def over_grid(field):
    return lax.all_to_all(field, "grid", 0, 0, tiled=True)


def small_sum(matrix):
    axes = ("band", "grid")
    flat = matrix.reshape(-1, LANES)
    spread = jnp.broadcast_to(flat[None], (lax.axis_size(axes),) + flat.shape)
    return jnp.sum(lax.all_to_all(spread, axes, 0, 0, tiled=True), axis=0).reshape(matrix.shape)


def spread_sum(matrix, axis):
    flat = matrix.reshape(-1, LANES)
    spread = jnp.broadcast_to(flat[None], (lax.axis_size(axis),) + flat.shape)
    return jnp.sum(lax.all_to_all(spread, axis, 0, 0, tiled=True), axis=0).reshape(matrix.shape)


def mixing_kernel(own, me_ref, corr_ref, root_ref, scale_ref, mix_ref):
    correlation = corr_ref[...]
    count = correlation.shape[0]
    bands = count // own
    scale = jnp.max(jnp.sum(jnp.abs(correlation), axis=1, keepdims=True), axis=0, keepdims=True)
    at = lax.broadcasted_iota(jnp.int32, (count, count), 0)
    to = lax.broadcasted_iota(jnp.int32, (count, count), 1)
    identity = jnp.where(at == to, 1.0, 0.0)

    def full(a, b):
        return jnp.dot(a, b, precision=HIGHEST, preferred_element_type=jnp.float32)

    current = correlation / scale
    root = identity
    for _ in range(NS_ITERS):
        turn = 1.5 * identity - 0.5 * full(root, current)
        current = full(current, turn)
        root = full(turn, root)
    root_ref[...] = root
    scale_ref[...] = jnp.broadcast_to(scale, scale_ref.shape)
    coeff = root.astype(jnp.bfloat16)
    rows = mix_ref.shape[0]
    me = me_ref[0]
    who = lax.broadcasted_iota(jnp.int32, (count, rows), 0)
    place = lax.broadcasted_iota(jnp.int32, (count, rows), 1) // ROWS
    source = jnp.where(owner(place, me, own, bands, -1) == who, 1.0, 0.0).astype(jnp.bfloat16)
    target = jnp.where(owner(place, me, own, bands, 1) == who, 1.0, 0.0).astype(jnp.bfloat16)
    over_target = lax.dot_general(
        coeff, target, (((1,), (0,)), ((), ())), preferred_element_type=jnp.float32
    ).astype(jnp.bfloat16)
    mix = lax.dot_general(
        over_target, source, (((0,), (0,)), ((), ())), preferred_element_type=jnp.float32
    )
    at = lax.broadcasted_iota(jnp.int32, (rows, rows), 0)
    to = lax.broadcasted_iota(jnp.int32, (rows, rows), 1)
    mix_ref[...] = jnp.where(at % ROWS == to % ROWS, mix, 0.0).astype(jnp.bfloat16)


def mixing(me, own, correlation):
    count = correlation.shape[0]
    rows = count * ROWS
    vmem = pl.BlockSpec(memory_space=pltpu.VMEM)
    return pl.pallas_call(
        functools.partial(mixing_kernel, own),
        in_specs=[pl.BlockSpec(memory_space=pltpu.SMEM), vmem],
        out_specs=[vmem] * 3,
        out_shape=[
            jax.ShapeDtypeStruct((count, count), jnp.float32),
            jax.ShapeDtypeStruct((1, LANES), jnp.float32),
            jax.ShapeDtypeStruct((rows, rows), jnp.bfloat16),
        ],
        cost_estimate=cost(1e9, 1e6),
        name="mixing",
    )(me, correlation)


def project(inverse_root, hamil, scale):
    left = jnp.dot(inverse_root.T, hamil, precision=HIGHEST)
    return jnp.dot(left, inverse_root, precision=HIGHEST) / scale


def per_device(orbitals, potential):
    own, planes, height, depth = orbitals.shape
    bands = lax.axis_size("band")
    me = jnp.full((1,), lax.axis_index("band"), jnp.int32)
    kx_t = second_derivative(planes * lax.axis_size("grid")).T
    ky_t = second_derivative(height).T
    k_z = second_derivative(depth)

    start = tile(orbitals)
    line = over_grid(derive_lines(over_grid(start), kx_t))
    first = first_step(start, line, potential, ky_t, k_z)
    line = over_grid(derive_lines(over_grid(first), kx_t))
    pieces, whole = filtered_step(me, first, line, start, potential, ky_t, k_z, bands)

    tiles = start.shape[0] // bands
    arrived = exchange(pieces, "band")
    local = local_step(me, whole, potential, ky_t, k_z, bands)
    arrived[4] = after(arrived[4], *local)[0]
    local[1:] = after(*local[1:], *arrived[2 : bands - 1])[: bands - 1]
    f_views = [(arrived[s], o) for s in range(bands) for o in range(own)]
    ends, second = (1, bands - 1), (2, bands - 2)
    far = tuple(range(3, bands - 2))
    for o in ends + far:
        local[o] = send(local[o], o, "band")
    correlation = gram(me, own, tiles, f_views)
    correlation = spread_sum(correlation, "band")
    held = after(correlation, *[local[o] for o in second])
    for o, piece in zip(second, held[1:]):
        local[o] = send(piece, o, "band")
    held = after(held[0], *[local[o] for o in ends])
    correlation = held[0]
    for o, piece in zip(ends, held[1:]):
        local[o] = piece
    correlation = spread_sum(correlation, "grid")
    held = after(correlation, *[local[s] for s in second + far])
    correlation = held[0]
    for s, piece in zip(second + far, held[1:]):
        local[s] = piece
    inverse_root, scale, mix = mixing(me, own, correlation)
    g_views = [(local[s], o) for s in range(bands) for o in range(own)]
    back = exchange(rotate(mix, own, tiles, f_views), "band")
    lines = over_grid(after(regroup(tiles, f_views), correlation)[0])
    lines = after(lines, *[back[s] for s in ends])[0]
    hamil = gram(me, own, tiles, g_views, f_views) - 0.5 * line_gram(me, own, lines, kx_t)
    hamil = spread_sum(spread_sum(hamil, "grid"), "band")
    projected = project(inverse_root, hamil, scale[0, 0])
    return (untile(me, back, orbitals.shape), projected)


def solution(mesh):
    in_specs = (P("band", "grid", None, None), P("grid", None, None))
    out_specs = (P("band", "grid", None, None), P())
    return jax.shard_map(
        per_device, mesh=mesh, in_specs=in_specs, out_specs=out_specs, check_vma=False
    )
```
